128 devices in a mesh: dp: 4 (over y), ep: 32 (over x, z, core).
Axes of the slice: x: 4, y: 4, z: 4, core: 2. Of those that a mesh axis runs over, the one named last changes fastest.
Arguments:
- hidden_rows: bfloat16 [1024, 7168], P(('dp', 'ep')), may hold values from -6 to 6
- expert_ids: int32 [1024, 8], P(('dp', 'ep')), may hold values from 0 to 31, all different within a row; in each aligned block of 8 rows (0 to 7, 8 to 15, ...) at most 3 rows name the same one
- gate_weights: float32 [1024, 8], P(('dp', 'ep')), may hold values from 0.1 to 0.6
- w_gate: bfloat16 [32, 7168, 2048], P('ep', None, 'dp'), may hold values from -0.0625 to 0.0625
- w_up: bfloat16 [32, 7168, 2048], P('ep', None, 'dp'), may hold values from -0.0625 to 0.0625
- w_down: bfloat16 [32, 2048, 7168], P('ep', 'dp'), may hold values from -0.125 to 0.125
- queries: bfloat16 [1024, 64, 576], P(('dp', 'ep')), may hold values from -300 to 300
- suffix_cache: bfloat16 [1024, 128, 576], P(('dp', 'ep')), may hold values from -6 to 6
- prefix_pages: bfloat16 [128, 256, 576], P(('dp', 'ep')), may hold values from -6 to 6
- tree_sizes: int32 [4, 24], P('dp'), may hold values from 1 to 3, 32 in all within a row
Outputs:
- context: bfloat16 [1024, 64, 512], P(('dp', 'ep'))
- expert_mix: bfloat16 [1024, 7168], P(('dp', 'ep'))
The draws below stay inside these ranges and needn't reach their ends.
Inputs may be any that keep to these rules, and one draw needn't show every extreme that they name: `expert_ids`: each row names 8 different experts; among the leaves of one device no expert is named more than 3 times, a bound that some block reaches. `tree_sizes`: each row sums to 32; some tree of each row spans exactly 3 devices.
All inputs are finite; a program needn't handle non-finite values.
Results may differ from the reference program's by a relative error of at most 0.015.
Values may be sent and summed in bfloat16 or wider, within the bound.
A program may use at most 128 MiB of HBM per device.

```python
import math
import jax
import jax.numpy as jnp
import numpy as np
from jax import lax

D = 7168
FF = 2048
HEADS = 64
LATENT = 512
QK = 576
TOPK = 8
LEAF_DEV = 8
PRE = 256
SUF = 128
EXPERTS = 32
CAP = 3
NTREE = 24
LEAVES = 1024
PAGES = 128
N_DP = 4
N_EP = 32


def draw_queries(key, part):
    key = jax.random.fold_in(key, 3)
    first_key = jax.random.fold_in(key, 0)
    values = jax.random.truncated_normal(first_key, -6.0, 6.0, (LEAVES, HEADS, QK), jnp.float32)
    return values.astype(jnp.bfloat16)


def draw_suffix_cache(key, part):
    key = jax.random.fold_in(key, 5)
    values = jax.random.truncated_normal(key, -6.0, 6.0, (LEAVES, SUF, QK), jnp.float32)
    return values.astype(jnp.bfloat16)


def level_of(stream_key, shape, pieces, least, high):
    factor_of = 1.0
    for dim, shards_of in pieces:
        steps = jax.random.uniform(jax.random.fold_in(jax.random.fold_in(stream_key, 6), dim), (shards_of,), jnp.float32, least / len(pieces), high / len(pieces))
        factor_of = factor_of * jnp.repeat(jnp.exp(steps), shape[dim] // shards_of).reshape((-1,) + (1,) * (len(shape) - 1 - dim))
    return factor_of


def length_profile(amount, total, most, skew):
    loads = [(1 << 20) // math.isqrt(standing ** skew) + 1 for standing in range(2, amount + 1)]
    spare, given = total - most - (amount - 1), [1] * (amount - 1)
    while spare > 0:
        movable = [i for i in range(amount - 1) if given[i] < most]
        whole, remaining = sum([loads[i] for i in movable]), spare
        for i in movable:
            addition = min(most - given[i], max(1, remaining * loads[i] // whole), spare)
            given[i] = given[i] + addition
            spare = spare - addition
    return np.array([most] + given)


def uneven_parts(rng, count, total, limit, slope):
    if count == 2:
        one = jax.random.randint(rng, (), max(1, total - limit), min(limit, total - 1) + 1)
        return jnp.stack([one, total - one])
    sizes = jnp.asarray(length_profile(count, total, limit, slope), jnp.int32)
    pairs = (count - 1) // 2
    donor, receiver = sizes[1:1 + 2 * pairs:2], sizes[2:2 + 2 * pairs:2]
    slack = jnp.minimum(donor - 1, limit - receiver)
    moved = jax.random.randint(jax.random.fold_in(rng, 1), (pairs,), 0, 1 << 20) % (slack + 1)
    sizes = sizes.at[1:1 + 2 * pairs:2].set(donor - moved).at[2:2 + 2 * pairs:2].set(receiver + moved)
    return sizes[jax.random.permutation(jax.random.fold_in(rng, 2), count)]


def shared_out(stream_key, own, number, rows, count, top, bound, skew):
    sequence = jax.random.permutation(stream_key, count)
    heavy_load, usual = load_shares(count, rows * top, bound, skew, True), load_shares(count, rows * top, bound, skew, False)
    places = jnp.arange(count)

    def named(tallies, offset_by):
        used = int((tallies > 0).sum())
        fixed = max(1, used // 4)
        shifted = fixed + (places - fixed + offset_by * (used - fixed)) % max(1, count - fixed)
        return jnp.zeros((count,), jnp.int32).at[sequence[jnp.where(places < fixed, places, shifted)]].set(jnp.asarray(tallies, jnp.int32))

    tallies = jnp.where(number % 4 == 0, named(heavy_load, number // 4), named(usual, number - number // 4 - 1))
    mixed = jax.random.permutation(jax.random.fold_in(own, 3), count)
    source_of, taker = mixed[0:count // 2 * 2:2], mixed[1:count // 2 * 2:2]
    margin = jnp.minimum(tallies[source_of] - 1, bound - tallies[taker]) // 2
    margin = jnp.where((source_of == sequence[0]) | (taker == sequence[0]) | (tallies[taker] == 0), 0, jnp.maximum(margin, 0))
    shifted = jax.random.randint(jax.random.fold_in(own, 4), (count // 2,), 0, 1 << 20) % (margin + 1)
    tallies = tallies.at[source_of].add(-shifted).at[taker].add(shifted)
    items = jnp.searchsorted(jnp.cumsum(tallies), jnp.arange(rows * top), side="right").astype(jnp.int32)
    grid = items.reshape(top, rows).T
    grid = grid[jax.random.permutation(jax.random.fold_in(own, 1), rows)]
    offset_by = jax.random.randint(jax.random.fold_in(own, 2), (rows, 1), 0, top)
    return jnp.take_along_axis(grid, (jnp.arange(top)[None, :] + offset_by) % top, axis=1)


def load_shares(count, total, most, slope, full):
    loads = [(1 << 20) // math.isqrt(standing ** slope) + 1 for standing in range(1, count + 1)]
    largest = most if full else min(most, max(-(-total // count), total * loads[0] // sum(loads)))
    least = 1 if total - largest >= count - 1 else 0
    holding, surplus = [largest] + [least] * (count - 1), total - largest - least * (count - 1)
    while surplus > 0:
        candidates = [i for i in range(1, count) if holding[i] < largest] or [i for i in range(1, count) if holding[i] < most]
        mass, budget = sum([loads[i] for i in candidates]), surplus
        for i in candidates:
            extra = min(most - holding[i], max(1, budget * loads[i] // mass), surplus)
            holding[i] = holding[i] + extra
            surplus = surplus - extra
    return np.array(holding)


def normal_values(stream_key, dims, spread, bound, cuts=(), kind=jnp.bfloat16):
    array = spread * jax.random.normal(stream_key, dims, jnp.float32)
    if cuts:
        array = array * level_of(stream_key, dims, cuts, -0.22, 0.18)
    return jnp.clip(array, -bound, bound).astype(kind)


def setup_inputs(seed: int = 0) -> dict:
    keys = jax.random.split(jax.random.key(seed), 11)
    hidden_rows = normal_values(keys[0], (LEAVES, D), 1.0, 6.0, ((0, 128),))
    expert_ids_keys = jax.random.split(jax.random.fold_in(keys[1], 1), LEAVES // LEAF_DEV)
    expert_ids_turns = jax.random.permutation(jax.random.fold_in(keys[1], 3), LEAVES // LEAF_DEV)
    expert_ids = jax.vmap(lambda own, number: shared_out(jax.random.fold_in(keys[1], 2), own, number, LEAF_DEV, EXPERTS, TOPK, CAP, 2))(expert_ids_keys, expert_ids_turns).reshape((LEAVES, TOPK))
    gate_weights = jnp.clip(0.1 + 0.5 * jax.random.uniform(keys[2], (LEAVES, TOPK), jnp.float32) ** level_of(keys[2], (LEAVES, TOPK), ((0, 128),), -0.2, 0.2), 0.1, 0.6)
    w_gate = normal_values(keys[3], (EXPERTS, D, FF), D ** -0.5, 0.0625, ((0, 32), (2, 4)))
    w_up = normal_values(keys[4], (EXPERTS, D, FF), D ** -0.5, 0.0625, ((0, 32), (2, 4)))
    w_down = normal_values(keys[5], (EXPERTS, FF, D), FF ** -0.5, 0.125, ((0, 32), (1, 4)))
    queries = draw_queries(jax.random.fold_in(keys[10], 71), 0)
    suffix_cache = draw_suffix_cache(jax.random.fold_in(keys[10], 71), 0)
    prefix_pages = normal_values(keys[8], (PAGES, PRE, QK), 1.0, 6.0, ((0, 128),))
    tree_sizes = jax.vmap(lambda own: uneven_parts(own, NTREE, N_EP, 3, 2))(jax.random.split(keys[9], N_DP)).reshape((N_DP, NTREE)).astype(jnp.int32)
    return {"hidden_rows": hidden_rows, "expert_ids": expert_ids, "gate_weights": gate_weights, "w_gate": w_gate, "w_up": w_up, "w_down": w_down, "queries": queries, "suffix_cache": suffix_cache, "prefix_pages": prefix_pages, "tree_sizes": tree_sizes}


score_scale = 192.0 ** -0.5


def tree_index(run_sizes, places):
    run_ends = jnp.cumsum(run_sizes)
    return jnp.sum((run_ends[None, :] <= places[:, None]).astype(jnp.int32), axis=1)


def page_valid(run_sizes, position, span_total):
    offsets = jnp.arange(5, dtype=jnp.int32) - 2
    neighbours = position + offsets
    inside = (neighbours >= 0) & (neighbours < span_total)
    own_tree = tree_index(run_sizes, jnp.reshape(position, (1,)))
    other_tree = tree_index(run_sizes, jnp.clip(neighbours, 0, span_total - 1))
    return inside & (other_tree == own_tree)


def attend_block(local_queries, window, usable, local_suffix):
    query_wide = local_queries.astype(jnp.float32)
    window_wide = window.astype(jnp.float32)
    suffix_wide = local_suffix.astype(jnp.float32)
    far_scores = jnp.einsum("lhc,pkc->lhpk", query_wide, window_wide) * score_scale
    far_scores = jnp.where(usable[None, None, :, None], far_scores, -1e30)
    near_scores = jnp.einsum("lhc,lkc->lhk", query_wide, suffix_wide) * score_scale
    top_score = jnp.maximum(jnp.max(far_scores, axis=(2, 3)), jnp.max(near_scores, axis=2))
    far_weights = jnp.exp(far_scores - top_score[:, :, None, None])
    near_weights = jnp.exp(near_scores - top_score[:, :, None])
    totals = jnp.sum(far_weights, axis=(2, 3)) + jnp.sum(near_weights, axis=2)
    far_probs = lax.optimization_barrier(far_weights.astype(jnp.bfloat16)).astype(jnp.float32)
    near_probs = lax.optimization_barrier(near_weights.astype(jnp.bfloat16)).astype(jnp.float32)
    mixed = jnp.einsum("lhpk,pkc->lhc", far_probs, window_wide[..., :LATENT])
    mixed = mixed + jnp.einsum("lhk,lkc->lhc", near_probs, suffix_wide[..., :LATENT])
    return (mixed / totals[:, :, None]).astype(jnp.bfloat16)


def slot_numbers(choices_flat, expert_count):
    onehot = (choices_flat[:, None] == jnp.arange(expert_count, dtype=jnp.int32)[None, :]).astype(jnp.int32)
    earlier = jnp.cumsum(onehot, axis=0) - onehot
    return jnp.sum(earlier * onehot, axis=1)


def expert_rows(token_block, gate_mat, up_mat, down_mat):
    quarter = FF // N_DP
    summed = jnp.zeros((token_block.shape[0], down_mat.shape[1]), jnp.float32)
    for quarter_index in range(N_DP):
        lower_edge = quarter_index * quarter
        gate_part = jnp.dot(token_block, gate_mat[:, lower_edge:lower_edge + quarter], preferred_element_type=jnp.float32)
        up_part = jnp.dot(token_block, up_mat[:, lower_edge:lower_edge + quarter], preferred_element_type=jnp.float32)
        hidden = (jax.nn.silu(gate_part) * up_part).astype(jnp.bfloat16)
        partial_value = jnp.dot(hidden, down_mat[lower_edge:lower_edge + quarter], preferred_element_type=jnp.float32)
        summed = summed + lax.optimization_barrier(partial_value.astype(jnp.bfloat16)).astype(jnp.float32)
    return summed.astype(jnp.bfloat16)


def reference(hidden_rows, expert_ids, gate_weights, w_gate, w_up, w_down, queries, suffix_cache, prefix_pages, tree_sizes):
    devices_all = N_DP * N_EP
    choices_all = expert_ids.reshape(devices_all, LEAF_DEV * TOPK)
    slots_all = jax.vmap(lambda row_choices: slot_numbers(row_choices, N_EP))(choices_all)
    sources = jnp.arange(devices_all, dtype=jnp.int32)[:, None]
    columns = sources * CAP + slots_all
    token_index = sources * LEAF_DEV + jnp.arange(LEAF_DEV * TOPK, dtype=jnp.int32)[None, :] // TOPK
    sectioned = jnp.zeros((N_EP, devices_all * CAP, D), jnp.bfloat16)
    sectioned = sectioned.at[choices_all, columns].set(hidden_rows[token_index])
    outputs = lax.map(lambda operands: expert_rows(*operands), (sectioned, w_gate, w_up, w_down))
    picked = outputs[choices_all, columns].astype(jnp.float32).reshape(LEAVES, TOPK, D)
    expert_mix = jnp.sum(picked * gate_weights[:, :, None], axis=1).astype(jnp.bfloat16)

    page_grid = jnp.pad(prefix_pages.reshape(N_DP, N_EP, PRE, QK), ((0, 0), (2, 2), (0, 0), (0, 0)))

    def one_device(device):
        row_index = device // N_EP
        position = device % N_EP
        anchor = device * 0
        window = lax.dynamic_slice(page_grid, (row_index, position, anchor, anchor), (1, 5, PRE, QK))[0]
        run_sizes = lax.dynamic_index_in_dim(tree_sizes, row_index, 0, keepdims=False)
        usable = page_valid(run_sizes, position, N_EP)
        first_leaf = device * LEAF_DEV
        local_queries = lax.dynamic_slice_in_dim(queries, first_leaf, LEAF_DEV, 0)
        local_suffix = lax.dynamic_slice_in_dim(suffix_cache, first_leaf, LEAF_DEV, 0)
        return attend_block(local_queries, window, usable, local_suffix)

    context = lax.map(one_device, jnp.arange(devices_all, dtype=jnp.int32)).reshape(LEAVES, HEADS, LATENT)
    return (context, expert_mix)
```

```python
import functools

import jax
import jax.numpy as jnp
from jax import lax
from jax.experimental import pallas as pl
from jax.experimental.pallas import tpu as pltpu
from jax.sharding import PartitionSpec as P

LATENT = 512
TILE = 128
CHUNK = 256
ROWS = 16
score_scale = 192.0 ** (-0.5)
MESH = pl.DeviceIdType.MESH
ORDERS = ((1, 2, 0), (2, 0, 1), (0, 1, 2))


def shifted(x, axis, by):
    length = lax.axis_size(axis)
    pairs = [(i, i + by) for i in range(length) if 0 <= i + by < length]
    return lax.ppermute(x, axis, pairs)


def tree_index(run_sizes, places):
    run_ends = jnp.cumsum(run_sizes)
    return jnp.sum((run_ends[None, :] <= places[:, None]).astype(jnp.int32), axis=1)


def page_valid(run_sizes, position, span_total):
    offsets = jnp.arange(5, dtype=jnp.int32) - 2
    neighbours = position + offsets
    inside = (neighbours >= 0) & (neighbours < span_total)
    own_tree = tree_index(run_sizes, jnp.reshape(position, (1,)))
    other_tree = tree_index(run_sizes, jnp.clip(neighbours, 0, span_total - 1))
    return inside & (other_tree == own_tree)


def attend_block(local_queries, window, usable, local_suffix):
    far_scores = (
        jnp.einsum("lhc,pkc->lhpk", local_queries, window, preferred_element_type=jnp.float32)
        * score_scale
    )
    far_scores = jnp.where(usable[None, None, :, None], far_scores, -1e30)
    near_scores = (
        jnp.einsum("lhc,lkc->lhk", local_queries, local_suffix, preferred_element_type=jnp.float32)
        * score_scale
    )
    top_score = jnp.maximum(jnp.max(far_scores, axis=(2, 3)), jnp.max(near_scores, axis=2))
    far_weights = jnp.exp(far_scores - top_score[:, :, None, None])
    near_weights = jnp.exp(near_scores - top_score[:, :, None])
    totals = jnp.sum(far_weights, axis=(2, 3)) + jnp.sum(near_weights, axis=2)
    far_probs = far_weights.astype(jnp.bfloat16)
    near_probs = near_weights.astype(jnp.bfloat16)
    mixed = jnp.einsum(
        "lhpk,pkc->lhc", far_probs, window[..., :LATENT], preferred_element_type=jnp.float32
    )
    mixed = mixed + jnp.einsum(
        "lhk,lkc->lhc", near_probs, local_suffix[..., :LATENT], preferred_element_type=jnp.float32
    )
    return (mixed / totals[:, :, None]).astype(jnp.bfloat16)


class Copies:
    def __init__(self, send, recv, coords):
        self.send, self.recv, self.coords = send, recv, coords
        self.number, self.made = {}, {}

    def start(self, key, src, dst, device):
        i = self.number.setdefault(key, len(self.number))
        copy = pltpu.make_async_remote_copy(
            src_ref=src,
            dst_ref=dst,
            send_sem=self.send.at[i],
            recv_sem=self.recv.at[i],
            device_id=device,
            device_id_type=MESH,
        )
        copy.start()
        self.made[key] = copy

    def recv_wait(self, key):
        self.made[key].wait_recv()

    def send_wait(self, key):
        self.made[key].wait_send()


def cut(part_tiles):
    first = (part_tiles + 1) // 2
    return ((0, first), (first, part_tiles - first))


def moe_kernel(
    data_parts,
    hin,
    wg_hbm,
    wu_hbm,
    wd_hbm,
    out,
    xs,
    wg,
    wu,
    wd,
    accg,
    accu,
    hid,
    dd,
    r1a,
    r2a,
    r1b,
    r2b,
    r1c,
    r2c,
    exin,
    exback,
    backsrc,
    wsem,
    send_sem,
    recv_sem,
):
    ffq = wg.shape[2]
    half_cols = wg.shape[1]
    y = lax.axis_index("dp")
    ep = lax.axis_index("ep")
    core = lax.rem(ep, 2)
    x = ep // 8
    z = lax.rem(ep // 2, 4)
    here = (x, y, z)
    other = 1 - core

    def shift(axis, by):
        return lax.rem(here[axis] + (by + 4) % 4, 4)

    def device(axis, by):
        place = [x, y, z]
        place[axis] = shift(axis, by)
        return (place[1], place[0] * 8 + place[2] * 2 + core)

    sibling = (y, x * 8 + z * 2 + other)

    barrier = pltpu.get_barrier_semaphore()
    for axis in range(3):
        for by in (1, -1):
            pl.semaphore_signal(barrier, inc=1, device_id=device(axis, by), device_id_type=MESH)
    pl.semaphore_signal(barrier, inc=1, device_id=sibling, device_id_type=MESH)
    pl.semaphore_wait(barrier, 7)

    copies = Copies(send_sem, recv_sem, here)
    copies.start("exin", hin.at[other], exin, sibling)

    loads = []
    for half in range(2):
        rows = pl.ds(half * half_cols, half_cols)
        loads.append(pltpu.make_async_copy(wg_hbm.at[rows], wg.at[half], wsem.at[half]))
        loads.append(pltpu.make_async_copy(wu_hbm.at[rows], wu.at[half], wsem.at[2 + half]))
    for half in range(2):
        cols = pl.ds(half * half_cols, half_cols)
        loads.append(pltpu.make_async_copy(wd_hbm.at[:, cols], wd.at[half], wsem.at[4 + half]))
    for load in loads:
        load.start()

    starts = []
    spans = []
    for p in range(3):
        starts.append(sum(data_parts[:p]))
        spans.append(data_parts[p] + (1 if p == 2 else 0))

    copies.recv_wait("exin")
    copies.send_wait("exin")
    mine = hin[core]
    theirs = exin[...]
    low = jnp.where(core == 0, mine, theirs)
    high = jnp.where(core == 0, theirs, mine)
    xs[core, x, y, z] = jnp.concatenate([low, high], axis=0).astype(jnp.bfloat16)

    def where_of(free, axis=None, by=0):
        index = [x, y, z]
        for a in free:
            index[a] = slice(None)
        if axis is not None:
            index[axis] = shift(axis, by)
        return tuple(index)

    def columns(p, piece):
        return pl.ds((starts[p] + piece[0]) * TILE, piece[1] * TILE)

    @pl.loop(0, 4)
    def _(i):
        accg[i] = jnp.zeros_like(accg[i])
        accu[i] = jnp.zeros_like(accu[i])

    def gather_start(p, k):
        axis, free = ORDERS[p][k], ORDERS[p][:k]
        pieces = cut(spans[p])
        for d, by in ((0, 1), (1, -1)):
            for m in range(2):
                ref = xs.at[(core,) + where_of(free, axis, 0) + (slice(None), columns(p, pieces[d ^ m]))]
                copies.start(("ag", p, k, d, m), ref, ref, device(axis, by))

    def gather_forward(p, k):
        axis, free = ORDERS[p][k], ORDERS[p][:k]
        pieces = cut(spans[p])
        for d, by in ((0, 1), (1, -1)):
            copies.recv_wait(("ag", p, k, d, 0))
            ref = xs.at[(core,) + where_of(free, axis, -by) + (slice(None), columns(p, pieces[d]))]
            copies.start(("ag", p, k, d, 2), ref, ref, device(axis, by))

    def share(p, name, free, axis, by, piece):
        ref = xs.at[(core,) + where_of(free, axis, by) + (slice(None), columns(p, piece))]
        copies.start(("dd", p) + name, ref, ref, sibling)

    for k in range(2):
        for p in range(3):
            gather_start(p, k)
        for p in range(3):
            gather_forward(p, k)
        for p in range(3):
            for d in range(2):
                copies.recv_wait(("ag", p, k, d, 1))
                copies.recv_wait(("ag", p, k, d, 2))
    for p in range(3):
        gather_start(p, 2)
    for p in range(3):
        share(p, ("own",), ORDERS[p][:2], ORDERS[p][2], 0, (0, spans[p]))

    def plane(p, by):
        return where_of(ORDERS[p][:2], ORDERS[p][2], by)

    def layer1(p, by):
        at = plane(p, by)
        width = data_parts[p] * TILE
        first = starts[p] * TILE
        cols = pl.ds(first, width)

        @pl.loop(0, ffq // CHUNK)
        def _(j):
            some = pl.ds(pl.multiple_of(j * CHUNK, CHUNK), CHUNK)
            x0 = xs[(0,) + at + (slice(None), cols)].reshape(16 * ROWS, width)
            x1 = xs[(1,) + at + (slice(None), cols)].reshape(16 * ROWS, width)
            for acc, w in ((accg, wg), (accu, wu)):
                got = jnp.dot(x0, w[0, cols, some], preferred_element_type=jnp.float32)
                got = got + jnp.dot(x1, w[1, cols, some], preferred_element_type=jnp.float32)
                acc[at + (slice(None), some)] += got.reshape(4, 4, ROWS, CHUNK)

    for load in loads:
        load.wait()
    for p in range(3):
        copies.recv_wait(("dd", p, "own"))
        layer1(p, 0)

    for p in range(3):
        gather_forward(p, 2)
        axis, free = ORDERS[p][2], ORDERS[p][:2]
        pieces = cut(spans[p])
        for d, by in ((0, 1), (1, -1)):
            share(p, (d, 0), free, axis, -by, pieces[d])
    for p in range(3):
        axis, free = ORDERS[p][2], ORDERS[p][:2]
        pieces = cut(spans[p])
        for d, by in ((0, 1), (1, -1)):
            copies.recv_wait(("ag", p, 2, d, 1))
            share(p, (d, 1), free, axis, -by, pieces[1 - d])
    for p in range(3):
        for d, by in ((0, 1), (1, -1)):
            copies.recv_wait(("dd", p, d, 0))
            copies.recv_wait(("dd", p, d, 1))
            layer1(p, -by)
    for p in range(3):
        axis, free = ORDERS[p][2], ORDERS[p][:2]
        pieces = cut(spans[p])
        for d in range(2):
            copies.recv_wait(("ag", p, 2, d, 2))
            share(p, (d, 2), free, axis, 2, pieces[d])
    for p in range(3):
        for d in range(2):
            copies.recv_wait(("dd", p, d, 2))
        layer1(p, 2)

    @pl.loop(0, 4)
    def _(i):
        @pl.loop(0, 4)
        def _(j):
            tile = pl.ds(half_cols, TILE)
            weight = xs[0, i, j, :, :, tile].astype(jnp.float32) + xs[1, i, j, :, :, tile].astype(
                jnp.float32
            )
            lane = lax.broadcasted_iota(jnp.int32, weight.shape, 2)
            weight = jnp.sum(jnp.where(lane == ep, weight, 0.0), axis=2, keepdims=True)
            gate = accg[i, j]
            hidden = gate * (1.0 / (1.0 + jnp.exp(-gate))) * accu[i, j] * weight
            hid[i, j] = hidden.astype(jnp.bfloat16)

    for key in list(copies.made):
        if key[0] in ("ag", "dd"):
            copies.send_wait(key)

    def layer2(p, by, half):
        at = plane(p, by)

        @pl.loop(0, data_parts[p] * TILE // CHUNK)
        def _(j):
            some = pl.ds(pl.multiple_of(starts[p] * TILE + j * CHUNK, CHUNK), CHUNK)
            rows = hid[at].reshape(16 * ROWS, ffq)
            got = jnp.dot(rows, wd[half, :, some], preferred_element_type=jnp.float32)
            xs[(half,) + at + (slice(None), some)] = got.astype(jnp.bfloat16).reshape(
                4, 4, ROWS, CHUNK
            )

    def at_unit(at, unit):
        index, unit = list(at), list(unit)
        for a in range(3):
            if isinstance(index[a], slice):
                index[a] = unit.pop(0)
        return tuple(index)

    def add_in(at, first, width, sources):
        free = sum(isinstance(i, slice) for i in at)
        cols = pl.ds(first, width)

        def one(unit):
            index = (core,) + at_unit(at, unit) + (slice(None), cols)
            total = xs[index].astype(jnp.float32)
            for ref, lead, begin in sources:
                total = total + ref[lead + tuple(unit) + (slice(None), pl.ds(begin, width))].astype(
                    jnp.float32
                )
            xs[index] = total.astype(jnp.bfloat16)

        if free == 0:
            one(())
        elif free == 1:
            pl.loop(0, 4)(lambda i: one((i,)))
        else:

            @pl.loop(0, 4)
            def _(i):
                pl.loop(0, 4)(lambda j: one((i, j)))

    stores = ((r1a, r2a), (r1b, r2b), (r1c, r2c))

    def rs_start(p, stage, d, m, by, piece, to):
        k = 2 - stage
        axis, free = ORDERS[p][k], ORDERS[p][:k]
        src = xs.at[(core,) + where_of(free, axis, by) + (slice(None), columns(p, piece))]
        lead = (d,) + (slice(None),) * k + (slice(None),)
        if m == 0:
            dst = stores[stage][0].at[lead + (pl.ds(starts[p] // 2 * TILE, piece[1] * TILE),)]
        else:
            dst = stores[stage][1].at[lead + (columns(p, piece),)]
        copies.start(("rs", p, stage, d, m), src, dst, device(axis, to))

    def rs_far(p, stage):
        pieces = cut(data_parts[p])
        rs_start(p, stage, 0, 0, 2, pieces[0], 1)
        rs_start(p, stage, 1, 0, 2, pieces[1], -1)

    def rs_near(p, stage, d):
        pieces = cut(data_parts[p])
        by = (1, -1)[d]
        rs_start(p, stage, d, 1, by, pieces[1 - d], by)

    def rs_pass(p, stage, d):
        k = 2 - stage
        axis, free = ORDERS[p][k], ORDERS[p][:k]
        piece = cut(data_parts[p])[d]
        by = (1, -1)[d]
        copies.recv_wait(("rs", p, stage, d, 0))
        add_in(
            where_of(free, axis, by),
            (starts[p] + piece[0]) * TILE,
            piece[1] * TILE,
            ((stores[stage][0], (d,), starts[p] // 2 * TILE),),
        )
        rs_start(p, stage, d, 2, by, piece, by)

    def rs_end(p, stage):
        k = 2 - stage
        axis, free = ORDERS[p][k], ORDERS[p][:k]
        for d in range(2):
            copies.recv_wait(("rs", p, stage, d, 1))
            copies.recv_wait(("rs", p, stage, d, 2))
        first = starts[p] * TILE
        add_in(
            where_of(free, axis, 0),
            first,
            data_parts[p] * TILE,
            ((stores[stage][1], (0,), first), (stores[stage][1], (1,), first)),
        )

    def make(p, by):
        layer2(p, by, other)
        cols = pl.ds(starts[p] * TILE, data_parts[p] * TILE)
        at = plane(p, by)
        copies.start(
            ("rd", p, by), xs.at[(other,) + at + (slice(None), cols)], dd.at[at + (slice(None), cols)], sibling
        )
        layer2(p, by, core)

    def settle(p, by):
        copies.recv_wait(("rd", p, by))
        at = plane(p, by)
        first, width = starts[p] * TILE, data_parts[p] * TILE
        free = [a for a in range(3) if isinstance(at[a], slice)]

        @pl.loop(0, 4)
        def _(i):
            @pl.loop(0, 4)
            def _(j):
                unit = at_unit(at, (i, j))
                cols = pl.ds(first, width)
                index = (core,) + unit + (slice(None), cols)
                total = xs[index].astype(jnp.float32) + dd[unit + (slice(None), cols)].astype(jnp.float32)
                xs[index] = total.astype(jnp.bfloat16)

        if by == 2:
            rs_far(p, 0)
        elif by != 0:
            rs_near(p, 0, 0 if by == 1 else 1)

    tasks = [(p, by) for by in (2, 1, -1, 0) for p in range(3)]
    for n, task in enumerate(tasks):
        make(*task)
        if n:
            settle(*tasks[n - 1])
        if n in (9, 10, 11):
            p = n - 9
            for d in range(2):
                rs_pass(p, 0, d)
    settle(*tasks[-1])
    for p in range(3):
        rs_end(p, 0)
        rs_far(p, 1)
        rs_near(p, 1, 0)
        rs_near(p, 1, 1)
    for stage in (1, 2):
        for p in range(3):
            rs_pass(p, stage, 0)
            rs_pass(p, stage, 1)
        for p in range(3):
            rs_end(p, stage)
            if stage == 1:
                rs_far(p, 2)
                rs_near(p, 2, 0)
                rs_near(p, 2, 1)

    whole = xs[core, x, y, z, :, pl.ds(0, half_cols)].astype(jnp.float32)
    low, high = whole[:8], whole[8:]
    backsrc[...] = jnp.where(core == 0, high, low)
    copies.start("back", backsrc, exback, sibling)
    mine = jnp.where(core == 0, low, high)
    copies.recv_wait("back")
    theirs = exback[...]
    out[:, pl.ds(0, half_cols)] = jnp.where(core == 0, mine, theirs).astype(jnp.bfloat16)
    out[:, pl.ds(half_cols, half_cols)] = jnp.where(core == 0, theirs, mine).astype(jnp.bfloat16)
    copies.send_wait("back")
    for key in list(copies.made):
        if key[0] in ("rs", "rd"):
            copies.send_wait(key)


def moe(hidden_rows, expert_ids, gate_weights, w_gate, w_up, w_down):
    leaves, width = hidden_rows.shape
    half = width // 2
    ffq = w_gate.shape[2]
    experts = lax.axis_size("ep")
    tiles = half // TILE
    pairs = tiles // 2
    data_parts = [2 * ((pairs + 2 - p) // 3) for p in range(3)]
    named = expert_ids[:, :, None] == jnp.arange(experts, dtype=jnp.int32)[None, None, :]
    weight = jnp.sum(jnp.where(named, gate_weights[:, :, None], 0.0), axis=1)
    coarse = lax.reduce_precision(weight, 8, 7)
    fine = weight - coarse
    extra = jnp.pad(jnp.stack([coarse, fine]), ((0, 0), (0, 0), (0, TILE - experts)))
    rows = hidden_rows.astype(jnp.float32).reshape(leaves, 2, half).transpose(1, 0, 2)
    hin = jnp.concatenate([rows, extra], axis=2)
    chips = (4, 4, 4)
    bf16 = jnp.bfloat16
    scratch = [
        pltpu.VMEM((2,) + chips + (ROWS, half + TILE), bf16),
        pltpu.VMEM((2, half, ffq), bf16),
        pltpu.VMEM((2, half, ffq), bf16),
        pltpu.VMEM((2, ffq, half), bf16),
        pltpu.VMEM(chips + (ROWS, ffq), jnp.float32),
        pltpu.VMEM(chips + (ROWS, ffq), jnp.float32),
        pltpu.VMEM(chips + (ROWS, ffq), bf16),
        pltpu.VMEM(chips + (ROWS, half), bf16),
    ]
    first_cut = sum((n + 1) // 2 for n in data_parts) * TILE
    for free in (2, 1, 0):
        scratch.append(pltpu.VMEM((2,) + (4,) * free + (ROWS, first_cut), bf16))
        scratch.append(pltpu.VMEM((2,) + (4,) * free + (ROWS, half), bf16))
    scratch += [
        pltpu.VMEM((leaves, half + TILE), jnp.float32),
        pltpu.VMEM((leaves, half), jnp.float32),
        pltpu.VMEM((leaves, half), jnp.float32),
        pltpu.SemaphoreType.DMA((6,)),
        pltpu.SemaphoreType.DMA((148,)),
        pltpu.SemaphoreType.DMA((148,)),
    ]
    return pl.pallas_call(
        functools.partial(moe_kernel, data_parts),
        out_shape=jax.ShapeDtypeStruct((leaves, width), bf16),
        in_specs=[pl.BlockSpec(memory_space=pltpu.VMEM)] + [pl.BlockSpec(memory_space=pl.ANY)] * 3,
        out_specs=pl.BlockSpec(memory_space=pltpu.VMEM),
        scratch_shapes=scratch,
        compiler_params=pltpu.CompilerParams(
            collective_id=0, has_side_effects=True, vmem_limit_bytes=62 * 1024 * 1024
        ),
        name="experts",
    )(hin, w_gate[0], w_up[0], w_down[0])


def local(
    hidden_rows,
    expert_ids,
    gate_weights,
    w_gate,
    w_up,
    w_down,
    queries,
    suffix_cache,
    prefix_pages,
    tree_sizes,
):
    pieces = []
    for distance in (2, 1, 0, -1, -2):
        if distance == 0:
            pieces.append(prefix_pages)
        else:
            pieces.append(shifted(prefix_pages, "ep", distance))
    expert_mix = moe(hidden_rows, expert_ids, gate_weights, w_gate, w_up, w_down)
    window = jnp.concatenate(pieces, axis=0)
    usable = page_valid(tree_sizes[0], lax.axis_index("ep"), lax.axis_size("ep"))
    context = attend_block(queries, window, usable, suffix_cache)
    return (context, expert_mix)


def solution(mesh):
    return jax.shard_map(
        local,
        mesh=mesh,
        in_specs=(
            P(("dp", "ep"), None),
            P(("dp", "ep"), None),
            P(("dp", "ep"), None),
            P("ep", None, "dp"),
            P("ep", None, "dp"),
            P("ep", "dp", None),
            P(("dp", "ep"), None, None),
            P(("dp", "ep"), None, None),
            P(("dp", "ep"), None, None),
            P("dp", None),
        ),
        out_specs=(P(("dp", "ep"), None, None), P(("dp", "ep"), None)),
        check_vma=False,
    )
```

```python
import functools

import jax
import jax.numpy as jnp
from jax import lax
from jax.experimental import pallas as pl
from jax.experimental.pallas import tpu as pltpu
from jax.sharding import PartitionSpec as P

LATENT = 512
TILE = 128
CHUNK = 256
ROWS = 16
score_scale = 192.0 ** (-0.5)
MESH = pl.DeviceIdType.MESH
LINES = (0, 1, -1, 2)
ORDERS = ((1, 2, 0), (2, 0, 1), (0, 1, 2))


class Links:
    def __init__(self, send, recv):
        self.send, self.recv = send, recv
        self.sent, self.got = {}, {}

    def start(self, sent, got, src, dst, device):
        pltpu.make_async_remote_copy(
            src_ref=src,
            dst_ref=dst,
            send_sem=self.send.at[self.sent.setdefault(sent, len(self.sent))],
            recv_sem=self.recv.at[self.got.setdefault(got, len(self.got))],
            device_id=device,
            device_id_type=MESH,
        ).start()

    def recv_wait(self, got, ref):
        pltpu.make_async_copy(ref, ref, self.recv.at[self.got[got]]).wait()

    def send_wait(self, sent, ref):
        pltpu.make_async_copy(ref, ref, self.send.at[self.sent[sent]]).wait()


def cut(part_tiles):
    first = (part_tiles + 1) // 2
    return ((0, first), (first, part_tiles - first))


def kernel(
    data_parts,
    hidden_rows,
    expert_ids,
    gate_weights,
    tree_sizes,
    wg_hbm,
    wu_hbm,
    wd_hbm,
    queries,
    suffix,
    page,
    context,
    out,
    xs,
    wg,
    wu,
    wd,
    accg,
    accu,
    hid,
    dd,
    r1a,
    r2a,
    r1b,
    r2b,
    rc,
    exsrc,
    exin,
    backsrc,
    exback,
    window,
    q_all,
    near_all,
    mixed_all,
    wsem,
    asem,
    send_sem,
    recv_sem,
):
    ffq = wg.shape[2]
    half_cols = wg.shape[1]
    y = lax.axis_index("dp")
    ep = lax.axis_index("ep")
    core = lax.rem(ep, 2)
    x = ep // 8
    z = lax.rem(ep // 2, 4)
    here = (x, y, z)
    other = 1 - core

    def shift(axis, by):
        return lax.rem(here[axis] + (by + 4) % 4, 4)

    def device(axis, by):
        place = [x, y, z]
        place[axis] = shift(axis, by)
        return (place[1], place[0] * 8 + place[2] * 2 + core)

    sibling = (y, x * 8 + z * 2 + other)
    ahead = (y, lax.rem(ep + 2, 32))
    behind = (y, lax.rem(ep + 30, 32))

    barrier = pltpu.get_barrier_semaphore()
    greeted = [device(axis, by) for axis in range(3) for by in (1, -1, 2)] + [sibling, ahead, behind]
    for other_device in greeted:
        pl.semaphore_signal(barrier, inc=1, device_id=other_device, device_id_type=MESH)

    loads = []
    for half in range(2):
        rows = pl.ds(half * half_cols, half_cols)
        loads.append(pltpu.make_async_copy(wg_hbm.at[0, rows], wg.at[half], wsem.at[half]))
        loads.append(pltpu.make_async_copy(wu_hbm.at[0, rows], wu.at[half], wsem.at[2 + half]))
    for half in range(2):
        cols = pl.ds(half * half_cols, half_cols)
        loads.append(pltpu.make_async_copy(wd_hbm.at[0, :, cols], wd.at[half], wsem.at[4 + half]))
    att_loads = [
        pltpu.make_async_copy(queries, q_all, asem.at[0]),
        pltpu.make_async_copy(suffix, near_all, asem.at[1]),
        pltpu.make_async_copy(page.at[0], window.at[2], asem.at[2]),
    ]

    rows_low = hidden_rows[:, pl.ds(0, half_cols)].astype(jnp.float32)
    rows_high = hidden_rows[:, pl.ds(half_cols, half_cols)].astype(jnp.float32)
    lane = lax.broadcasted_iota(jnp.int32, (8, TILE), 1)
    weight = jnp.zeros((8, TILE), jnp.float32)
    for k in range(expert_ids.shape[1]):
        chosen = lane == expert_ids[:, pl.ds(k, 1)]
        weight = weight + jnp.where(chosen, gate_weights[:, pl.ds(k, 1)], 0.0)
    coarse = weight.astype(jnp.bfloat16).astype(jnp.float32)
    fine = weight - coarse
    exsrc[:, pl.ds(0, half_cols)] = jnp.where(core == 0, rows_high, rows_low)
    exsrc[:, pl.ds(half_cols, TILE)] = jnp.where(core == 0, fine, coarse)

    pl.semaphore_wait(barrier, len(greeted))
    links = Links(send_sem, recv_sem)
    links.start("ex", "ex", exsrc, exin, sibling)
    for load in loads + att_loads:
        load.start()

    starts = []
    spans = []
    for p in range(3):
        starts.append(sum(data_parts[:p]))
        spans.append(data_parts[p] + (1 if p == 2 else 0))

    links.recv_wait("ex", exin)
    theirs = exin[:, pl.ds(0, half_cols)]
    mine = jnp.where(core == 0, rows_low, rows_high)
    low = jnp.where(core == 0, mine, theirs)
    high = jnp.where(core == 0, theirs, mine)
    xs[core, x, y, z, :, pl.ds(0, half_cols)] = jnp.concatenate([low, high], axis=0).astype(jnp.bfloat16)
    theirs = exin[:, pl.ds(half_cols, TILE)]
    mine = jnp.where(core == 0, coarse, fine)
    low = jnp.where(core == 0, mine, theirs)
    high = jnp.where(core == 0, theirs, mine)
    xs[core, x, y, z, :, pl.ds(half_cols, TILE)] = jnp.concatenate([low, high], axis=0).astype(
        jnp.bfloat16
    )

    def chips(p, moves):
        index = [None, None, None]
        for axis, by in zip(ORDERS[p], moves):
            index[axis] = slice(None) if by is None else shift(axis, by)
        return tuple(index)

    def columns(p, piece):
        return pl.ds((starts[p] + piece[0]) * TILE, piece[1] * TILE)

    def rows_at(p, moves, piece):
        return xs.at[(core,) + chips(p, moves) + (slice(None), columns(p, piece))]

    def whole(p, lead):
        lead = tuple(pl.ds(0, n) if n else 0 for n in lead)
        return xs.at[(0,) + lead + (slice(None), columns(p, (0, spans[p])))]

    def gather(key, m, p, moves, piece, axis, by):
        ref = rows_at(p, moves, piece)
        links.start((key, p), (key, p) + m, ref, ref, device(axis, by))

    def share(p, plane, line):
        ref = rows_at(p, (None, line, plane), (0, spans[p]))
        links.start(("dd", p), ("dd", p, line), ref, ref, sibling)

    DIRS = ((0, 1), (1, -1))

    def start2(p):
        pieces = cut(spans[p])
        for m in range(2):
            for d, by in DIRS:
                gather("a2", (m,), p, (None, 0, 0), pieces[d ^ m], ORDERS[p][1], by)

    def wait2(p, m):
        links.recv_wait(("a2", p, m), whole(p, (0, 0, 4)))

    def forward2(p):
        wait2(p, 0)
        for d, by in DIRS:
            gather("a2", (2,), p, (None, -by, 0), cut(spans[p])[d], ORDERS[p][1], by)

    def start3(p, line, m):
        pieces = cut(spans[p])
        for d, by in DIRS:
            gather("a3", (line, m), p, (None, line, 0), pieces[d ^ m], ORDERS[p][2], by)

    def wait3(p, line, m):
        links.recv_wait(("a3", p, line, m), whole(p, (0, 0, 4)))

    def forward3(p, line):
        wait3(p, line, 0)
        for d, by in DIRS:
            gather("a3", (line, 2), p, (None, line, -by), cut(spans[p])[d], ORDERS[p][2], by)

    def plane(p, line):
        return chips(p, (None, line, None))

    def layer1(p, line):
        at = plane(p, line)
        width = data_parts[p] * TILE
        cols = pl.ds(starts[p] * TILE, width)
        x0 = xs[(0,) + at + (slice(None), cols)].reshape(16 * ROWS, width)
        x1 = xs[(1,) + at + (slice(None), cols)].reshape(16 * ROWS, width)
        for acc, w in ((accg, wg), (accu, wu)):
            got = jnp.dot(x0, w[0, cols, :], preferred_element_type=jnp.float32)
            got = got + jnp.dot(x1, w[1, cols, :], preferred_element_type=jnp.float32)
            acc[at] += got.reshape(4, 4, ROWS, ffq)

    for p in range(3):
        for by in (1, -1, 2):
            gather("a1", (), p, (0, 0, 0), (0, spans[p]), ORDERS[p][0], by)

    @pl.loop(0, 4)
    def _(i):
        accg[i] = jnp.zeros_like(accg[i])
        accu[i] = jnp.zeros_like(accu[i])

    for p in range(3):
        links.recv_wait(("a1", p), whole(p, (0, 0, 3)))
        start2(p)
    for p in range(3):
        start3(p, 0, 0)
        start3(p, 0, 1)
        share(p, 0, 0)
    for p in range(3):
        forward2(p)
    for p in range(3):
        wait2(p, 1)
        start3(p, 1, 0)
        share(p, 0, 1)
        share(p, 0, -1)
    for p in range(3):
        forward3(p, 0)
        start3(p, 1, 1)
        start3(p, -1, 0)
    for p in range(3):
        wait3(p, 0, 1)
        share(p, 1, 0)
        share(p, -1, 0)
    for p in range(3):
        wait2(p, 2)
        share(p, 0, 2)
    for p in range(3):
        forward3(p, 1)
        start3(p, -1, 1)
        start3(p, 2, 0)

    def beside(p, line):
        wait3(p, line, 1)
        share(p, 1, line)
        share(p, -1, line)

    def far(p, line):
        wait3(p, line, 2)
        share(p, 2, line)

    def first_layer(p, line):
        links.recv_wait(("dd", p, line), whole(p, (0, 4, 4)))
        layer1(p, line)

    for p in range(3):
        beside(p, 1)
    for p in range(3):
        far(p, 0)
    for load in loads:
        load.wait()
    first_layer(0, 0)
    first_layer(1, 0)
    for p in range(3):
        forward3(p, -1)
        start3(p, 2, 1)
    first_layer(2, 0)
    for p in range(3):
        far(p, 1)
        beside(p, -1)
    first_layer(0, 1)
    first_layer(1, 1)
    for p in range(3):
        forward3(p, 2)
    first_layer(2, 1)
    for p in range(3):
        far(p, -1)
        beside(p, 2)
    for p in range(3):
        first_layer(p, -1)
    for p in range(3):
        far(p, 2)
    links.start("page", "page", page.at[0], window.at[0], ahead)
    links.start("page", "page", page.at[0], window.at[4], behind)
    links.start("page", "near", page.at[0], window.at[1 + 2 * core], sibling)
    for p in range(3):
        first_layer(p, 2)

    @pl.loop(0, 4)
    def _(i):
        @pl.loop(0, 4)
        def _(j):
            tile = pl.ds(half_cols, TILE)
            weight = xs[0, i, j, :, :, tile].astype(jnp.float32) + xs[1, i, j, :, :, tile].astype(
                jnp.float32
            )
            lane = lax.broadcasted_iota(jnp.int32, weight.shape, 2)
            weight = jnp.sum(jnp.where(lane == ep, weight, 0.0), axis=2, keepdims=True)
            gate = accg[i, j]
            hidden = gate * (1.0 / (1.0 + jnp.exp(-gate))) * accu[i, j] * weight
            hid[i, j] = hidden.astype(jnp.bfloat16)

    for p in range(3):
        links.send_wait(("a1", p), whole(p, (0, 0, 3)))
        links.send_wait(("a2", p), whole(p, (0, 3, 4)))
        links.send_wait(("a3", p), whole(p, (3, 4, 4)))
        links.send_wait(("dd", p), whole(p, (4, 4, 4)))

    def layer2(p, line, half, extra=None):
        at = plane(p, line)
        width = data_parts[p] * TILE
        cols = pl.ds(starts[p] * TILE, width)
        rows = hid[at].reshape(16 * ROWS, ffq)
        got = jnp.dot(rows, wd[half, :, cols], preferred_element_type=jnp.float32)
        got = got.reshape(4, 4, ROWS, width)
        if extra is not None:
            got = got + extra[at + (slice(None), cols)].astype(jnp.float32)
        xs[(half,) + at + (slice(None), cols)] = got.astype(jnp.bfloat16)

    def add_in(p, moves, piece, sources):
        at = chips(p, moves)
        free = [a for a in range(3) if isinstance(at[a], slice)]
        cols = columns(p, piece)
        width = piece[1] * TILE

        def one(i):
            unit = tuple(i if a in free else at[a] for a in range(3))
            index = (core,) + unit + (slice(None), cols)
            total = xs[index].astype(jnp.float32)
            for ref, lead, first in sources:
                lead = tuple(i if isinstance(l, slice) else l for l in lead)
                total = total + ref[lead + (slice(None), pl.ds(first, width))].astype(jnp.float32)
            xs[index] = total.astype(jnp.bfloat16)

        if free:
            pl.loop(0, 4)(one)
        else:
            one(0)

    def block(p, lead):
        lead = tuple(pl.ds(0, n) if n else 0 for n in lead)
        return dd.at[lead + (slice(None), columns(p, (0, data_parts[p])))]

    def make(p, line):
        layer2(p, line, other)
        at = plane(p, line) + (slice(None), columns(p, (0, data_parts[p])))
        links.start(("rd", p), ("rd", p, line), xs.at[(other,) + at], dd.at[at], sibling)

    def near_place(p, line):
        at = chips(p, (None, line, 0))
        return tuple(at[a] for a in range(3) if a != ORDERS[p][2])

    def scatter(key, m, p, moves, piece, dst, axis, by):
        links.start((key, p), (key, p) + m, rows_at(p, moves, piece), dst, device(axis, by))

    def far1(p, line):
        for d, by in DIRS:
            piece = cut(data_parts[p])[d]
            dst = r1a.at[
                (d,) + near_place(p, line) + (slice(None), pl.ds(starts[p] // 2 * TILE, piece[1] * TILE))
            ]
            scatter("r1", (line, 0), p, (None, line, 2), piece, dst, ORDERS[p][2], by)

    def near1(p, line, d, m):
        by = (1, -1)[d]
        piece = cut(data_parts[p])[d if m == 2 else 1 - d]
        dst = r2a.at[(d,) + near_place(p, line) + (slice(None), columns(p, piece))]
        scatter("r1", (line, 1), p, (None, line, by), piece, dst, ORDERS[p][2], by)

    def pass1(p, line):
        links.recv_wait(("r1", p, line, 0), block(p, (0, 0, 4)))
        for d, by in DIRS:
            piece = cut(data_parts[p])[d]
            add_in(p, (None, line, by), piece, ((r1a, (d,) + near_place(p, line), starts[p] // 2 * TILE),))
            near1(p, line, d, 2)

    def end1(p, line):
        links.recv_wait(("r1", p, line, 1), block(p, (0, 2, 4)))
        place = near_place(p, line)
        first = starts[p] * TILE
        add_in(
            p, (None, line, 0), (0, data_parts[p]), ((r2a, (0,) + place, first), (r2a, (1,) + place, first))
        )

    def far2(p):
        for d, by in DIRS:
            piece = cut(data_parts[p])[d]
            dst = r1b.at[d, :, :, pl.ds(starts[p] // 2 * TILE, piece[1] * TILE)]
            scatter("r2", (0,), p, (None, 2, 0), piece, dst, ORDERS[p][1], by)

    def near2(p, d, m):
        by = (1, -1)[d]
        piece = cut(data_parts[p])[d if m == 2 else 1 - d]
        dst = r2b.at[d, :, :, columns(p, piece)]
        scatter("r2", (1,), p, (None, by, 0), piece, dst, ORDERS[p][1], by)

    def pass2(p):
        links.recv_wait(("r2", p, 0), block(p, (0, 0, 4)))
        for d, by in DIRS:
            piece = cut(data_parts[p])[d]
            add_in(p, (None, by, 0), piece, ((r1b, (d, slice(None)), starts[p] // 2 * TILE),))
            near2(p, d, 2)

    def end2(p):
        links.recv_wait(("r2", p, 1), block(p, (0, 2, 4)))
        first = starts[p] * TILE
        add_in(
            p,
            (None, 0, 0),
            (0, data_parts[p]),
            ((r2b, (0, slice(None)), first), (r2b, (1, slice(None)), first)),
        )

    def units(p):
        piece = (0, data_parts[p])
        for i, by in ((2, 2), (0, 1), (1, -1)):
            dst = rc.at[i, :, columns(p, piece)]
            scatter("r3", (), p, (by, 0, 0), piece, dst, ORDERS[p][0], by)

    def end3(p):
        links.recv_wait(("r3", p), block(p, (0, 0, 3)))
        first = starts[p] * TILE
        add_in(p, (0, 0, 0), (0, data_parts[p]), tuple((rc, (i,), first) for i in range(3)))

    BACK = (2, 1, -1, 0)

    def settle(p, line):
        links.recv_wait(("rd", p, line), block(p, (0, 4, 4)))
        layer2(p, line, core, dd)
        far1(p, line)
        for d in range(2):
            near1(p, line, d, 1)

    def onward(line):
        for p in range(3):
            end1(p, line)
            if line == 2:
                far2(p)
            elif line != 0:
                near2(p, 0 if line == 1 else 1, 1)

    begin, first_page, span = 0, 0, 0
    for i in range(tree_sizes.shape[1]):
        size = tree_sizes[0, i]
        inside = (begin <= ep) & (ep < begin + size)
        first_page = jnp.where(inside, begin, first_page)
        span = jnp.where(inside, size, span)
        begin = begin + size
    first_slot = jnp.clip(first_page - ep + 2, 0, 2)

    def dot_t(a, b):
        return lax.dot_general(a, b, (((1,), (1,)), ((), ())), preferred_element_type=jnp.float32)

    def attend(i):
        leaves = (2 * i, 2 * i + 1)
        rows = q_all[pl.ds(2 * i, 2)].reshape(2 * q_all.shape[1], q_all.shape[2])
        scores = []
        for k in range(3):
            got = dot_t(rows, window[first_slot + k]) * score_scale
            scores.append(jnp.where(k < span, got, -1e30))
        near = [dot_t(q_all[leaf], near_all[leaf]) * score_scale for leaf in leaves]
        scores.append(jnp.concatenate(near, axis=0))
        top = scores[3].max(axis=1, keepdims=True)
        for k in range(3):
            top = jnp.maximum(top, scores[k].max(axis=1, keepdims=True))
        weights = [jnp.exp(got - top) for got in scores]
        total = weights[3].sum(axis=1, keepdims=True)
        for k in range(3):
            total = total + weights[k].sum(axis=1, keepdims=True)
        probs = [got.astype(jnp.bfloat16) for got in weights]
        heads = q_all.shape[1]
        mixed = jnp.concatenate(
            [
                jnp.dot(
                    probs[3][n * heads : (n + 1) * heads],
                    near_all[leaf, :, pl.ds(0, LATENT)],
                    preferred_element_type=jnp.float32,
                )
                for n, leaf in enumerate(leaves)
            ],
            axis=0,
        )
        for k in range(3):
            mixed = mixed + jnp.dot(
                probs[k], window[first_slot + k, :, pl.ds(0, LATENT)], preferred_element_type=jnp.float32
            )
        mixed_all[pl.ds(2 * i, 2)] = (mixed / total).astype(jnp.bfloat16).reshape(2, heads, LATENT)
        pltpu.make_async_copy(mixed_all.at[pl.ds(2 * i, 2)], context.at[pl.ds(2 * i, 2)], asem.at[3 + i]).start()

    tasks = [(p, line) for line in BACK for p in range(3)]
    for n, task in enumerate(tasks):
        make(*task)
        if n:
            settle(*tasks[n - 1])
        if n == 3:
            links.recv_wait("page", window.at[pl.ds(0, 2)])
            links.start("page", "near", window.at[4 * other], window.at[3 - 2 * core], sibling)
        if n in (6, 9):
            for p in range(3):
                pass1(p, BACK[n // 3 - 2])
        if n == 9:
            onward(2)
            for load in att_loads:
                load.wait()
            links.recv_wait("near", window.at[pl.ds(0, 2)])
            attend(0)
    settle(*tasks[-1])
    for p in range(3):
        pass1(p, -1)
    onward(1)
    attend(1)
    for p in range(3):
        pass1(p, 0)
    onward(-1)
    attend(2)
    for p in range(3):
        pass2(p)
    for p in range(3):
        end1(p, 0)
    attend(3)
    for p in range(3):
        end2(p)
        units(p)
    for p in range(3):
        end3(p)

    total = xs[core, x, y, z, :, pl.ds(0, half_cols)].astype(jnp.float32)
    low, high = total[:8], total[8:]
    backsrc[...] = jnp.where(core == 0, high, low)
    links.start("back", "back", backsrc, exback, sibling)
    mine = jnp.where(core == 0, low, high)
    for p in range(3):
        links.send_wait(("rd", p), block(p, (4, 4, 4)))
        links.send_wait(("r1", p), block(p, (3, 4, 4)))
        links.send_wait(("r2", p), block(p, (0, 3, 4)))
        links.send_wait(("r3", p), block(p, (0, 0, 3)))
    links.send_wait("page", window.at[pl.ds(0, 4)])
    links.send_wait("ex", exsrc)
    for i in range(4):
        pltpu.make_async_copy(mixed_all.at[pl.ds(2 * i, 2)], context.at[pl.ds(2 * i, 2)], asem.at[3 + i]).wait()
    links.recv_wait("back", exback)
    theirs = exback[...]
    out[:, pl.ds(0, half_cols)] = jnp.where(core == 0, mine, theirs).astype(jnp.bfloat16)
    out[:, pl.ds(half_cols, half_cols)] = jnp.where(core == 0, theirs, mine).astype(jnp.bfloat16)
    links.send_wait("back", backsrc)


def local(
    hidden_rows,
    expert_ids,
    gate_weights,
    w_gate,
    w_up,
    w_down,
    queries,
    suffix_cache,
    prefix_pages,
    tree_sizes,
):
    leaves, width = hidden_rows.shape
    half = width // 2
    ffq = w_gate.shape[2]
    pairs = half // TILE // 2
    data_parts = [2 * ((pairs + 2 - p) // 3) for p in range(3)]
    grid = (4, 4, 4)
    bf16, f32 = jnp.bfloat16, jnp.float32
    first_cut = sum(cut(n)[0][1] for n in data_parts) * TILE
    heads, channels = queries.shape[1:]
    shapes = [
        ((2,) + grid + (ROWS, half + TILE), bf16),
        ((2, half, ffq), bf16),
        ((2, half, ffq), bf16),
        ((2, ffq, half), bf16),
        (grid + (ROWS, ffq), f32),
        (grid + (ROWS, ffq), f32),
        (grid + (ROWS, ffq), bf16),
        (grid + (ROWS, half), bf16),
        ((2, 4, 4, ROWS, first_cut), bf16),
        ((2, 4, 4, ROWS, half), bf16),
        ((2, 4, ROWS, first_cut), bf16),
        ((2, 4, ROWS, half), bf16),
        ((3, ROWS, half), bf16),
        ((leaves, half + TILE), f32),
        ((leaves, half + TILE), f32),
        ((leaves, half), f32),
        ((leaves, half), f32),
        ((5,) + prefix_pages.shape[1:], bf16),
        (queries.shape, bf16),
        (suffix_cache.shape, bf16),
        ((leaves, heads, LATENT), bf16),
    ]
    scratch = [pltpu.VMEM(shape, kind) for shape, kind in shapes]
    scratch += [pltpu.SemaphoreType.DMA((n,)) for n in (6, 7, 27, 109)]
    vmem, hbm = pl.BlockSpec(memory_space=pltpu.VMEM), pl.BlockSpec(memory_space=pl.ANY)
    smem = pl.BlockSpec(memory_space=pltpu.SMEM)
    return pl.pallas_call(
        functools.partial(kernel, data_parts),
        out_shape=(
            jax.ShapeDtypeStruct((leaves, heads, LATENT), bf16),
            jax.ShapeDtypeStruct((leaves, width), bf16),
        ),
        in_specs=[vmem] * 3 + [smem] + [hbm] * 6,
        out_specs=(hbm, vmem),
        scratch_shapes=scratch,
        compiler_params=pltpu.CompilerParams(
            collective_id=0, has_side_effects=True, vmem_limit_bytes=63 * 1024 * 1024
        ),
        name="experts",
    )(
        hidden_rows,
        expert_ids,
        gate_weights,
        tree_sizes,
        w_gate,
        w_up,
        w_down,
        queries,
        suffix_cache,
        prefix_pages,
    )


def solution(mesh):
    return jax.shard_map(
        local,
        mesh=mesh,
        in_specs=(
            P(("dp", "ep"), None),
            P(("dp", "ep"), None),
            P(("dp", "ep"), None),
            P("ep", None, "dp"),
            P("ep", None, "dp"),
            P("ep", "dp", None),
            P(("dp", "ep"), None, None),
            P(("dp", "ep"), None, None),
            P(("dp", "ep"), None, None),
            P("dp", None),
        ),
        out_specs=(P(("dp", "ep"), None, None), P(("dp", "ep"), None)),
        check_vma=False,
    )
```

```python
import functools

import jax
import jax.numpy as jnp
from jax import lax
from jax.experimental import pallas as pl
from jax.experimental.pallas import tpu as pltpu
from jax.sharding import PartitionSpec as P

LATENT = 512
TILE = 128
CHUNK = 256
ROWS = 16
score_scale = 192.0 ** (-0.5)
MESH = pl.DeviceIdType.MESH
LINES = (0, 1, -1, 2)
ORDERS = ((1, 2, 0), (2, 0, 1), (0, 1, 2))


class Links:
    def __init__(self, send, recv):
        self.send, self.recv = send, recv
        self.sent, self.got = {}, {}

    def start(self, sent, got, src, dst, device):
        pltpu.make_async_remote_copy(
            src_ref=src,
            dst_ref=dst,
            send_sem=self.send.at[self.sent.setdefault(sent, len(self.sent))],
            recv_sem=self.recv.at[self.got.setdefault(got, len(self.got))],
            device_id=device,
            device_id_type=MESH,
        ).start()

    def recv_wait(self, got, ref):
        pltpu.make_async_copy(ref, ref, self.recv.at[self.got[got]]).wait()

    def send_wait(self, sent, ref):
        pltpu.make_async_copy(ref, ref, self.send.at[self.sent[sent]]).wait()


def cut(part_tiles):
    first = (part_tiles + 1) // 2
    return ((0, first), (first, part_tiles - first))


def kernel(
    data_parts,
    hidden_rows,
    expert_ids,
    gate_weights,
    tree_sizes,
    wg_hbm,
    wu_hbm,
    wd_hbm,
    queries,
    suffix,
    page,
    context,
    out,
    xs,
    wg,
    wu,
    wd,
    accg,
    accu,
    hid,
    dd,
    r1a,
    r2a,
    r1b,
    r2b,
    rc,
    exsrc,
    exin,
    backsrc,
    exback,
    window,
    q_all,
    near_all,
    mixed_all,
    wsem,
    asem,
    send_sem,
    recv_sem,
):
    ffq = wg.shape[2]
    half_cols = wg.shape[1]
    y = lax.axis_index("dp")
    ep = lax.axis_index("ep")
    core = lax.rem(ep, 2)
    x = ep // 8
    z = lax.rem(ep // 2, 4)
    here = (x, y, z)
    other = 1 - core

    def shift(axis, by):
        return lax.rem(here[axis] + (by + 4) % 4, 4)

    def device(axis, by):
        place = [x, y, z]
        place[axis] = shift(axis, by)
        return (place[1], place[0] * 8 + place[2] * 2 + core)

    sibling = (y, x * 8 + z * 2 + other)
    ahead = (y, lax.rem(ep + 2, 32))
    behind = (y, lax.rem(ep + 30, 32))

    barrier = pltpu.get_barrier_semaphore()
    greeted = [device(axis, by) for axis in range(3) for by in (1, -1, 2)] + [sibling, ahead, behind]
    for other_device in greeted:
        pl.semaphore_signal(barrier, inc=1, device_id=other_device, device_id_type=MESH)

    loads = []
    for half in range(2):
        rows = pl.ds(half * half_cols, half_cols)
        loads.append(pltpu.make_async_copy(wg_hbm.at[0, rows], wg.at[half], wsem.at[half]))
        loads.append(pltpu.make_async_copy(wu_hbm.at[0, rows], wu.at[half], wsem.at[2 + half]))
    for half in range(2):
        cols = pl.ds(half * half_cols, half_cols)
        loads.append(pltpu.make_async_copy(wd_hbm.at[0, :, cols], wd.at[half], wsem.at[4 + half]))
    att_loads = [
        pltpu.make_async_copy(queries, q_all, asem.at[0]),
        pltpu.make_async_copy(suffix, near_all, asem.at[1]),
        pltpu.make_async_copy(page.at[0], window.at[2], asem.at[2]),
    ]

    rows_low = hidden_rows[:, pl.ds(0, half_cols)].astype(jnp.float32)
    rows_high = hidden_rows[:, pl.ds(half_cols, half_cols)].astype(jnp.float32)
    lane = lax.broadcasted_iota(jnp.int32, (8, TILE), 1)
    weight = jnp.zeros((8, TILE), jnp.float32)
    for k in range(expert_ids.shape[1]):
        chosen = lane == expert_ids[:, pl.ds(k, 1)]
        weight = weight + jnp.where(chosen, gate_weights[:, pl.ds(k, 1)], 0.0)
    coarse = weight.astype(jnp.bfloat16).astype(jnp.float32)
    fine = weight - coarse
    exsrc[:, pl.ds(0, half_cols)] = jnp.where(core == 0, rows_high, rows_low)
    exsrc[:, pl.ds(half_cols, TILE)] = jnp.where(core == 0, fine, coarse)

    pl.semaphore_wait(barrier, len(greeted))
    links = Links(send_sem, recv_sem)
    links.start("ex", "ex", exsrc, exin, sibling)
    for load in loads + att_loads:
        load.start()

    starts = []
    spans = []
    for p in range(3):
        starts.append(sum(data_parts[:p]))
        spans.append(data_parts[p] + (1 if p == 2 else 0))

    links.recv_wait("ex", exin)
    theirs = exin[:, pl.ds(0, half_cols)]
    mine = jnp.where(core == 0, rows_low, rows_high)
    low = jnp.where(core == 0, mine, theirs)
    high = jnp.where(core == 0, theirs, mine)
    xs[core, x, y, z, :, pl.ds(0, half_cols)] = jnp.concatenate([low, high], axis=0).astype(jnp.bfloat16)
    theirs = exin[:, pl.ds(half_cols, TILE)]
    mine = jnp.where(core == 0, coarse, fine)
    low = jnp.where(core == 0, mine, theirs)
    high = jnp.where(core == 0, theirs, mine)
    xs[core, x, y, z, :, pl.ds(half_cols, TILE)] = jnp.concatenate([low, high], axis=0).astype(
        jnp.bfloat16
    )

    def chips(p, moves):
        index = [None, None, None]
        for axis, by in zip(ORDERS[p], moves):
            index[axis] = slice(None) if by is None else shift(axis, by)
        return tuple(index)

    def columns(p, piece):
        return pl.ds((starts[p] + piece[0]) * TILE, piece[1] * TILE)

    def rows_at(p, moves, piece):
        return xs.at[(core,) + chips(p, moves) + (slice(None), columns(p, piece))]

    def whole(p, lead):
        lead = tuple(pl.ds(0, n) if n else 0 for n in lead)
        return xs.at[(0,) + lead + (slice(None), columns(p, (0, spans[p])))]

    def gather(key, m, p, moves, piece, axis, by):
        ref = rows_at(p, moves, piece)
        links.start((key, p), (key, p) + m, ref, ref, device(axis, by))

    def share(name, p, by, line):
        ref = rows_at(p, (None, line, by), (0, spans[p]))
        links.start(("dd", p), ("dd", p, name), ref, ref, sibling)

    DIRS = ((0, 1), (1, -1))

    def start2(p):
        pieces = cut(spans[p])
        for m in range(2):
            for d, by in DIRS:
                gather("a2", (m,), p, (None, 0, 0), pieces[d ^ m], ORDERS[p][1], by)

    def wait2(p, m):
        links.recv_wait(("a2", p, m), whole(p, (0, 0, 4)))

    def forward2(p):
        wait2(p, 0)
        for d, by in DIRS:
            gather("a2", (2,), p, (None, -by, 0), cut(spans[p])[d], ORDERS[p][1], by)

    def start3(p, line, m):
        pieces = cut(spans[p])
        for d, by in DIRS:
            gather("a3", (line, m), p, (None, line, 0), pieces[d ^ m], ORDERS[p][2], by)

    def wait3(p, line, m):
        links.recv_wait(("a3", p, line, m), whole(p, (0, 0, 4)))

    def forward3(p, line):
        wait3(p, line, 0)
        for d, by in DIRS:
            gather("a3", (line, 2), p, (None, line, -by), cut(spans[p])[d], ORDERS[p][2], by)

    OWN = ((None, 0),)

    def places(p, spots):
        return [chips(p, (None, line, by)) for line, by in spots]

    def stacked(parts):
        parts = [part.reshape(-1, part.shape[-1]) for part in parts]
        return parts[0] if len(parts) == 1 else jnp.concatenate(parts, axis=0)

    def apart(value, ats):
        first = 0
        for at in ats:
            lead = (4,) * sum(isinstance(i, slice) for i in at)
            count = 4 ** len(lead) * ROWS
            yield at, value[first : first + count].reshape(lead + (ROWS, value.shape[-1]))
            first += count

    def layer1(p, spots):
        ats = places(p, spots)
        cols = pl.ds(starts[p] * TILE, data_parts[p] * TILE)
        x0, x1 = [stacked([xs[(half,) + at + (slice(None), cols)] for at in ats]) for half in range(2)]
        for acc, w in ((accg, wg), (accu, wu)):
            got = jnp.dot(x0, w[0, cols, :], preferred_element_type=jnp.float32)
            got = got + jnp.dot(x1, w[1, cols, :], preferred_element_type=jnp.float32)
            for at, rows in apart(got, ats):
                acc[at] += rows

    for p in range(3):
        for by in (1, -1, 2):
            gather("a1", (), p, (0, 0, 0), (0, spans[p]), ORDERS[p][0], by)

    @pl.loop(0, 4)
    def _(i):
        accg[i] = jnp.zeros_like(accg[i])
        accu[i] = jnp.zeros_like(accu[i])

    def beside(name, p, line):
        wait3(p, line, 1)
        share(name, p, 1, line)
        share(name, p, -1, line)

    def far(name, p, line):
        wait3(p, line, 2)
        share(name, p, 2, line)

    def first_layer(name, p):
        spots = {
            "own": OWN,
            "near0": ((0, 1), (0, -1)),
            "near1": ((1, 1), (1, -1), (-1, 1), (-1, -1)),
            "near2": ((2, 1), (2, -1)),
            "far0": ((0, 2), (1, 2)),
            "far1": ((-1, 2), (2, 2)),
        }[name]
        count = 4 if name == "own" else len(spots)
        links.recv_wait(("dd", p, name), whole(p, (0, count, 4)))
        layer1(p, spots)

    for p in range(3):
        links.recv_wait(("a1", p), whole(p, (0, 0, 3)))
        start2(p)
    for p in range(3):
        start3(p, 0, 0)
        start3(p, 0, 1)
        share("own", p, 0, 0)
    for p in range(3):
        forward2(p)
    for p in range(3):
        wait2(p, 1)
        start3(p, 1, 0)
        start3(p, -1, 0)
        share("own", p, 0, 1)
        share("own", p, 0, -1)
    for p in range(3):
        forward3(p, 0)
        start3(p, 1, 1)
    for p in range(3):
        beside("near0", p, 0)
    for p in range(3):
        wait2(p, 2)
        share("own", p, 0, 2)
        start3(p, 2, 0)
        start3(p, -1, 1)
    for load in loads:
        load.wait()
    for p in range(3):
        forward3(p, 1)
        first_layer("own", p)
    for p in range(3):
        forward3(p, -1)
        start3(p, 2, 1)
    for p in range(3):
        far("far0", p, 0)
    first_layer("near0", 0)
    first_layer("near0", 1)
    for p in range(3):
        beside("near1", p, 1)
    first_layer("near0", 2)
    for p in range(3):
        forward3(p, 2)
    for p in range(3):
        beside("near1", p, -1)
    first_layer("near1", 0)
    first_layer("near1", 1)
    for p in range(3):
        far("far0", p, 1)
    first_layer("near1", 2)
    for p in range(3):
        far("far1", p, -1)
    first_layer("far0", 0)
    first_layer("far0", 1)
    for p in range(3):
        beside("near2", p, 2)
    first_layer("far0", 2)
    first_layer("near2", 0)
    for p in range(3):
        far("far1", p, 2)
    links.start("page", "page", page.at[0], window.at[0], ahead)
    links.start("page", "page", page.at[0], window.at[4], behind)
    links.start("page", "near", page.at[0], window.at[1 + 2 * core], sibling)
    first_layer("near2", 1)
    first_layer("near2", 2)
    for p in range(3):
        first_layer("far1", p)

    @pl.loop(0, 4)
    def _(i):
        @pl.loop(0, 4)
        def _(j):
            tile = pl.ds(half_cols, TILE)
            weight = xs[0, i, j, :, :, tile].astype(jnp.float32) + xs[1, i, j, :, :, tile].astype(
                jnp.float32
            )
            lane = lax.broadcasted_iota(jnp.int32, weight.shape, 2)
            weight = jnp.sum(jnp.where(lane == ep, weight, 0.0), axis=2, keepdims=True)
            gate = accg[i, j]
            hidden = gate * (1.0 / (1.0 + jnp.exp(-gate))) * accu[i, j] * weight
            hid[i, j] = hidden.astype(jnp.bfloat16)

    for p in range(3):
        links.send_wait(("a1", p), whole(p, (0, 0, 3)))
        links.send_wait(("a2", p), whole(p, (0, 3, 4)))
        links.send_wait(("a3", p), whole(p, (3, 4, 4)))
        links.send_wait(("dd", p), whole(p, (4, 4, 4)))

    def layer2(p, spots, half, extra=None):
        ats = places(p, spots)
        cols = pl.ds(starts[p] * TILE, data_parts[p] * TILE)
        rows = stacked([hid[at] for at in ats])
        got = jnp.dot(rows, wd[half, :, cols], preferred_element_type=jnp.float32)
        for at, part in apart(got, ats):
            if extra is not None:
                part = part + extra[at + (slice(None), cols)].astype(jnp.float32)
            xs[(half,) + at + (slice(None), cols)] = part.astype(jnp.bfloat16)

    def add_in(p, moves, piece, sources):
        at = chips(p, moves)
        free = [a for a in range(3) if isinstance(at[a], slice)]
        cols = columns(p, piece)
        width = piece[1] * TILE

        def one(i):
            unit = tuple(i if a in free else at[a] for a in range(3))
            index = (core,) + unit + (slice(None), cols)
            total = xs[index].astype(jnp.float32)
            for ref, lead, first in sources:
                lead = tuple(i if isinstance(l, slice) else l for l in lead)
                total = total + ref[lead + (slice(None), pl.ds(first, width))].astype(jnp.float32)
            xs[index] = total.astype(jnp.bfloat16)

        if free:
            pl.loop(0, 4)(one)
        else:
            one(0)

    def block(p, lead):
        lead = tuple(pl.ds(0, n) if n else 0 for n in lead)
        return dd.at[lead + (slice(None), columns(p, (0, data_parts[p])))]

    def spots_of(line):
        return OWN if line is None else ((line, 2), (line, 1), (line, -1))

    def make(p, line):
        spots = spots_of(line)
        layer2(p, spots, other)
        for at in places(p, spots):
            at = at + (slice(None), columns(p, (0, data_parts[p])))
            links.start(("rd", p), ("rd", p, line), xs.at[(other,) + at], dd.at[at], sibling)

    def near_place(p, line):
        at = chips(p, (None, line, 0))
        return tuple(at[a] for a in range(3) if a != ORDERS[p][2])

    def scatter(key, m, p, moves, piece, dst, axis, by):
        links.start((key, p), (key, p) + m, rows_at(p, moves, piece), dst, device(axis, by))

    def far1(p, line):
        for d, by in DIRS:
            piece = cut(data_parts[p])[d]
            dst = r1a.at[
                (d,) + near_place(p, line) + (slice(None), pl.ds(starts[p] // 2 * TILE, piece[1] * TILE))
            ]
            scatter("r1", (line, 0), p, (None, line, 2), piece, dst, ORDERS[p][2], by)

    def near1(p, line, d, m):
        by = (1, -1)[d]
        piece = cut(data_parts[p])[d if m == 2 else 1 - d]
        dst = r2a.at[(d,) + near_place(p, line) + (slice(None), columns(p, piece))]
        scatter("r1", (line, 1), p, (None, line, by), piece, dst, ORDERS[p][2], by)

    def pass1(p, line):
        links.recv_wait(("r1", p, line, 0), block(p, (0, 0, 4)))
        for d, by in DIRS:
            piece = cut(data_parts[p])[d]
            add_in(p, (None, line, by), piece, ((r1a, (d,) + near_place(p, line), starts[p] // 2 * TILE),))
            near1(p, line, d, 2)

    def end1(p, line):
        links.recv_wait(("r1", p, line, 1), block(p, (0, 2, 4)))
        place = near_place(p, line)
        first = starts[p] * TILE
        add_in(
            p, (None, line, 0), (0, data_parts[p]), ((r2a, (0,) + place, first), (r2a, (1,) + place, first))
        )

    def far2(p):
        for d, by in DIRS:
            piece = cut(data_parts[p])[d]
            dst = r1b.at[d, :, :, pl.ds(starts[p] // 2 * TILE, piece[1] * TILE)]
            scatter("r2", (0,), p, (None, 2, 0), piece, dst, ORDERS[p][1], by)

    def near2(p, d, m):
        by = (1, -1)[d]
        piece = cut(data_parts[p])[d if m == 2 else 1 - d]
        dst = r2b.at[d, :, :, columns(p, piece)]
        scatter("r2", (1,), p, (None, by, 0), piece, dst, ORDERS[p][1], by)

    def pass2(p):
        links.recv_wait(("r2", p, 0), block(p, (0, 0, 4)))
        for d, by in DIRS:
            piece = cut(data_parts[p])[d]
            add_in(p, (None, by, 0), piece, ((r1b, (d, slice(None)), starts[p] // 2 * TILE),))
            near2(p, d, 2)

    def end2(p):
        links.recv_wait(("r2", p, 1), block(p, (0, 2, 4)))
        first = starts[p] * TILE
        add_in(
            p,
            (None, 0, 0),
            (0, data_parts[p]),
            ((r2b, (0, slice(None)), first), (r2b, (1, slice(None)), first)),
        )

    def units(p):
        piece = (0, data_parts[p])
        for i, by in ((2, 2), (0, 1), (1, -1)):
            dst = rc.at[i, :, columns(p, piece)]
            scatter("r3", (), p, (by, 0, 0), piece, dst, ORDERS[p][0], by)

    def end3(p):
        links.recv_wait(("r3", p), block(p, (0, 0, 3)))
        first = starts[p] * TILE
        add_in(p, (0, 0, 0), (0, data_parts[p]), tuple((rc, (i,), first) for i in range(3)))

    BACK = (2, 1, -1, 0)

    def settle(p, line):
        links.recv_wait(("rd", p, line), block(p, (0, 4 if line is None else 3, 4)))
        layer2(p, spots_of(line), core, dd)
        if line is not None:
            far1(p, line)
            for d in range(2):
                near1(p, line, d, 1)

    def onward(line):
        for p in range(3):
            end1(p, line)
            if line == 2:
                far2(p)
            elif line != 0:
                near2(p, 0 if line == 1 else 1, 1)

    begin, first_page, span = 0, 0, 0
    for i in range(tree_sizes.shape[1]):
        size = tree_sizes[0, i]
        inside = (begin <= ep) & (ep < begin + size)
        first_page = jnp.where(inside, begin, first_page)
        span = jnp.where(inside, size, span)
        begin = begin + size
    first_slot = jnp.clip(first_page - ep + 2, 0, 2)

    def dot_t(a, b):
        return lax.dot_general(a, b, (((1,), (1,)), ((), ())), preferred_element_type=jnp.float32)

    def attend(i):
        leaves = (2 * i, 2 * i + 1)
        rows = q_all[pl.ds(2 * i, 2)].reshape(2 * q_all.shape[1], q_all.shape[2])
        scores = []
        for k in range(3):
            got = jnp.dot(rows, window[first_slot + k], preferred_element_type=jnp.float32) * score_scale
            scores.append(jnp.where(k < span, got, -1e30))
        near = [
            jnp.dot(q_all[leaf], near_all[leaf], preferred_element_type=jnp.float32) * score_scale
            for leaf in leaves
        ]
        scores.append(jnp.concatenate(near, axis=0))
        top = scores[3].max(axis=1, keepdims=True)
        for k in range(3):
            top = jnp.maximum(top, scores[k].max(axis=1, keepdims=True))
        weights = [jnp.exp(got - top) for got in scores]
        total = weights[3].sum(axis=1, keepdims=True)
        for k in range(3):
            total = total + weights[k].sum(axis=1, keepdims=True)
        probs = [got.astype(jnp.bfloat16) for got in weights]
        heads = q_all.shape[1]
        mixed = jnp.concatenate(
            [
                dot_t(probs[3][n * heads : (n + 1) * heads], near_all[leaf, pl.ds(0, LATENT)])
                for n, leaf in enumerate(leaves)
            ],
            axis=0,
        )
        for k in range(3):
            mixed = mixed + dot_t(probs[k], window[first_slot + k, pl.ds(0, LATENT)])
        mixed_all[pl.ds(2 * i, 2)] = (mixed / total).astype(jnp.bfloat16).reshape(2, heads, LATENT)
        pltpu.make_async_copy(mixed_all.at[pl.ds(2 * i, 2)], context.at[pl.ds(2 * i, 2)], asem.at[3 + i]).start()

    tasks = [(p, line) for line in BACK + (None,) for p in range(3)]
    make(*tasks[0])
    make(*tasks[1])
    for n, task in enumerate(tasks):
        if n + 2 < len(tasks):
            make(*tasks[n + 2])
        settle(*task)
        if n == 5:
            for p in range(3):
                pass1(p, 2)
            links.recv_wait("page", window.at[pl.ds(0, 2)])
            links.start("page", "near", window.at[4 * other], window.at[3 - 2 * core], sibling)
        if n == 8:
            for p in range(3):
                pass1(p, 1)
            for load in att_loads:
                load.wait()
            links.recv_wait("near", window.at[pl.ds(0, 2)])
            attend(0)
    for p in range(3):
        pass1(p, -1)
    onward(2)
    attend(1)
    onward(1)
    for p in range(3):
        pass1(p, 0)
    onward(-1)
    attend(2)
    for p in range(3):
        pass2(p)
    for p in range(3):
        end1(p, 0)
    attend(3)
    for p in range(3):
        end2(p)
        units(p)
    for p in range(3):
        end3(p)

    total = xs[core, x, y, z, :, pl.ds(0, half_cols)].astype(jnp.float32)
    low, high = total[:8], total[8:]
    backsrc[...] = jnp.where(core == 0, high, low)
    links.start("back", "back", backsrc, exback, sibling)
    mine = jnp.where(core == 0, low, high)
    for p in range(3):
        links.send_wait(("rd", p), block(p, (4, 4, 4)))
        links.send_wait(("r1", p), block(p, (3, 4, 4)))
        links.send_wait(("r2", p), block(p, (0, 3, 4)))
        links.send_wait(("r3", p), block(p, (0, 0, 3)))
    links.send_wait("page", window.at[pl.ds(0, 4)])
    links.send_wait("ex", exsrc)
    for i in range(4):
        pltpu.make_async_copy(mixed_all.at[pl.ds(2 * i, 2)], context.at[pl.ds(2 * i, 2)], asem.at[3 + i]).wait()
    links.recv_wait("back", exback)
    theirs = exback[...]
    out[:, pl.ds(0, half_cols)] = jnp.where(core == 0, mine, theirs).astype(jnp.bfloat16)
    out[:, pl.ds(half_cols, half_cols)] = jnp.where(core == 0, theirs, mine).astype(jnp.bfloat16)
    links.send_wait("back", backsrc)


def local(
    hidden_rows,
    expert_ids,
    gate_weights,
    w_gate,
    w_up,
    w_down,
    queries,
    suffix_cache,
    prefix_pages,
    tree_sizes,
):
    leaves, width = hidden_rows.shape
    half = width // 2
    ffq = w_gate.shape[2]
    pairs = half // TILE // 2
    data_parts = [2 * ((pairs + 2 - p) // 3) for p in range(3)]
    grid = (4, 4, 4)
    bf16, f32 = jnp.bfloat16, jnp.float32
    first_cut = sum(cut(n)[0][1] for n in data_parts) * TILE
    heads, channels = queries.shape[1:]
    suffix_cache, prefix_pages = jnp.swapaxes(suffix_cache, 1, 2), jnp.swapaxes(prefix_pages, 1, 2)
    shapes = [
        ((2,) + grid + (ROWS, half + TILE), bf16),
        ((2, half, ffq), bf16),
        ((2, half, ffq), bf16),
        ((2, ffq, half), bf16),
        (grid + (ROWS, ffq), f32),
        (grid + (ROWS, ffq), f32),
        (grid + (ROWS, ffq), bf16),
        (grid + (ROWS, half), bf16),
        ((2, 4, 4, ROWS, first_cut), bf16),
        ((2, 4, 4, ROWS, half), bf16),
        ((2, 4, ROWS, first_cut), bf16),
        ((2, 4, ROWS, half), bf16),
        ((3, ROWS, half), bf16),
        ((leaves, half + TILE), f32),
        ((leaves, half + TILE), f32),
        ((leaves, half), f32),
        ((leaves, half), f32),
        ((5,) + prefix_pages.shape[1:], bf16),
        (queries.shape, bf16),
        (suffix_cache.shape, bf16),
        ((leaves, heads, LATENT), bf16),
    ]
    scratch = [pltpu.VMEM(shape, kind) for shape, kind in shapes]
    scratch += [pltpu.SemaphoreType.DMA((n,)) for n in (6, 7, 27, 118)]
    vmem, hbm = pl.BlockSpec(memory_space=pltpu.VMEM), pl.BlockSpec(memory_space=pl.ANY)
    smem = pl.BlockSpec(memory_space=pltpu.SMEM)
    return pl.pallas_call(
        functools.partial(kernel, data_parts),
        out_shape=(
            jax.ShapeDtypeStruct((leaves, heads, LATENT), bf16),
            jax.ShapeDtypeStruct((leaves, width), bf16),
        ),
        in_specs=[vmem] * 3 + [smem] + [hbm] * 6,
        out_specs=(hbm, vmem),
        scratch_shapes=scratch,
        compiler_params=pltpu.CompilerParams(
            collective_id=0, has_side_effects=True, vmem_limit_bytes=63 * 1024 * 1024
        ),
        name="experts",
    )(
        hidden_rows,
        expert_ids,
        gate_weights,
        tree_sizes,
        w_gate,
        w_up,
        w_down,
        queries,
        suffix_cache,
        prefix_pages,
    )


def solution(mesh):
    return jax.shard_map(
        local,
        mesh=mesh,
        in_specs=(
            P(("dp", "ep"), None),
            P(("dp", "ep"), None),
            P(("dp", "ep"), None),
            P("ep", None, "dp"),
            P("ep", None, "dp"),
            P("ep", "dp", None),
            P(("dp", "ep"), None, None),
            P(("dp", "ep"), None, None),
            P(("dp", "ep"), None, None),
            P("dp", None),
        ),
        out_specs=(P(("dp", "ep"), None, None), P(("dp", "ep"), None)),
        check_vma=False,
    )
```

```python
import functools

import jax
import jax.numpy as jnp
from jax import lax
from jax.experimental import pallas as pl
from jax.experimental.pallas import tpu as pltpu
from jax.sharding import PartitionSpec as P

LATENT = 512
TILE = 128
CHUNK = 256
ROWS = 16
score_scale = 192.0 ** (-0.5)
MESH = pl.DeviceIdType.MESH
LINES = (0, 1, -1, 2)
ORDERS = ((1, 2, 0), (2, 0, 1), (0, 1, 2))


class Links:
    def __init__(self, send, recv):
        self.send, self.recv = send, recv
        self.sent, self.got = {}, {}

    def start(self, sent, got, src, dst, device):
        pltpu.make_async_remote_copy(
            src_ref=src,
            dst_ref=dst,
            send_sem=self.send.at[self.sent.setdefault(sent, len(self.sent))],
            recv_sem=self.recv.at[self.got.setdefault(got, len(self.got))],
            device_id=device,
            device_id_type=MESH,
        ).start()

    def recv_wait(self, got, ref):
        pltpu.make_async_copy(ref, ref, self.recv.at[self.got[got]]).wait()

    def send_wait(self, sent, ref):
        pltpu.make_async_copy(ref, ref, self.send.at[self.sent[sent]]).wait()


def cut(part_tiles):
    first = (part_tiles + 1) // 2
    return ((0, first), (first, part_tiles - first))


def kernel(
    data_parts,
    hidden_rows,
    expert_ids,
    gate_weights,
    tree_sizes,
    wg_hbm,
    wu_hbm,
    wd_hbm,
    queries,
    suffix,
    page,
    context,
    out,
    xs,
    wg,
    wu,
    wd,
    accg,
    accu,
    hid,
    dd,
    r1a,
    r2a,
    r1b,
    r2b,
    rc,
    exsrc,
    exin,
    backsrc,
    exback,
    window,
    q_all,
    near_all,
    mixed_all,
    wsem,
    asem,
    send_sem,
    recv_sem,
):
    ffq = wg.shape[2]
    half_cols = wg.shape[1]
    y = lax.axis_index("dp")
    ep = lax.axis_index("ep")
    core = lax.rem(ep, 2)
    x = ep // 8
    z = lax.rem(ep // 2, 4)
    here = (x, y, z)
    other = 1 - core

    def shift(axis, by):
        return lax.rem(here[axis] + (by + 4) % 4, 4)

    def device(axis, by):
        place = [x, y, z]
        place[axis] = shift(axis, by)
        return (place[1], place[0] * 8 + place[2] * 2 + core)

    sibling = (y, x * 8 + z * 2 + other)
    ahead = (y, lax.rem(ep + 2, 32))
    behind = (y, lax.rem(ep + 30, 32))

    barrier = pltpu.get_barrier_semaphore()
    greeted = [device(axis, by) for axis in range(3) for by in (1, -1, 2)] + [sibling, ahead, behind]
    for other_device in greeted:
        pl.semaphore_signal(barrier, inc=1, device_id=other_device, device_id_type=MESH)

    loads = []
    for half in range(2):
        rows = pl.ds(half * half_cols, half_cols)
        loads.append(pltpu.make_async_copy(wg_hbm.at[0, rows], wg.at[half], wsem.at[half]))
        loads.append(pltpu.make_async_copy(wu_hbm.at[0, rows], wu.at[half], wsem.at[2 + half]))
    for half in range(2):
        cols = pl.ds(half * half_cols, half_cols)
        loads.append(pltpu.make_async_copy(wd_hbm.at[0, :, cols], wd.at[half], wsem.at[4 + half]))
    att_loads = [
        pltpu.make_async_copy(queries, q_all, asem.at[0]),
        pltpu.make_async_copy(suffix, near_all, asem.at[1]),
        pltpu.make_async_copy(page.at[0], window.at[2], asem.at[2]),
    ]

    rows_low = hidden_rows[:, pl.ds(0, half_cols)].astype(jnp.float32)
    rows_high = hidden_rows[:, pl.ds(half_cols, half_cols)].astype(jnp.float32)
    lane = lax.broadcasted_iota(jnp.int32, (8, TILE), 1)
    weight = jnp.zeros((8, TILE), jnp.float32)
    for k in range(expert_ids.shape[1]):
        chosen = lane == expert_ids[:, pl.ds(k, 1)]
        weight = weight + jnp.where(chosen, gate_weights[:, pl.ds(k, 1)], 0.0)
    coarse = weight.astype(jnp.bfloat16).astype(jnp.float32)
    fine = weight - coarse
    exsrc[:, pl.ds(0, half_cols)] = jnp.where(core == 0, rows_high, rows_low)
    exsrc[:, pl.ds(half_cols, TILE)] = jnp.where(core == 0, fine, coarse)

    pl.semaphore_wait(barrier, len(greeted))
    links = Links(send_sem, recv_sem)
    links.start("ex", "ex", exsrc, exin, sibling)
    for load in loads + att_loads:
        load.start()

    starts = []
    spans = []
    for p in range(3):
        starts.append(sum(data_parts[:p]))
        spans.append(data_parts[p] + (1 if p == 2 else 0))

    links.recv_wait("ex", exin)
    theirs = exin[:, pl.ds(0, half_cols)]
    mine = jnp.where(core == 0, rows_low, rows_high)
    low = jnp.where(core == 0, mine, theirs)
    high = jnp.where(core == 0, theirs, mine)
    xs[core, 0, 0, 0, :, pl.ds(0, half_cols)] = jnp.concatenate([low, high], axis=0).astype(jnp.bfloat16)
    theirs = exin[:, pl.ds(half_cols, TILE)]
    mine = jnp.where(core == 0, coarse, fine)
    low = jnp.where(core == 0, mine, theirs)
    high = jnp.where(core == 0, theirs, mine)
    xs[core, 0, 0, 0, :, pl.ds(half_cols, TILE)] = jnp.concatenate([low, high], axis=0).astype(
        jnp.bfloat16
    )

    REST = slice(1, 4)

    def chips(p, moves):
        index = [None, None, None]
        for axis, by in zip(ORDERS[p], moves):
            index[axis] = slice(0, 4) if by is None else by if isinstance(by, slice) else by % 4
        return tuple(index)

    def columns(p, piece):
        return pl.ds((starts[p] + piece[0]) * TILE, piece[1] * TILE)

    def rows_at(p, moves, piece):
        return xs.at[(core,) + chips(p, moves) + (slice(None), columns(p, piece))]

    def whole(p, lead):
        lead = tuple(pl.ds(0, n) if n else 0 for n in lead)
        return xs.at[(0,) + lead + (slice(None), columns(p, (0, spans[p])))]

    def gather(key, m, p, moves, piece, axis, by):
        there = [move - by if a == axis else move for a, move in zip(ORDERS[p], moves)]
        links.start(
            (key, p), (key, p) + m, rows_at(p, moves, piece), rows_at(p, there, piece), device(axis, by)
        )

    def share(name, p, by, line):
        ref = rows_at(p, (None, line, by), (0, spans[p]))
        links.start(("dd", p), ("dd", p, name), ref, ref, sibling)

    DIRS = ((0, 1), (1, -1))

    def start2(p, unit):
        pieces = cut(spans[p])
        for m in range(2):
            for d, by in DIRS:
                gather("a2", (m,), p, (unit, 0, 0), pieces[d ^ m], ORDERS[p][1], by)

    def wait2(p, m):
        links.recv_wait(("a2", p, m), whole(p, (0, 0, 4)))

    def forward2(p):
        wait2(p, 0)
        for d, by in DIRS:
            gather("a2", (2,), p, (None, -by, 0), cut(spans[p])[d], ORDERS[p][1], by)

    def start3(p, line, m, unit=None):
        pieces = cut(spans[p])
        for d, by in DIRS:
            gather("a3", (line, m), p, (unit, line, 0), pieces[d ^ m], ORDERS[p][2], by)

    def wait3(p, line, m):
        links.recv_wait(("a3", p, line, m), whole(p, (0, 0, 4)))

    def forward3(p, line):
        wait3(p, line, 0)
        for d, by in DIRS:
            gather("a3", (line, 2), p, (None, line, -by), cut(spans[p])[d], ORDERS[p][2], by)

    OWN = ((None, 0),)

    def places(p, spots):
        return [chips(p, (None, line, by)) for line, by in spots]

    def stacked(parts):
        parts = [part.reshape(-1, part.shape[-1]) for part in parts]
        return parts[0] if len(parts) == 1 else jnp.concatenate(parts, axis=0)

    def apart(value, ats):
        first = 0
        for at in ats:
            lead = (4,) * sum(isinstance(i, slice) for i in at)
            count = 4 ** len(lead) * ROWS
            yield at, value[first : first + count].reshape(lead + (ROWS, value.shape[-1]))
            first += count

    def layer1(p, spots):
        ats = places(p, spots)
        cols = pl.ds(starts[p] * TILE, data_parts[p] * TILE)
        x0, x1 = [stacked([xs[(half,) + at + (slice(None), cols)] for at in ats]) for half in range(2)]
        for acc, w in ((accg, wg), (accu, wu)):
            got = jnp.dot(x0, w[0, cols, :], preferred_element_type=jnp.float32)
            got = got + jnp.dot(x1, w[1, cols, :], preferred_element_type=jnp.float32)
            for at, rows in apart(got, ats):
                acc[at] += rows

    for p in range(3):
        for by in (1, -1, 2):
            gather("a1", (), p, (0, 0, 0), (0, spans[p]), ORDERS[p][0], by)
    for p in range(3):
        start2(p, 0)
    for p in range(3):
        start3(p, 0, 0, 0)
        start3(p, 0, 1, 0)

    @pl.loop(0, 4)
    def _(i):
        accg[i] = jnp.zeros_like(accg[i])
        accu[i] = jnp.zeros_like(accu[i])

    def beside(line):
        for p in range(3):
            wait3(p, line, 1)
            share(("near", line), p, 1, line)
            share(("near", line), p, -1, line)

    def far(line):
        for p in range(3):
            wait3(p, line, 2)
            share(("far", line), p, 2, line)

    def first_own(p):
        links.recv_wait(("dd", p, "own"), whole(p, (0, 4, 4)))
        layer1(p, OWN)

    def first_near(p, line):
        links.recv_wait(("dd", p, ("near", line)), whole(p, (0, 2, 4)))
        layer1(p, ((line, 1), (line, -1)))

    def first_far(p, line):
        links.recv_wait(("dd", p, ("far", line)), whole(p, (0, 0, 4)))
        layer1(p, ((line, 2),))

    for p in range(3):
        links.recv_wait(("a1", p), whole(p, (0, 0, 3)))
        start2(p, REST)
    for p in range(3):
        start3(p, 0, 0, REST)
        start3(p, 0, 1, REST)
        share("own", p, 0, 0)
    for p in range(3):
        forward2(p)
    for p in range(3):
        wait2(p, 1)
        start3(p, 1, 0)
        start3(p, -1, 0)
        share("own", p, 0, 1)
        share("own", p, 0, -1)
    for p in range(3):
        forward3(p, 0)
        start3(p, 1, 1)
    beside(0)
    for p in range(3):
        wait2(p, 2)
        share("own", p, 0, 2)
        start3(p, 2, 0)
        start3(p, -1, 1)
    for load in loads:
        load.wait()
    for p in range(3):
        forward3(p, 1)
        first_own(p)
    for p in range(3):
        forward3(p, -1)
        start3(p, 2, 1)
    far(0)
    first_near(0, 0)
    first_near(1, 0)
    beside(1)
    first_near(2, 0)
    for p in range(3):
        forward3(p, 2)
    for p in range(3):
        first_far(p, 0)
    beside(-1)
    for p in range(3):
        first_near(p, 1)
    far(1)
    first_near(0, -1)
    first_near(1, -1)
    far(-1)
    first_near(2, -1)
    first_far(0, 1)
    beside(2)
    first_far(1, 1)
    first_far(2, 1)
    for p in range(3):
        first_far(p, -1)
    first_near(0, 2)
    far(2)
    links.start("page", "page", page.at[0], window.at[0], ahead)
    links.start("page", "page", page.at[0], window.at[4], behind)
    links.start("page", "near", page.at[0], window.at[1 + 2 * core], sibling)
    first_near(1, 2)
    first_near(2, 2)
    for p in range(3):
        first_far(p, 2)

    @pl.loop(0, 4)
    def _(i):
        @pl.loop(0, 4)
        def _(j):
            tile = pl.ds(half_cols, TILE)
            weight = xs[0, i, j, :, :, tile].astype(jnp.float32) + xs[1, i, j, :, :, tile].astype(
                jnp.float32
            )
            lane = lax.broadcasted_iota(jnp.int32, weight.shape, 2)
            weight = jnp.sum(jnp.where(lane == ep, weight, 0.0), axis=2, keepdims=True)
            gate = accg[i, j]
            hidden = gate * (1.0 / (1.0 + jnp.exp(-gate))) * accu[i, j] * weight
            hid[i, j] = hidden.astype(jnp.bfloat16)

    for p in range(3):
        links.send_wait(("a1", p), whole(p, (0, 0, 3)))
        links.send_wait(("a2", p), whole(p, (0, 3, 4)))
        links.send_wait(("a3", p), whole(p, (3, 4, 4)))
        links.send_wait(("dd", p), whole(p, (4, 4, 4)))

    def layer2(p, spots, half, extra=None):
        ats = places(p, spots)
        cols = pl.ds(starts[p] * TILE, data_parts[p] * TILE)
        rows = stacked([hid[at] for at in ats])
        got = jnp.dot(rows, wd[half, :, cols], preferred_element_type=jnp.float32)
        for at, part in apart(got, ats):
            if extra is not None:
                part = part + extra[at + (slice(None), cols)].astype(jnp.float32)
            xs[(half,) + at + (slice(None), cols)] = part.astype(jnp.bfloat16)

    def add_in(p, moves, piece, sources):
        at = chips(p, moves)
        free = [a for a in range(3) if isinstance(at[a], slice)]
        cols = columns(p, piece)
        width = piece[1] * TILE

        def one(i):
            unit = tuple(i if a in free else at[a] for a in range(3))
            index = (core,) + unit + (slice(None), cols)
            total = xs[index].astype(jnp.float32)
            for ref, lead, first in sources:
                lead = tuple(i if isinstance(l, slice) else l for l in lead)
                total = total + ref[lead + (slice(None), pl.ds(first, width))].astype(jnp.float32)
            xs[index] = total.astype(jnp.bfloat16)

        if free:
            pl.loop(at[free[0]].start, at[free[0]].stop)(one)
        else:
            one(0)

    def block(p, lead):
        lead = tuple(pl.ds(0, n) if n else 0 for n in lead)
        return dd.at[lead + (slice(None), columns(p, (0, data_parts[p])))]

    def make(p, name, spots):
        layer2(p, spots, other)
        for at in places(p, spots):
            at = at + (slice(None), columns(p, (0, data_parts[p])))
            links.start(("rd", p), ("rd", p, name), xs.at[(other,) + at], dd.at[at], sibling)

    def near_place(p, line, unit=None):
        at = chips(p, (unit, line, 0))
        return tuple(at[a] for a in range(3) if a != ORDERS[p][2])

    def scatter(key, m, p, moves, piece, dst, axis, by):
        links.start((key, p), (key, p) + m, rows_at(p, moves, piece), dst, device(axis, by))

    def far1(p, line):
        for d, by in DIRS:
            piece = cut(data_parts[p])[d]
            dst = r1a.at[
                (d,) + near_place(p, line) + (slice(None), pl.ds(starts[p] // 2 * TILE, piece[1] * TILE))
            ]
            scatter("r1", (line, 0), p, (None, line, 2), piece, dst, ORDERS[p][2], by)

    def near1(p, line, m, unit=None):
        last = "last" if unit == 0 else 1
        for d, by in DIRS:
            piece = cut(data_parts[p])[d if m == 2 else 1 - d]
            dst = r2a.at[(d,) + near_place(p, line, unit) + (slice(None), columns(p, piece))]
            scatter("r1", (line, last), p, (unit, line, by), piece, dst, ORDERS[p][2], by)

    def pass1(p, line, unit=None):
        if unit != 0:
            links.recv_wait(("r1", p, line, 0), block(p, (0, 0, 4)))
        for d, by in DIRS:
            piece = cut(data_parts[p])[d]
            place = (d,) + near_place(p, line, unit)
            add_in(p, (unit, line, by), piece, ((r1a, place, starts[p] // 2 * TILE),))
        near1(p, line, 2, unit)

    def lead_of(unit):
        return (0, 0, 2) if unit == 0 else (0, 2, 3) if unit == REST else (0, 2, 4)

    def end1(p, line, unit=None):
        links.recv_wait(("r1", p, line, "last" if unit == 0 else 1), block(p, lead_of(unit)))
        place = near_place(p, line, unit)
        first = starts[p] * TILE
        add_in(
            p,
            (unit, line, 0),
            (0, data_parts[p]),
            ((r2a, (0,) + place, first), (r2a, (1,) + place, first)),
        )

    def far2(p):
        for d, by in DIRS:
            piece = cut(data_parts[p])[d]
            dst = r1b.at[d, :, :, pl.ds(starts[p] // 2 * TILE, piece[1] * TILE)]
            scatter("r2", (0,), p, (None, 2, 0), piece, dst, ORDERS[p][1], by)

    def near2(p, d, m, unit):
        by = (1, -1)[d]
        piece = cut(data_parts[p])[d if m == 2 else 1 - d]
        dst = r2b.at[d, unit, :, columns(p, piece)]
        scatter("r2", ("last" if unit == 0 else 1,), p, (unit, by, 0), piece, dst, ORDERS[p][1], by)

    def pass2(p):
        links.recv_wait(("r2", p, 0), block(p, (0, 0, 4)))
        for d, by in DIRS:
            piece = cut(data_parts[p])[d]
            add_in(p, (None, by, 0), piece, ((r1b, (d, slice(None)), starts[p] // 2 * TILE),))
            near2(p, d, 2, REST)

    def end2(p, unit):
        links.recv_wait(("r2", p, "last" if unit == 0 else 1), block(p, lead_of(unit)))
        first = starts[p] * TILE
        add_in(
            p,
            (unit, 0, 0),
            (0, data_parts[p]),
            ((r2b, (0, unit), first), (r2b, (1, unit), first)),
        )

    def units(p):
        piece = (0, data_parts[p])
        for i, by in ((2, 2), (0, 1), (1, -1)):
            dst = rc.at[i, :, columns(p, piece)]
            scatter("r3", (), p, (by, 0, 0), piece, dst, ORDERS[p][0], by)

    def end3(p):
        links.recv_wait(("r3", p), block(p, (0, 0, 3)))
        first = starts[p] * TILE
        add_in(p, (0, 0, 0), (0, data_parts[p]), tuple((rc, (i,), first) for i in range(3)))

    BACK = (2, 1, -1, 0)

    def settle(p, name, spots):
        links.recv_wait(("rd", p, name), block(p, (0, 4 if name == "own" else len(spots), 4)))
        layer2(p, spots, core, dd)

    def onward(line):
        for p in range(3):
            end1(p, line)
            if line == 2:
                far2(p)
            else:
                near2(p, 0 if line == 1 else 1, 1, REST)

    begin, first_page, span = 0, 0, 0
    for i in range(tree_sizes.shape[1]):
        size = tree_sizes[0, i]
        inside = (begin <= ep) & (ep < begin + size)
        first_page = jnp.where(inside, begin, first_page)
        span = jnp.where(inside, size, span)
        begin = begin + size
    first_slot = jnp.clip(first_page - ep + 2, 0, 2)

    def dot_t(a, b):
        return lax.dot_general(a, b, (((1,), (1,)), ((), ())), preferred_element_type=jnp.float32)

    def attend(i):
        leaves = (2 * i, 2 * i + 1)
        rows = q_all[pl.ds(2 * i, 2)].reshape(2 * q_all.shape[1], q_all.shape[2])
        scores = []
        for k in range(3):
            got = jnp.dot(rows, window[first_slot + k], preferred_element_type=jnp.float32) * score_scale
            scores.append(jnp.where(k < span, got, -1e30))
        near = [
            jnp.dot(q_all[leaf], near_all[leaf], preferred_element_type=jnp.float32) * score_scale
            for leaf in leaves
        ]
        scores.append(jnp.concatenate(near, axis=0))
        top = scores[3].max(axis=1, keepdims=True)
        for k in range(3):
            top = jnp.maximum(top, scores[k].max(axis=1, keepdims=True))
        weights = [jnp.exp(got - top) for got in scores]
        total = weights[3].sum(axis=1, keepdims=True)
        for k in range(3):
            total = total + weights[k].sum(axis=1, keepdims=True)
        probs = [got.astype(jnp.bfloat16) for got in weights]
        heads = q_all.shape[1]
        mixed = jnp.concatenate(
            [
                dot_t(probs[3][n * heads : (n + 1) * heads], near_all[leaf, pl.ds(0, LATENT)])
                for n, leaf in enumerate(leaves)
            ],
            axis=0,
        )
        for k in range(3):
            mixed = mixed + dot_t(probs[k], window[first_slot + k, pl.ds(0, LATENT)])
        mixed_all[pl.ds(2 * i, 2)] = (mixed / total).astype(jnp.bfloat16).reshape(2, heads, LATENT)
        pltpu.make_async_copy(mixed_all.at[pl.ds(2 * i, 2)], context.at[pl.ds(2 * i, 2)], asem.at[3 + i]).start()

    FAR, NEAR = ((2, 2),), ((2, 1), (2, -1))
    for p in range(3):
        make(p, "far", FAR)
    for p in range(3):
        make(p, "near", NEAR)
        settle(p, "far", FAR)
        far1(p, 2)
    tasks = [(p, line, ((line, 2), (line, 1), (line, -1))) for line in BACK[1:] for p in range(3)]
    tasks += [(p, "own", OWN) for p in range(3)]
    make(*tasks[0])
    settle(0, "near", NEAR)
    near1(0, 2, 1)
    make(*tasks[1])
    for p in (1, 2):
        settle(p, "near", NEAR)
        near1(p, 2, 1)
    for n, (p, line, spots) in enumerate(tasks):
        if n + 2 < len(tasks):
            make(*tasks[n + 2])
        settle(p, line, spots)
        if line != "own":
            far1(p, line)
            near1(p, line, 1, REST if line == 0 else None)
        if n == 2:
            for q in range(3):
                pass1(q, 2)
            links.recv_wait("page", window.at[pl.ds(0, 2)])
            links.start("page", "near", window.at[4 * other], window.at[3 - 2 * core], sibling)
        if n == 5:
            for q in range(3):
                pass1(q, 1)
            for load in att_loads:
                load.wait()
            links.recv_wait("near", window.at[pl.ds(0, 2)])
            attend(0)
    for p in range(3):
        pass1(p, -1)
    onward(2)
    attend(1)
    onward(1)
    for p in range(3):
        pass1(p, 0, REST)
    onward(-1)
    attend(2)
    for p in range(3):
        pass2(p)
    for p in range(3):
        near1(p, 0, 1, 0)
        pass1(p, 0, 0)
    for p in range(3):
        for d in range(2):
            near2(p, d, 1, 0)
            near2(p, d, 2, 0)
    attend(3)
    for p in range(3):
        end1(p, 0, REST)
    for p in range(3):
        end2(p, REST)
        units(p)
    for p in range(3):
        end1(p, 0, 0)
        end2(p, 0)
    for p in range(3):
        end3(p)

    total = xs[core, 0, 0, 0, :, pl.ds(0, half_cols)].astype(jnp.float32)
    low, high = total[:8], total[8:]
    backsrc[...] = jnp.where(core == 0, high, low)
    links.start("back", "back", backsrc, exback, sibling)
    mine = jnp.where(core == 0, low, high)
    for p in range(3):
        links.send_wait(("rd", p), block(p, (4, 4, 4)))
        links.send_wait(("r1", p), block(p, (3, 4, 4)))
        links.send_wait(("r2", p), block(p, (0, 3, 4)))
        links.send_wait(("r3", p), block(p, (0, 0, 3)))
    links.send_wait("page", window.at[pl.ds(0, 4)])
    links.send_wait("ex", exsrc)
    for i in range(4):
        pltpu.make_async_copy(mixed_all.at[pl.ds(2 * i, 2)], context.at[pl.ds(2 * i, 2)], asem.at[3 + i]).wait()
    links.recv_wait("back", exback)
    theirs = exback[...]
    out[:, pl.ds(0, half_cols)] = jnp.where(core == 0, mine, theirs).astype(jnp.bfloat16)
    out[:, pl.ds(half_cols, half_cols)] = jnp.where(core == 0, theirs, mine).astype(jnp.bfloat16)
    links.send_wait("back", backsrc)


def hand_over(context, mix, context_out, mix_out, sems):
    copies = [
        pltpu.make_async_copy(context, context_out, sems.at[0]),
        pltpu.make_async_copy(mix, mix_out, sems.at[1]),
    ]
    for copy in copies:
        copy.start()
    for copy in copies:
        copy.wait()


def local(
    hidden_rows,
    expert_ids,
    gate_weights,
    w_gate,
    w_up,
    w_down,
    queries,
    suffix_cache,
    prefix_pages,
    tree_sizes,
):
    leaves, width = hidden_rows.shape
    half = width // 2
    ffq = w_gate.shape[2]
    pairs = half // TILE // 2
    data_parts = [2 * ((pairs + 2 - p) // 3) for p in range(3)]
    grid = (4, 4, 4)
    bf16, f32 = jnp.bfloat16, jnp.float32
    first_cut = sum(cut(n)[0][1] for n in data_parts) * TILE
    heads, channels = queries.shape[1:]
    suffix_cache, prefix_pages = jnp.swapaxes(suffix_cache, 1, 2), jnp.swapaxes(prefix_pages, 1, 2)
    shapes = [
        ((2,) + grid + (ROWS, half + TILE), bf16),
        ((2, half, ffq), bf16),
        ((2, half, ffq), bf16),
        ((2, ffq, half), bf16),
        (grid + (ROWS, ffq), f32),
        (grid + (ROWS, ffq), f32),
        (grid + (ROWS, ffq), bf16),
        (grid + (ROWS, half), bf16),
        ((2, 4, 4, ROWS, first_cut), bf16),
        ((2, 4, 4, ROWS, half), bf16),
        ((2, 4, ROWS, first_cut), bf16),
        ((2, 4, ROWS, half), bf16),
        ((3, ROWS, half), bf16),
        ((leaves, half + TILE), f32),
        ((leaves, half + TILE), f32),
        ((leaves, half), f32),
        ((leaves, half), f32),
        ((5,) + prefix_pages.shape[1:], bf16),
        (queries.shape, bf16),
        (suffix_cache.shape, bf16),
        ((leaves, heads, LATENT), bf16),
    ]
    scratch = [pltpu.VMEM(shape, kind) for shape, kind in shapes]
    scratch += [pltpu.SemaphoreType.DMA((n,)) for n in (6, 7, 27, 136)]
    vmem, hbm = pl.BlockSpec(memory_space=pltpu.VMEM), pl.BlockSpec(memory_space=pl.ANY)
    smem = pl.BlockSpec(memory_space=pltpu.SMEM)
    results = pl.pallas_call(
        functools.partial(kernel, data_parts),
        out_shape=(
            jax.ShapeDtypeStruct((leaves, heads, LATENT), bf16),
            jax.ShapeDtypeStruct((leaves, width), bf16),
        ),
        in_specs=[vmem] * 3 + [smem] + [hbm] * 6,
        out_specs=(hbm, vmem),
        scratch_shapes=scratch,
        compiler_params=pltpu.CompilerParams(
            collective_id=0, has_side_effects=True, vmem_limit_bytes=63 * 1024 * 1024
        ),
        name="experts",
    )(
        hidden_rows,
        expert_ids,
        gate_weights,
        tree_sizes,
        w_gate,
        w_up,
        w_down,
        queries,
        suffix_cache,
        prefix_pages,
    )
    return pl.pallas_call(
        hand_over,
        out_shape=tuple(jax.ShapeDtypeStruct(r.shape, r.dtype) for r in results),
        in_specs=[hbm] * 2,
        out_specs=(hbm, hbm),
        scratch_shapes=[pltpu.SemaphoreType.DMA((2,))],
        compiler_params=pltpu.CompilerParams(vmem_limit_bytes=63 * 1024 * 1024),
        name="results",
    )(*results)


def solution(mesh):
    return jax.shard_map(
        local,
        mesh=mesh,
        in_specs=(
            P(("dp", "ep"), None),
            P(("dp", "ep"), None),
            P(("dp", "ep"), None),
            P("ep", None, "dp"),
            P("ep", None, "dp"),
            P("ep", "dp", None),
            P(("dp", "ep"), None, None),
            P(("dp", "ep"), None, None),
            P(("dp", "ep"), None, None),
            P("dp", None),
        ),
        out_specs=(P(("dp", "ep"), None, None), P(("dp", "ep"), None)),
        check_vma=False,
    )
```

```python
import functools

import jax
import jax.numpy as jnp
from jax import lax
from jax.experimental import pallas as pl
from jax.experimental.pallas import tpu as pltpu
from jax.sharding import PartitionSpec as P

LATENT = 512
TILE = 128
CHUNK = 256
ROWS = 16
score_scale = 192.0 ** (-0.5)
MESH = pl.DeviceIdType.MESH
LINES = (0, 1, -1, 2)
ORDERS = ((1, 2, 0), (2, 0, 1), (0, 1, 2))


class Links:
    def __init__(self, send, recv):
        self.send, self.recv = send, recv
        self.sent, self.got = {}, {}

    def start(self, sent, got, src, dst, device):
        pltpu.make_async_remote_copy(
            src_ref=src,
            dst_ref=dst,
            send_sem=self.send.at[self.sent.setdefault(sent, len(self.sent))],
            recv_sem=self.recv.at[self.got.setdefault(got, len(self.got))],
            device_id=device,
            device_id_type=MESH,
        ).start()

    def recv_wait(self, got, ref):
        pltpu.make_async_copy(ref, ref, self.recv.at[self.got[got]]).wait()

    def send_wait(self, sent, ref):
        pltpu.make_async_copy(ref, ref, self.send.at[self.sent[sent]]).wait()


def cut(part_tiles):
    first = (part_tiles + 1) // 2
    return ((0, first), (first, part_tiles - first))


def kernel(
    data_parts,
    hidden_rows,
    expert_ids,
    gate_weights,
    tree_sizes,
    wg_hbm,
    wu_hbm,
    wd_hbm,
    queries,
    suffix,
    page,
    context,
    out,
    xs,
    wg,
    wu,
    wd,
    accg,
    accu,
    hid,
    dd,
    r1a,
    r2a,
    r1b,
    r2b,
    rc,
    exsrc,
    exin,
    backsrc,
    exback,
    window,
    q_all,
    near_all,
    mixed_all,
    wsem,
    asem,
    send_sem,
    recv_sem,
):
    ffq = wg.shape[2]
    half_cols = wg.shape[1]
    y = lax.axis_index("dp")
    ep = lax.axis_index("ep")
    core = lax.rem(ep, 2)
    x = ep // 8
    z = lax.rem(ep // 2, 4)
    here = (x, y, z)
    other = 1 - core

    def shift(axis, by):
        return lax.rem(here[axis] + (by + 4) % 4, 4)

    def device(axis, by):
        place = [x, y, z]
        place[axis] = shift(axis, by)
        return (place[1], place[0] * 8 + place[2] * 2 + core)

    sibling = (y, x * 8 + z * 2 + other)
    ahead = (y, lax.rem(ep + 2, 32))
    behind = (y, lax.rem(ep + 30, 32))

    barrier = pltpu.get_barrier_semaphore()
    greeted = [device(axis, by) for axis in range(3) for by in (1, -1, 2)] + [sibling, ahead, behind]
    for other_device in greeted:
        pl.semaphore_signal(barrier, inc=1, device_id=other_device, device_id_type=MESH)

    loads = []
    for half in range(2):
        rows = pl.ds(half * half_cols, half_cols)
        loads.append(pltpu.make_async_copy(wg_hbm.at[0, rows], wg.at[half], wsem.at[half]))
        loads.append(pltpu.make_async_copy(wu_hbm.at[0, rows], wu.at[half], wsem.at[2 + half]))
    for half in range(2):
        cols = pl.ds(half * half_cols, half_cols)
        loads.append(pltpu.make_async_copy(wd_hbm.at[0, :, cols], wd.at[half], wsem.at[4 + half]))
    att_loads = [
        pltpu.make_async_copy(queries, q_all, asem.at[0]),
        pltpu.make_async_copy(suffix, near_all, asem.at[1]),
        pltpu.make_async_copy(page.at[0], window.at[2], asem.at[2]),
    ]

    rows_low = hidden_rows[:, pl.ds(0, half_cols)].astype(jnp.float32)
    rows_high = hidden_rows[:, pl.ds(half_cols, half_cols)].astype(jnp.float32)
    lane = lax.broadcasted_iota(jnp.int32, (8, TILE), 1)
    weight = jnp.zeros((8, TILE), jnp.float32)
    for k in range(expert_ids.shape[1]):
        chosen = lane == expert_ids[:, pl.ds(k, 1)]
        weight = weight + jnp.where(chosen, gate_weights[:, pl.ds(k, 1)], 0.0)
    coarse = weight.astype(jnp.bfloat16).astype(jnp.float32)
    fine = weight - coarse
    exsrc[:, pl.ds(0, half_cols)] = jnp.where(core == 0, rows_high, rows_low)
    exsrc[:, pl.ds(half_cols, TILE)] = jnp.where(core == 0, fine, coarse)

    pl.semaphore_wait(barrier, len(greeted))
    links = Links(send_sem, recv_sem)
    links.start("ex", "ex", exsrc, exin, sibling)
    for load in loads + att_loads:
        load.start()

    starts = []
    spans = []
    for p in range(3):
        starts.append(sum(data_parts[:p]))
        spans.append(data_parts[p] + (1 if p == 2 else 0))

    links.recv_wait("ex", exin)
    theirs = exin[:, pl.ds(0, half_cols)]
    mine = jnp.where(core == 0, rows_low, rows_high)
    low = jnp.where(core == 0, mine, theirs)
    high = jnp.where(core == 0, theirs, mine)
    xs[core, 0, 0, 0, :, pl.ds(0, half_cols)] = jnp.concatenate([low, high], axis=0).astype(jnp.bfloat16)
    theirs = exin[:, pl.ds(half_cols, TILE)]
    mine = jnp.where(core == 0, coarse, fine)
    low = jnp.where(core == 0, mine, theirs)
    high = jnp.where(core == 0, theirs, mine)
    xs[core, 0, 0, 0, :, pl.ds(half_cols, TILE)] = jnp.concatenate([low, high], axis=0).astype(
        jnp.bfloat16
    )

    REST = slice(1, 4)

    def chips(p, moves):
        index = [None, None, None]
        for axis, by in zip(ORDERS[p], moves):
            index[axis] = slice(0, 4) if by is None else by if isinstance(by, slice) else by % 4
        return tuple(index)

    def columns(p, piece):
        return pl.ds((starts[p] + piece[0]) * TILE, piece[1] * TILE)

    def rows_at(p, moves, piece):
        return xs.at[(core,) + chips(p, moves) + (slice(None), columns(p, piece))]

    def whole(p, lead):
        lead = tuple(pl.ds(0, n) if n else 0 for n in lead)
        return xs.at[(0,) + lead + (slice(None), columns(p, (0, spans[p])))]

    def gather(key, m, p, moves, piece, axis, by):
        there = [move - by if a == axis else move for a, move in zip(ORDERS[p], moves)]
        links.start(
            (key, p), (key, p) + m, rows_at(p, moves, piece), rows_at(p, there, piece), device(axis, by)
        )

    def share(name, p, by, line):
        ref = rows_at(p, (None, line, by), (0, spans[p]))
        links.start(("dd", p), ("dd", p, name), ref, ref, sibling)

    DIRS = ((0, 1), (1, -1))

    def start2(p, unit):
        pieces = cut(spans[p])
        for m in range(2):
            for d, by in DIRS:
                gather("a2", (m,), p, (unit, 0, 0), pieces[d ^ m], ORDERS[p][1], by)

    def wait2(p, m):
        links.recv_wait(("a2", p, m), whole(p, (0, 0, 4)))

    def forward2(p):
        wait2(p, 0)
        for d, by in DIRS:
            gather("a2", (2,), p, (None, -by, 0), cut(spans[p])[d], ORDERS[p][1], by)

    def start3(p, line, m, unit=None):
        pieces = cut(spans[p])
        for d, by in DIRS:
            gather("a3", (line, m), p, (unit, line, 0), pieces[d ^ m], ORDERS[p][2], by)

    def wait3(p, line, m):
        links.recv_wait(("a3", p, line, m), whole(p, (0, 0, 4)))

    def forward3(p, line):
        wait3(p, line, 0)
        for d, by in DIRS:
            gather("a3", (line, 2), p, (None, line, -by), cut(spans[p])[d], ORDERS[p][2], by)

    OWN = ((None, 0),)

    def places(p, spots):
        return [chips(p, (None, line, by)) for line, by in spots]

    def stacked(parts):
        parts = [part.reshape(-1, part.shape[-1]) for part in parts]
        return parts[0] if len(parts) == 1 else jnp.concatenate(parts, axis=0)

    def apart(value, ats):
        first = 0
        for at in ats:
            lead = (4,) * sum(isinstance(i, slice) for i in at)
            count = 4 ** len(lead) * ROWS
            yield at, value[first : first + count].reshape(lead + (ROWS, value.shape[-1]))
            first += count

    def layer1(p, spots):
        ats = places(p, spots)
        cols = pl.ds(starts[p] * TILE, data_parts[p] * TILE)
        x0, x1 = [stacked([xs[(half,) + at + (slice(None), cols)] for at in ats]) for half in range(2)]
        for acc, w in ((accg, wg), (accu, wu)):
            got = jnp.dot(x0, w[0, cols, :], preferred_element_type=jnp.float32)
            got = got + jnp.dot(x1, w[1, cols, :], preferred_element_type=jnp.float32)
            for at, rows in apart(got, ats):
                acc[at] += rows

    for p in range(3):
        for by in (1, -1, 2):
            gather("a1", (), p, (0, 0, 0), (0, spans[p]), ORDERS[p][0], by)
    for p in range(3):
        start2(p, 0)
    for p in range(3):
        start3(p, 0, 0, 0)
        start3(p, 0, 1, 0)

    @pl.loop(0, 4)
    def _(i):
        accg[i] = jnp.zeros_like(accg[i])
        accu[i] = jnp.zeros_like(accu[i])

    def beside(line):
        for p in range(3):
            wait3(p, line, 1)
            share(("near", line), p, 1, line)
            share(("near", line), p, -1, line)

    def far(line):
        for p in range(3):
            wait3(p, line, 2)
            share(("far", line in (0, 1)), p, 2, line)

    def first_own(p):
        links.recv_wait(("dd", p, "own"), whole(p, (0, 4, 4)))
        layer1(p, OWN)

    def first_near(p, line):
        links.recv_wait(("dd", p, ("near", line)), whole(p, (0, 2, 4)))
        layer1(p, ((line, 1), (line, -1)))

    def first_far(p, lines):
        links.recv_wait(("dd", p, ("far", 0 in lines)), whole(p, (0, 2, 4)))
        layer1(p, tuple((line, 2) for line in lines))

    for p in range(3):
        links.recv_wait(("a1", p), whole(p, (0, 0, 3)))
        start2(p, REST)
    for p in range(3):
        start3(p, 0, 0, REST)
        start3(p, 0, 1, REST)
        share("own", p, 0, 0)
    for p in range(3):
        forward2(p)
    for p in range(3):
        wait2(p, 1)
        start3(p, 1, 0)
        start3(p, -1, 0)
        share("own", p, 0, 1)
        share("own", p, 0, -1)
    for p in range(3):
        forward3(p, 0)
        start3(p, 1, 1)
    beside(0)
    for p in range(3):
        wait2(p, 2)
        share("own", p, 0, 2)
        start3(p, 2, 0)
        start3(p, -1, 1)
    for load in loads:
        load.wait()
    for p in range(3):
        forward3(p, 1)
        first_own(p)
    for p in range(3):
        forward3(p, -1)
        start3(p, 2, 1)
    far(0)
    first_near(0, 0)
    first_near(1, 0)
    beside(1)
    first_near(2, 0)
    for p in range(3):
        forward3(p, 2)
    beside(-1)
    for p in range(3):
        first_near(p, 1)
    far(1)
    first_near(0, -1)
    first_near(1, -1)
    far(-1)
    first_near(2, -1)
    first_far(0, (0, 1))
    beside(2)
    first_far(1, (0, 1))
    first_far(2, (0, 1))
    first_near(0, 2)
    far(2)
    links.start("page", "page", page.at[0], window.at[0], ahead)
    links.start("page", "page", page.at[0], window.at[4], behind)
    links.start("page", "near", page.at[0], window.at[1 + 2 * core], sibling)
    first_near(1, 2)
    first_near(2, 2)
    for p in range(3):
        first_far(p, (-1, 2))

    @pl.loop(0, 4)
    def _(i):
        @pl.loop(0, 4)
        def _(j):
            tile = pl.ds(half_cols, TILE)
            weight = xs[0, i, j, :, :, tile].astype(jnp.float32) + xs[1, i, j, :, :, tile].astype(
                jnp.float32
            )
            lane = lax.broadcasted_iota(jnp.int32, weight.shape, 2)
            weight = jnp.sum(jnp.where(lane == ep, weight, 0.0), axis=2, keepdims=True)
            gate = accg[i, j]
            hidden = gate * (1.0 / (1.0 + jnp.exp(-gate))) * accu[i, j] * weight
            hid[i, j] = hidden.astype(jnp.bfloat16)

    for p in range(3):
        links.send_wait(("a1", p), whole(p, (0, 0, 3)))
        links.send_wait(("a2", p), whole(p, (0, 3, 4)))
        links.send_wait(("a3", p), whole(p, (3, 4, 4)))
        links.send_wait(("dd", p), whole(p, (4, 4, 4)))

    def layer2(p, spots, half, extra=None):
        ats = places(p, spots)
        cols = pl.ds(starts[p] * TILE, data_parts[p] * TILE)
        rows = stacked([hid[at] for at in ats])
        got = jnp.dot(rows, wd[half, :, cols], preferred_element_type=jnp.float32)
        for at, part in apart(got, ats):
            if extra is not None:
                part = part + extra[at + (slice(None), cols)].astype(jnp.float32)
            xs[(half,) + at + (slice(None), cols)] = part.astype(jnp.bfloat16)

    def add_in(p, moves, piece, sources):
        at = chips(p, moves)
        free = [a for a in range(3) if isinstance(at[a], slice)]
        cols = columns(p, piece)
        width = piece[1] * TILE

        def one(i):
            unit = tuple(i if a in free else at[a] for a in range(3))
            index = (core,) + unit + (slice(None), cols)
            total = xs[index].astype(jnp.float32)
            for ref, lead, first in sources:
                lead = tuple(i if isinstance(l, slice) else l for l in lead)
                total = total + ref[lead + (slice(None), pl.ds(first, width))].astype(jnp.float32)
            xs[index] = total.astype(jnp.bfloat16)

        if free:
            pl.loop(at[free[0]].start, at[free[0]].stop)(one)
        else:
            one(0)

    def block(p, lead):
        lead = tuple(pl.ds(0, n) if n else 0 for n in lead)
        return dd.at[lead + (slice(None), columns(p, (0, data_parts[p])))]

    def make(p, name, spots):
        layer2(p, spots, other)
        for at in places(p, spots):
            at = at + (slice(None), columns(p, (0, data_parts[p])))
            links.start(("rd", p), ("rd", p, name), xs.at[(other,) + at], dd.at[at], sibling)

    def near_place(p, line, unit=None):
        at = chips(p, (unit, line, 0))
        return tuple(at[a] for a in range(3) if a != ORDERS[p][2])

    def scatter(key, m, p, moves, piece, dst, axis, by):
        links.start((key, p), (key, p) + m, rows_at(p, moves, piece), dst, device(axis, by))

    def far1(p, line):
        for d, by in DIRS:
            piece = cut(data_parts[p])[d]
            dst = r1a.at[
                (d,) + near_place(p, line) + (slice(None), pl.ds(starts[p] // 2 * TILE, piece[1] * TILE))
            ]
            scatter("r1", (line, 0), p, (None, line, 2), piece, dst, ORDERS[p][2], by)

    def near1(p, line, m, unit=None):
        last = "last" if unit == 0 else 1
        for d, by in DIRS:
            piece = cut(data_parts[p])[d if m == 2 else 1 - d]
            dst = r2a.at[(d,) + near_place(p, line, unit) + (slice(None), columns(p, piece))]
            scatter("r1", (line, last), p, (unit, line, by), piece, dst, ORDERS[p][2], by)

    def pass1(p, line, unit=None):
        if unit != 0:
            links.recv_wait(("r1", p, line, 0), block(p, (0, 0, 4)))
        for d, by in DIRS:
            piece = cut(data_parts[p])[d]
            place = (d,) + near_place(p, line, unit)
            add_in(p, (unit, line, by), piece, ((r1a, place, starts[p] // 2 * TILE),))
        near1(p, line, 2, unit)

    def lead_of(unit):
        return (0, 0, 2) if unit == 0 else (0, 2, 3) if unit == REST else (0, 2, 4)

    def end1(p, line, unit=None):
        links.recv_wait(("r1", p, line, "last" if unit == 0 else 1), block(p, lead_of(unit)))
        place = near_place(p, line, unit)
        first = starts[p] * TILE
        add_in(
            p,
            (unit, line, 0),
            (0, data_parts[p]),
            ((r2a, (0,) + place, first), (r2a, (1,) + place, first)),
        )

    def far2(p):
        for d, by in DIRS:
            piece = cut(data_parts[p])[d]
            dst = r1b.at[d, :, :, pl.ds(starts[p] // 2 * TILE, piece[1] * TILE)]
            scatter("r2", (0,), p, (None, 2, 0), piece, dst, ORDERS[p][1], by)

    def near2(p, d, m, unit):
        by = (1, -1)[d]
        piece = cut(data_parts[p])[d if m == 2 else 1 - d]
        dst = r2b.at[d, unit, :, columns(p, piece)]
        scatter("r2", ("last" if unit == 0 else 1,), p, (unit, by, 0), piece, dst, ORDERS[p][1], by)

    def pass2(p):
        links.recv_wait(("r2", p, 0), block(p, (0, 0, 4)))
        for d, by in DIRS:
            piece = cut(data_parts[p])[d]
            add_in(p, (None, by, 0), piece, ((r1b, (d, slice(None)), starts[p] // 2 * TILE),))
            near2(p, d, 2, REST)

    def end2(p, unit):
        links.recv_wait(("r2", p, "last" if unit == 0 else 1), block(p, lead_of(unit)))
        first = starts[p] * TILE
        add_in(
            p,
            (unit, 0, 0),
            (0, data_parts[p]),
            ((r2b, (0, unit), first), (r2b, (1, unit), first)),
        )

    def units(p):
        piece = (0, data_parts[p])
        for i, by in ((2, 2), (0, 1), (1, -1)):
            dst = rc.at[i, :, columns(p, piece)]
            scatter("r3", (), p, (by, 0, 0), piece, dst, ORDERS[p][0], by)

    def end3(p):
        links.recv_wait(("r3", p), block(p, (0, 0, 3)))
        first = starts[p] * TILE
        add_in(p, (0, 0, 0), (0, data_parts[p]), tuple((rc, (i,), first) for i in range(3)))

    BACK = (2, 1, -1, 0)

    def settle(p, name, spots):
        links.recv_wait(("rd", p, name), block(p, (0, 4 if name == "own" else len(spots), 4)))
        layer2(p, spots, core, dd)

    def onward(line):
        for p in range(3):
            end1(p, line)
            if line == 2:
                far2(p)
            else:
                near2(p, 0 if line == 1 else 1, 1, REST)

    begin, first_page, span = 0, 0, 0
    for i in range(tree_sizes.shape[1]):
        size = tree_sizes[0, i]
        inside = (begin <= ep) & (ep < begin + size)
        first_page = jnp.where(inside, begin, first_page)
        span = jnp.where(inside, size, span)
        begin = begin + size
    first_slot = jnp.clip(first_page - ep + 2, 0, 2)

    def dot_t(a, b):
        return lax.dot_general(a, b, (((1,), (1,)), ((), ())), preferred_element_type=jnp.float32)

    def attend(i):
        leaves = (2 * i, 2 * i + 1)
        rows = q_all[pl.ds(2 * i, 2)].reshape(2 * q_all.shape[1], q_all.shape[2])
        scores = []
        for k in range(3):
            got = jnp.dot(rows, window[first_slot + k], preferred_element_type=jnp.float32) * score_scale
            scores.append(jnp.where(k < span, got, -1e30))
        near = [
            jnp.dot(q_all[leaf], near_all[leaf], preferred_element_type=jnp.float32) * score_scale
            for leaf in leaves
        ]
        scores.append(jnp.concatenate(near, axis=0))
        top = scores[3].max(axis=1, keepdims=True)
        for k in range(3):
            top = jnp.maximum(top, scores[k].max(axis=1, keepdims=True))
        weights = [jnp.exp(got - top) for got in scores]
        total = weights[3].sum(axis=1, keepdims=True)
        for k in range(3):
            total = total + weights[k].sum(axis=1, keepdims=True)
        probs = [got.astype(jnp.bfloat16) for got in weights]
        heads = q_all.shape[1]
        mixed = jnp.concatenate(
            [
                dot_t(probs[3][n * heads : (n + 1) * heads], near_all[leaf, pl.ds(0, LATENT)])
                for n, leaf in enumerate(leaves)
            ],
            axis=0,
        )
        for k in range(3):
            mixed = mixed + dot_t(probs[k], window[first_slot + k, pl.ds(0, LATENT)])
        mixed_all[pl.ds(2 * i, 2)] = (mixed / total).astype(jnp.bfloat16).reshape(2, heads, LATENT)
        pltpu.make_async_copy(mixed_all.at[pl.ds(2 * i, 2)], context.at[pl.ds(2 * i, 2)], asem.at[3 + i]).start()

    FAR, NEAR = ((2, 2),), ((2, 1), (2, -1))
    for p in range(3):
        make(p, "far", FAR)
    for p in range(3):
        make(p, "near", NEAR)
        settle(p, "far", FAR)
        far1(p, 2)
    tasks = [(p, line, ((line, 2), (line, 1), (line, -1))) for line in BACK[1:] for p in range(3)]
    tasks += [(p, "own", OWN) for p in range(3)]
    make(*tasks[0])
    settle(0, "near", NEAR)
    near1(0, 2, 1)
    make(*tasks[1])
    for p in (1, 2):
        settle(p, "near", NEAR)
        near1(p, 2, 1)
    for n, (p, line, spots) in enumerate(tasks):
        if n + 2 < len(tasks):
            make(*tasks[n + 2])
        settle(p, line, spots)
        if line != "own":
            far1(p, line)
            near1(p, line, 1, REST if line == 0 else None)
        if n == 2:
            for q in range(3):
                pass1(q, 2)
            links.recv_wait("page", window.at[pl.ds(0, 2)])
            links.start("page", "near", window.at[4 * other], window.at[3 - 2 * core], sibling)
        if n == 5:
            for q in range(3):
                pass1(q, 1)
            for load in att_loads:
                load.wait()
            links.recv_wait("near", window.at[pl.ds(0, 2)])
            attend(0)
    for p in range(3):
        pass1(p, -1)
    onward(2)
    attend(1)
    onward(1)
    for p in range(3):
        pass1(p, 0, REST)
    onward(-1)
    attend(2)
    for p in range(3):
        pass2(p)
    for p in range(3):
        near1(p, 0, 1, 0)
        pass1(p, 0, 0)
    for p in range(3):
        for d in range(2):
            near2(p, d, 1, 0)
            near2(p, d, 2, 0)
    attend(3)
    for p in range(3):
        end1(p, 0, REST)
    for p in range(3):
        end2(p, REST)
        units(p)
    for p in range(3):
        end1(p, 0, 0)
        end2(p, 0)
    for p in range(3):
        end3(p)

    total = xs[core, 0, 0, 0, :, pl.ds(0, half_cols)].astype(jnp.float32)
    low, high = total[:8], total[8:]
    backsrc[...] = jnp.where(core == 0, high, low)
    links.start("back", "back", backsrc, exback, sibling)
    mine = jnp.where(core == 0, low, high)
    for p in range(3):
        links.send_wait(("rd", p), block(p, (4, 4, 4)))
        links.send_wait(("r1", p), block(p, (3, 4, 4)))
        links.send_wait(("r2", p), block(p, (0, 3, 4)))
        links.send_wait(("r3", p), block(p, (0, 0, 3)))
    links.send_wait("page", window.at[pl.ds(0, 4)])
    links.send_wait("ex", exsrc)
    for i in range(4):
        pltpu.make_async_copy(mixed_all.at[pl.ds(2 * i, 2)], context.at[pl.ds(2 * i, 2)], asem.at[3 + i]).wait()
    links.recv_wait("back", exback)
    theirs = exback[...]
    out[:, pl.ds(0, half_cols)] = jnp.where(core == 0, mine, theirs).astype(jnp.bfloat16)
    out[:, pl.ds(half_cols, half_cols)] = jnp.where(core == 0, theirs, mine).astype(jnp.bfloat16)
    links.send_wait("back", backsrc)


def hand_over(context, mix, context_out, mix_out, context_held, mix_held, sems):
    into = [
        pltpu.make_async_copy(context, context_held, sems.at[0]),
        pltpu.make_async_copy(mix, mix_held, sems.at[1]),
    ]
    onward = [
        pltpu.make_async_copy(context_held, context_out, sems.at[2]),
        pltpu.make_async_copy(mix_held, mix_out, sems.at[3]),
    ]
    for copy in into:
        copy.start()
    for first, second in zip(into, onward):
        first.wait()
        second.start()
    for copy in onward:
        copy.wait()


def local(
    hidden_rows,
    expert_ids,
    gate_weights,
    w_gate,
    w_up,
    w_down,
    queries,
    suffix_cache,
    prefix_pages,
    tree_sizes,
):
    leaves, width = hidden_rows.shape
    half = width // 2
    ffq = w_gate.shape[2]
    pairs = half // TILE // 2
    data_parts = [2 * ((pairs + 2 - p) // 3) for p in range(3)]
    grid = (4, 4, 4)
    bf16, f32 = jnp.bfloat16, jnp.float32
    first_cut = sum(cut(n)[0][1] for n in data_parts) * TILE
    heads, channels = queries.shape[1:]
    suffix_cache, prefix_pages = jnp.swapaxes(suffix_cache, 1, 2), jnp.swapaxes(prefix_pages, 1, 2)
    shapes = [
        ((2,) + grid + (ROWS, half + TILE), bf16),
        ((2, half, ffq), bf16),
        ((2, half, ffq), bf16),
        ((2, ffq, half), bf16),
        (grid + (ROWS, ffq), f32),
        (grid + (ROWS, ffq), f32),
        (grid + (ROWS, ffq), bf16),
        (grid + (ROWS, half), bf16),
        ((2, 4, 4, ROWS, first_cut), bf16),
        ((2, 4, 4, ROWS, half), bf16),
        ((2, 4, ROWS, first_cut), bf16),
        ((2, 4, ROWS, half), bf16),
        ((3, ROWS, half), bf16),
        ((leaves, half + TILE), f32),
        ((leaves, half + TILE), f32),
        ((leaves, half), f32),
        ((leaves, half), f32),
        ((5,) + prefix_pages.shape[1:], bf16),
        (queries.shape, bf16),
        (suffix_cache.shape, bf16),
        ((leaves, heads, LATENT), bf16),
    ]
    scratch = [pltpu.VMEM(shape, kind) for shape, kind in shapes]
    scratch += [pltpu.SemaphoreType.DMA((n,)) for n in (6, 7, 27, 130)]
    vmem, hbm = pl.BlockSpec(memory_space=pltpu.VMEM), pl.BlockSpec(memory_space=pl.ANY)
    smem = pl.BlockSpec(memory_space=pltpu.SMEM)
    results = pl.pallas_call(
        functools.partial(kernel, data_parts),
        out_shape=(
            jax.ShapeDtypeStruct((leaves, heads, LATENT), bf16),
            jax.ShapeDtypeStruct((leaves, width), bf16),
        ),
        in_specs=[vmem] * 3 + [smem] + [hbm] * 6,
        out_specs=(hbm, vmem),
        scratch_shapes=scratch,
        compiler_params=pltpu.CompilerParams(
            collective_id=0, has_side_effects=True, vmem_limit_bytes=63 * 1024 * 1024
        ),
        name="experts",
    )(
        hidden_rows,
        expert_ids,
        gate_weights,
        tree_sizes,
        w_gate,
        w_up,
        w_down,
        queries,
        suffix_cache,
        prefix_pages,
    )
    return pl.pallas_call(
        hand_over,
        out_shape=tuple(jax.ShapeDtypeStruct(r.shape, r.dtype) for r in results),
        in_specs=[hbm] * 2,
        out_specs=(hbm, hbm),
        scratch_shapes=[pltpu.VMEM(r.shape, r.dtype) for r in results] + [pltpu.SemaphoreType.DMA((4,))],
        compiler_params=pltpu.CompilerParams(vmem_limit_bytes=63 * 1024 * 1024),
        name="results",
    )(*results)


def solution(mesh):
    return jax.shard_map(
        local,
        mesh=mesh,
        in_specs=(
            P(("dp", "ep"), None),
            P(("dp", "ep"), None),
            P(("dp", "ep"), None),
            P("ep", None, "dp"),
            P("ep", None, "dp"),
            P("ep", "dp", None),
            P(("dp", "ep"), None, None),
            P(("dp", "ep"), None, None),
            P(("dp", "ep"), None, None),
            P("dp", None),
        ),
        out_specs=(P(("dp", "ep"), None, None), P(("dp", "ep"), None)),
        check_vma=False,
    )
```

```python
import functools

import jax
import jax.numpy as jnp
from jax import lax
from jax.experimental import pallas as pl
from jax.experimental.pallas import tpu as pltpu
from jax.sharding import PartitionSpec as P

LATENT = 512
TILE = 128
CHUNK = 256
ROWS = 16
score_scale = 192.0 ** (-0.5)
MESH = pl.DeviceIdType.MESH
LINES = (0, 1, -1, 2)
ORDERS = ((1, 2, 0), (2, 0, 1), (0, 1, 2))


class Links:
    def __init__(self, send, recv):
        self.send, self.recv = send, recv
        self.sent, self.got = {}, {}

    def start(self, sent, got, src, dst, device):
        pltpu.make_async_remote_copy(
            src_ref=src,
            dst_ref=dst,
            send_sem=self.send.at[self.sent.setdefault(sent, len(self.sent))],
            recv_sem=self.recv.at[self.got.setdefault(got, len(self.got))],
            device_id=device,
            device_id_type=MESH,
        ).start()

    def recv_wait(self, got, ref):
        pltpu.make_async_copy(ref, ref, self.recv.at[self.got[got]]).wait()

    def send_wait(self, sent, ref):
        pltpu.make_async_copy(ref, ref, self.send.at[self.sent[sent]]).wait()


def cut(part_tiles):
    first = (part_tiles + 1) // 2
    return ((0, first), (first, part_tiles - first))


def kernel(
    data_parts,
    hidden_hbm,
    ids_hbm,
    gates_hbm,
    tree_hbm,
    wg_hbm,
    wu_hbm,
    wd_hbm,
    queries,
    suffix,
    page,
    context,
    out,
    xs,
    wg,
    wu,
    wd,
    accg,
    accu,
    hid,
    dd,
    r1a,
    r2a,
    r1b,
    r2b,
    rc,
    exsrc,
    exin,
    backsrc,
    exback,
    window,
    q_all,
    near_all,
    hidden_rows,
    expert_ids,
    gate_weights,
    tree_sizes,
    wsem,
    asem,
    send_sem,
    recv_sem,
):
    ffq = wg.shape[2]
    half_cols = wg.shape[1]
    y = lax.axis_index("dp")
    ep = lax.axis_index("ep")
    core = lax.rem(ep, 2)
    x = ep // 8
    z = lax.rem(ep // 2, 4)
    here = (x, y, z)
    other = 1 - core

    def shift(axis, by):
        return lax.rem(here[axis] + (by + 4) % 4, 4)

    def device(axis, by):
        place = [x, y, z]
        place[axis] = shift(axis, by)
        return (place[1], place[0] * 8 + place[2] * 2 + core)

    sibling = (y, x * 8 + z * 2 + other)
    ahead = (y, lax.rem(ep + 2, 32))
    behind = (y, lax.rem(ep + 30, 32))

    barrier = pltpu.get_barrier_semaphore()
    greeted = [device(axis, by) for axis in range(3) for by in (1, -1, 2)] + [sibling, ahead, behind]
    for other_device in greeted:
        pl.semaphore_signal(barrier, inc=1, device_id=other_device, device_id_type=MESH)

    first_loads = [
        pltpu.make_async_copy(src, dst, asem.at[3 + i])
        for i, (src, dst) in enumerate(
            (
                (hidden_hbm, hidden_rows),
                (ids_hbm, expert_ids),
                (gates_hbm, gate_weights),
                (tree_hbm, tree_sizes),
            )
        )
    ]
    for load in first_loads:
        load.start()
    loads = []
    for half in range(2):
        rows = pl.ds(half * half_cols, half_cols)
        loads.append(pltpu.make_async_copy(wg_hbm.at[0, rows], wg.at[half], wsem.at[half]))
        loads.append(pltpu.make_async_copy(wu_hbm.at[0, rows], wu.at[half], wsem.at[2 + half]))
    for half in range(2):
        cols = pl.ds(half * half_cols, half_cols)
        loads.append(pltpu.make_async_copy(wd_hbm.at[0, :, cols], wd.at[half], wsem.at[4 + half]))
    att_loads = [
        pltpu.make_async_copy(queries, q_all, asem.at[0]),
        pltpu.make_async_copy(suffix, near_all, asem.at[1]),
        pltpu.make_async_copy(page.at[0], window.at[2], asem.at[2]),
    ]

    for load in first_loads:
        load.wait()
    rows_low = hidden_rows[:, pl.ds(0, half_cols)].astype(jnp.float32)
    rows_high = hidden_rows[:, pl.ds(half_cols, half_cols)].astype(jnp.float32)
    lane = lax.broadcasted_iota(jnp.int32, (8, TILE), 1)
    weight = jnp.zeros((8, TILE), jnp.float32)
    for k in range(expert_ids.shape[1]):
        chosen = lane == expert_ids[:, pl.ds(k, 1)]
        weight = weight + jnp.where(chosen, gate_weights[:, pl.ds(k, 1)], 0.0)
    coarse = weight.astype(jnp.bfloat16).astype(jnp.float32)
    fine = weight - coarse
    exsrc[:, pl.ds(0, half_cols)] = jnp.where(core == 0, rows_high, rows_low)
    exsrc[:, pl.ds(half_cols, TILE)] = jnp.where(core == 0, fine, coarse)

    pl.semaphore_wait(barrier, len(greeted))
    links = Links(send_sem, recv_sem)
    links.start("ex", "ex", exsrc, exin, sibling)
    for load in loads + att_loads:
        load.start()

    starts = []
    spans = []
    for p in range(3):
        starts.append(sum(data_parts[:p]))
        spans.append(data_parts[p] + (1 if p == 2 else 0))

    links.recv_wait("ex", exin)
    theirs = exin[:, pl.ds(0, half_cols)]
    mine = jnp.where(core == 0, rows_low, rows_high)
    low = jnp.where(core == 0, mine, theirs)
    high = jnp.where(core == 0, theirs, mine)
    xs[core, 0, 0, 0, :, pl.ds(0, half_cols)] = jnp.concatenate([low, high], axis=0).astype(jnp.bfloat16)
    theirs = exin[:, pl.ds(half_cols, TILE)]
    mine = jnp.where(core == 0, coarse, fine)
    low = jnp.where(core == 0, mine, theirs)
    high = jnp.where(core == 0, theirs, mine)
    xs[core, 0, 0, 0, :, pl.ds(half_cols, TILE)] = jnp.concatenate([low, high], axis=0).astype(
        jnp.bfloat16
    )

    REST = slice(1, 4)

    def chips(p, moves):
        index = [None, None, None]
        for axis, by in zip(ORDERS[p], moves):
            index[axis] = slice(0, 4) if by is None else by if isinstance(by, slice) else by % 4
        return tuple(index)

    def columns(p, piece):
        return pl.ds((starts[p] + piece[0]) * TILE, piece[1] * TILE)

    def rows_at(p, moves, piece):
        return xs.at[(core,) + chips(p, moves) + (slice(None), columns(p, piece))]

    def whole(p, lead):
        lead = tuple(pl.ds(0, n) if n else 0 for n in lead)
        return xs.at[(0,) + lead + (slice(None), columns(p, (0, spans[p])))]

    def gather(key, m, p, moves, piece, axis, by):
        there = [move - by if a == axis else move for a, move in zip(ORDERS[p], moves)]
        links.start(
            (key, p), (key, p) + m, rows_at(p, moves, piece), rows_at(p, there, piece), device(axis, by)
        )

    def share(name, p, by, line):
        ref = rows_at(p, (None, line, by), (0, spans[p]))
        links.start(("dd", p), ("dd", p, name), ref, ref, sibling)

    DIRS = ((0, 1), (1, -1))

    def start2(p, unit):
        pieces = cut(spans[p])
        for m in range(2):
            for d, by in DIRS:
                gather("a2", (m,), p, (unit, 0, 0), pieces[d ^ m], ORDERS[p][1], by)

    def wait2(p, m):
        links.recv_wait(("a2", p, m), whole(p, (0, 0, 4)))

    def forward2(p):
        wait2(p, 0)
        for d, by in DIRS:
            gather("a2", (2,), p, (None, -by, 0), cut(spans[p])[d], ORDERS[p][1], by)

    def start3(p, line, m, unit=None):
        pieces = cut(spans[p])
        for d, by in DIRS:
            gather("a3", (line, m), p, (unit, line, 0), pieces[d ^ m], ORDERS[p][2], by)

    def wait3(p, line, m):
        links.recv_wait(("a3", p, line, m), whole(p, (0, 0, 4)))

    def forward3(p, line):
        wait3(p, line, 0)
        for d, by in DIRS:
            gather("a3", (line, 2), p, (None, line, -by), cut(spans[p])[d], ORDERS[p][2], by)

    OWN = ((None, 0),)

    def places(p, spots):
        return [chips(p, (None, line, by)) for line, by in spots]

    def stacked(parts):
        parts = [part.reshape(-1, part.shape[-1]) for part in parts]
        return parts[0] if len(parts) == 1 else jnp.concatenate(parts, axis=0)

    def apart(value, ats):
        first = 0
        for at in ats:
            lead = (4,) * sum(isinstance(i, slice) for i in at)
            count = 4 ** len(lead) * ROWS
            yield at, value[first : first + count].reshape(lead + (ROWS, value.shape[-1]))
            first += count

    def layer1(p, spots):
        ats = places(p, spots)
        cols = pl.ds(starts[p] * TILE, data_parts[p] * TILE)
        x0, x1 = [stacked([xs[(half,) + at + (slice(None), cols)] for at in ats]) for half in range(2)]
        for acc, w in ((accg, wg), (accu, wu)):
            got = jnp.dot(x0, w[0, cols, :], preferred_element_type=jnp.float32)
            got = got + jnp.dot(x1, w[1, cols, :], preferred_element_type=jnp.float32)
            for at, rows in apart(got, ats):
                acc[at] += rows

    for p in range(3):
        for by in (1, -1, 2):
            gather("a1", (), p, (0, 0, 0), (0, spans[p]), ORDERS[p][0], by)
    for p in range(3):
        start2(p, 0)
    for p in range(3):
        start3(p, 0, 0, 0)
        start3(p, 0, 1, 0)

    @pl.loop(0, 4)
    def _(i):
        accg[i] = jnp.zeros_like(accg[i])
        accu[i] = jnp.zeros_like(accu[i])

    def beside(line):
        for p in range(3):
            wait3(p, line, 1)
            share(("near", line), p, 1, line)
            share(("near", line), p, -1, line)

    def far(line):
        for p in range(3):
            wait3(p, line, 2)
            share(("far", line in (0, 1)), p, 2, line)

    def first_own(p):
        links.recv_wait(("dd", p, "own"), whole(p, (0, 4, 4)))
        layer1(p, OWN)

    def first_near(p, line):
        links.recv_wait(("dd", p, ("near", line)), whole(p, (0, 2, 4)))
        layer1(p, ((line, 1), (line, -1)))

    def first_far(p, lines):
        links.recv_wait(("dd", p, ("far", 0 in lines)), whole(p, (0, 2, 4)))
        layer1(p, tuple((line, 2) for line in lines))

    for p in range(3):
        links.recv_wait(("a1", p), whole(p, (0, 0, 3)))
        start2(p, REST)
    for p in range(3):
        start3(p, 0, 0, REST)
        start3(p, 0, 1, REST)
        share("own", p, 0, 0)
    for p in range(3):
        forward2(p)
    for p in range(3):
        wait2(p, 1)
        start3(p, 1, 0)
        start3(p, -1, 0)
        share("own", p, 0, 1)
        share("own", p, 0, -1)
    for p in range(3):
        forward3(p, 0)
        start3(p, 1, 1)
    beside(0)
    for p in range(3):
        wait2(p, 2)
        share("own", p, 0, 2)
        start3(p, 2, 0)
        start3(p, -1, 1)
    for load in loads:
        load.wait()
    for p in range(3):
        forward3(p, 1)
        first_own(p)
    for p in range(3):
        forward3(p, -1)
        start3(p, 2, 1)
    far(0)
    first_near(0, 0)
    first_near(1, 0)
    beside(1)
    first_near(2, 0)
    for p in range(3):
        forward3(p, 2)
    beside(-1)
    for p in range(3):
        first_near(p, 1)
    far(1)
    first_near(0, -1)
    first_near(1, -1)
    far(-1)
    first_near(2, -1)
    first_far(0, (0, 1))
    beside(2)
    first_far(1, (0, 1))
    first_far(2, (0, 1))
    first_near(0, 2)
    far(2)
    links.start("page", "page", page.at[0], window.at[0], ahead)
    links.start("page", "page", page.at[0], window.at[4], behind)
    links.start("page", "near", page.at[0], window.at[1 + 2 * core], sibling)
    first_near(1, 2)
    first_near(2, 2)
    for p in range(3):
        first_far(p, (-1, 2))

    @pl.loop(0, 4)
    def _(i):
        @pl.loop(0, 4)
        def _(j):
            tile = pl.ds(half_cols, TILE)
            weight = xs[0, i, j, :, :, tile].astype(jnp.float32) + xs[1, i, j, :, :, tile].astype(
                jnp.float32
            )
            lane = lax.broadcasted_iota(jnp.int32, weight.shape, 2)
            weight = jnp.sum(jnp.where(lane == ep, weight, 0.0), axis=2, keepdims=True)
            gate = accg[i, j]
            hidden = gate * (1.0 / (1.0 + jnp.exp(-gate))) * accu[i, j] * weight
            hid[i, j] = hidden.astype(jnp.bfloat16)

    for p in range(3):
        links.send_wait(("a1", p), whole(p, (0, 0, 3)))
        links.send_wait(("a2", p), whole(p, (0, 3, 4)))
        links.send_wait(("a3", p), whole(p, (3, 4, 4)))
        links.send_wait(("dd", p), whole(p, (4, 4, 4)))

    def layer2(p, spots, half, extra=None):
        ats = places(p, spots)
        cols = pl.ds(starts[p] * TILE, data_parts[p] * TILE)
        rows = stacked([hid[at] for at in ats])
        got = jnp.dot(rows, wd[half, :, cols], preferred_element_type=jnp.float32)
        for at, part in apart(got, ats):
            if extra is not None:
                part = part + extra[at + (slice(None), cols)].astype(jnp.float32)
            xs[(half,) + at + (slice(None), cols)] = part.astype(jnp.bfloat16)

    def add_in(p, moves, piece, sources):
        at = chips(p, moves)
        free = [a for a in range(3) if isinstance(at[a], slice)]
        cols = columns(p, piece)
        width = piece[1] * TILE

        def one(i):
            unit = tuple(i if a in free else at[a] for a in range(3))
            index = (core,) + unit + (slice(None), cols)
            total = xs[index].astype(jnp.float32)
            for ref, lead, first in sources:
                lead = tuple(i if isinstance(l, slice) else l for l in lead)
                total = total + ref[lead + (slice(None), pl.ds(first, width))].astype(jnp.float32)
            xs[index] = total.astype(jnp.bfloat16)

        if free:
            pl.loop(at[free[0]].start, at[free[0]].stop)(one)
        else:
            one(0)

    def block(p, lead):
        lead = tuple(pl.ds(0, n) if n else 0 for n in lead)
        return dd.at[lead + (slice(None), columns(p, (0, data_parts[p])))]

    def make(p, name, spots):
        layer2(p, spots, other)
        for at in places(p, spots):
            at = at + (slice(None), columns(p, (0, data_parts[p])))
            links.start(("rd", p), ("rd", p, name), xs.at[(other,) + at], dd.at[at], sibling)

    def near_place(p, line, unit=None):
        at = chips(p, (unit, line, 0))
        return tuple(at[a] for a in range(3) if a != ORDERS[p][2])

    def scatter(key, m, p, moves, piece, dst, axis, by):
        links.start((key, p), (key, p) + m, rows_at(p, moves, piece), dst, device(axis, by))

    def far1(p, line):
        for d, by in DIRS:
            piece = cut(data_parts[p])[d]
            dst = r1a.at[
                (d,) + near_place(p, line) + (slice(None), pl.ds(starts[p] // 2 * TILE, piece[1] * TILE))
            ]
            scatter("r1", (line, 0), p, (None, line, 2), piece, dst, ORDERS[p][2], by)

    def near1(p, line, m, unit=None):
        last = "last" if unit == 0 else 1
        for d, by in DIRS:
            piece = cut(data_parts[p])[d if m == 2 else 1 - d]
            dst = r2a.at[(d,) + near_place(p, line, unit) + (slice(None), columns(p, piece))]
            scatter("r1", (line, last), p, (unit, line, by), piece, dst, ORDERS[p][2], by)

    def pass1(p, line, unit=None):
        if unit != 0:
            links.recv_wait(("r1", p, line, 0), block(p, (0, 0, 4)))
        for d, by in DIRS:
            piece = cut(data_parts[p])[d]
            place = (d,) + near_place(p, line, unit)
            add_in(p, (unit, line, by), piece, ((r1a, place, starts[p] // 2 * TILE),))
        near1(p, line, 2, unit)

    def lead_of(unit):
        return (0, 0, 2) if unit == 0 else (0, 2, 3) if unit == REST else (0, 2, 4)

    def end1(p, line, unit=None):
        links.recv_wait(("r1", p, line, "last" if unit == 0 else 1), block(p, lead_of(unit)))
        place = near_place(p, line, unit)
        first = starts[p] * TILE
        add_in(
            p,
            (unit, line, 0),
            (0, data_parts[p]),
            ((r2a, (0,) + place, first), (r2a, (1,) + place, first)),
        )

    def far2(p):
        for d, by in DIRS:
            piece = cut(data_parts[p])[d]
            dst = r1b.at[d, :, :, pl.ds(starts[p] // 2 * TILE, piece[1] * TILE)]
            scatter("r2", (0,), p, (None, 2, 0), piece, dst, ORDERS[p][1], by)

    def near2(p, d, m, unit):
        by = (1, -1)[d]
        piece = cut(data_parts[p])[d if m == 2 else 1 - d]
        dst = r2b.at[d, unit, :, columns(p, piece)]
        scatter("r2", ("last" if unit == 0 else 1,), p, (unit, by, 0), piece, dst, ORDERS[p][1], by)

    def pass2(p):
        links.recv_wait(("r2", p, 0), block(p, (0, 0, 4)))
        for d, by in DIRS:
            piece = cut(data_parts[p])[d]
            add_in(p, (None, by, 0), piece, ((r1b, (d, slice(None)), starts[p] // 2 * TILE),))
            near2(p, d, 2, REST)

    def end2(p, unit):
        links.recv_wait(("r2", p, "last" if unit == 0 else 1), block(p, lead_of(unit)))
        first = starts[p] * TILE
        add_in(
            p,
            (unit, 0, 0),
            (0, data_parts[p]),
            ((r2b, (0, unit), first), (r2b, (1, unit), first)),
        )

    def units(p):
        piece = (0, data_parts[p])
        for i, by in ((2, 2), (0, 1), (1, -1)):
            dst = rc.at[i, :, columns(p, piece)]
            scatter("r3", (), p, (by, 0, 0), piece, dst, ORDERS[p][0], by)

    def end3(p):
        links.recv_wait(("r3", p), block(p, (0, 0, 3)))
        first = starts[p] * TILE
        add_in(p, (0, 0, 0), (0, data_parts[p]), tuple((rc, (i,), first) for i in range(3)))

    BACK = (2, 1, -1, 0)

    def settle(p, name, spots):
        links.recv_wait(("rd", p, name), block(p, (0, 4 if name == "own" else len(spots), 4)))
        layer2(p, spots, core, dd)

    def onward(line):
        for p in range(3):
            end1(p, line)
            if line == 2:
                far2(p)
            else:
                near2(p, 0 if line == 1 else 1, 1, REST)

    begin, first_page, span = 0, 0, 0
    for i in range(tree_sizes.shape[1]):
        size = tree_sizes[0, i]
        inside = (begin <= ep) & (ep < begin + size)
        first_page = jnp.where(inside, begin, first_page)
        span = jnp.where(inside, size, span)
        begin = begin + size
    first_slot = jnp.clip(first_page - ep + 2, 0, 2)

    def dot_t(a, b):
        return lax.dot_general(a, b, (((1,), (1,)), ((), ())), preferred_element_type=jnp.float32)

    def attend(i):
        leaves = (2 * i, 2 * i + 1)
        rows = q_all[pl.ds(2 * i, 2)].reshape(2 * q_all.shape[1], q_all.shape[2])
        scores = []
        for k in range(3):
            got = jnp.dot(rows, window[first_slot + k], preferred_element_type=jnp.float32) * score_scale
            scores.append(jnp.where(k < span, got, -1e30))
        near = [
            jnp.dot(q_all[leaf], near_all[leaf], preferred_element_type=jnp.float32) * score_scale
            for leaf in leaves
        ]
        scores.append(jnp.concatenate(near, axis=0))
        top = scores[3].max(axis=1, keepdims=True)
        for k in range(3):
            top = jnp.maximum(top, scores[k].max(axis=1, keepdims=True))
        weights = [jnp.exp(got - top) for got in scores]
        total = weights[3].sum(axis=1, keepdims=True)
        for k in range(3):
            total = total + weights[k].sum(axis=1, keepdims=True)
        probs = [got.astype(jnp.bfloat16) for got in weights]
        heads = q_all.shape[1]
        mixed = jnp.concatenate(
            [
                dot_t(probs[3][n * heads : (n + 1) * heads], near_all[leaf, pl.ds(0, LATENT)])
                for n, leaf in enumerate(leaves)
            ],
            axis=0,
        )
        for k in range(3):
            mixed = mixed + dot_t(probs[k], window[first_slot + k, pl.ds(0, LATENT)])
        context[pl.ds(2 * i, 2)] = (mixed / total).astype(jnp.bfloat16).reshape(2, heads, LATENT)

    FAR, NEAR = ((2, 2),), ((2, 1), (2, -1))
    for p in range(3):
        make(p, "far", FAR)
    for p in range(3):
        make(p, "near", NEAR)
        settle(p, "far", FAR)
        far1(p, 2)
    tasks = [(p, line, ((line, 2), (line, 1), (line, -1))) for line in BACK[1:] for p in range(3)]
    tasks += [(p, "own", OWN) for p in range(3)]
    make(*tasks[0])
    settle(0, "near", NEAR)
    near1(0, 2, 1)
    make(*tasks[1])
    for p in (1, 2):
        settle(p, "near", NEAR)
        near1(p, 2, 1)
    for n, (p, line, spots) in enumerate(tasks):
        if n + 2 < len(tasks):
            make(*tasks[n + 2])
        settle(p, line, spots)
        if line != "own":
            far1(p, line)
            near1(p, line, 1, REST if line == 0 else None)
        if n == 2:
            for q in range(3):
                pass1(q, 2)
            links.recv_wait("page", window.at[pl.ds(0, 2)])
            links.start("page", "near", window.at[4 * other], window.at[3 - 2 * core], sibling)
        if n == 5:
            for q in range(3):
                pass1(q, 1)
            for load in att_loads:
                load.wait()
            links.recv_wait("near", window.at[pl.ds(0, 2)])
            attend(0)
    for p in range(3):
        pass1(p, -1)
    onward(2)
    attend(1)
    onward(1)
    for p in range(3):
        pass1(p, 0, REST)
    onward(-1)
    attend(2)
    for p in range(3):
        pass2(p)
    for p in range(3):
        near1(p, 0, 1, 0)
        pass1(p, 0, 0)
    for p in range(3):
        for d in range(2):
            near2(p, d, 1, 0)
            near2(p, d, 2, 0)
    attend(3)
    for p in range(3):
        end1(p, 0, REST)
    for p in range(3):
        end2(p, REST)
        units(p)
    for p in range(3):
        end1(p, 0, 0)
        end2(p, 0)
    mine = []
    for p in range(3):
        end3(p)
        cols = columns(p, (0, data_parts[p]))
        total = xs[core, 0, 0, 0, :, cols].astype(jnp.float32)
        low, high = total[:8], total[8:]
        backsrc[:, cols] = jnp.where(core == 0, high, low)
        links.start("back", "back", backsrc.at[:, cols], exback.at[:, cols], sibling)
        mine.append(jnp.where(core == 0, low, high))
    mine = jnp.concatenate(mine, axis=1)
    for p in range(3):
        links.send_wait(("rd", p), block(p, (4, 4, 4)))
        links.send_wait(("r1", p), block(p, (3, 4, 4)))
        links.send_wait(("r2", p), block(p, (0, 3, 4)))
        links.send_wait(("r3", p), block(p, (0, 0, 3)))
    links.send_wait("page", window.at[pl.ds(0, 4)])
    links.send_wait("ex", exsrc)
    links.recv_wait("back", exback)
    theirs = exback[...]
    out[:, pl.ds(0, half_cols)] = jnp.where(core == 0, mine, theirs).astype(jnp.bfloat16)
    out[:, pl.ds(half_cols, half_cols)] = jnp.where(core == 0, theirs, mine).astype(jnp.bfloat16)
    links.send_wait("back", backsrc)


def hand_over(context, mix, context_out, mix_out, sems):
    copies = [
        pltpu.make_async_copy(context, context_out, sems.at[0]),
        pltpu.make_async_copy(mix, mix_out, sems.at[1]),
    ]
    for copy in copies:
        copy.start()
    for copy in copies:
        copy.wait()


def local(
    hidden_rows,
    expert_ids,
    gate_weights,
    w_gate,
    w_up,
    w_down,
    queries,
    suffix_cache,
    prefix_pages,
    tree_sizes,
):
    leaves, width = hidden_rows.shape
    half = width // 2
    ffq = w_gate.shape[2]
    pairs = half // TILE // 2
    data_parts = [2 * ((pairs + 2 - p) // 3) for p in range(3)]
    grid = (4, 4, 4)
    bf16, f32 = jnp.bfloat16, jnp.float32
    first_cut = sum(cut(n)[0][1] for n in data_parts) * TILE
    heads, channels = queries.shape[1:]
    suffix_cache, prefix_pages = jnp.swapaxes(suffix_cache, 1, 2), jnp.swapaxes(prefix_pages, 1, 2)
    shapes = [
        ((2,) + grid + (ROWS, half + TILE), bf16),
        ((2, half, ffq), bf16),
        ((2, half, ffq), bf16),
        ((2, ffq, half), bf16),
        (grid + (ROWS, ffq), f32),
        (grid + (ROWS, ffq), f32),
        (grid + (ROWS, ffq), bf16),
        (grid + (ROWS, half), bf16),
        ((2, 4, 4, ROWS, first_cut), bf16),
        ((2, 4, 4, ROWS, half), bf16),
        ((2, 4, ROWS, first_cut), bf16),
        ((2, 4, ROWS, half), bf16),
        ((3, ROWS, half), bf16),
        ((leaves, half + TILE), f32),
        ((leaves, half + TILE), f32),
        ((leaves, half), f32),
        ((leaves, half), f32),
        ((5,) + prefix_pages.shape[1:], bf16),
        (queries.shape, bf16),
        (suffix_cache.shape, bf16),
        ((leaves, width), bf16),
        (expert_ids.shape, expert_ids.dtype),
        (gate_weights.shape, gate_weights.dtype),
    ]
    scratch = [pltpu.VMEM(shape, kind) for shape, kind in shapes]
    scratch.append(pltpu.SMEM(tree_sizes.shape, tree_sizes.dtype))
    scratch += [pltpu.SemaphoreType.DMA((n,)) for n in (6, 7, 27, 130)]
    vmem, hbm = pl.BlockSpec(memory_space=pltpu.VMEM), pl.BlockSpec(memory_space=pl.ANY)
    results = pl.pallas_call(
        functools.partial(kernel, data_parts),
        out_shape=(pltpu.VMEM((leaves, heads, LATENT), bf16), pltpu.VMEM((leaves, width), bf16)),
        in_specs=[hbm] * 10,
        out_specs=(vmem, vmem),
        scratch_shapes=scratch,
        compiler_params=pltpu.CompilerParams(
            collective_id=0, has_side_effects=True, vmem_limit_bytes=61 * 1024 * 1024
        ),
        name="experts",
    )(
        hidden_rows,
        expert_ids,
        gate_weights,
        tree_sizes,
        w_gate,
        w_up,
        w_down,
        queries,
        suffix_cache,
        prefix_pages,
    )
    return pl.pallas_call(
        hand_over,
        out_shape=tuple(jax.ShapeDtypeStruct(r.shape, r.dtype) for r in results),
        in_specs=[vmem] * 2,
        out_specs=(hbm, hbm),
        scratch_shapes=[pltpu.SemaphoreType.DMA((2,))],
        name="results",
    )(*results)


def solution(mesh):
    return jax.shard_map(
        local,
        mesh=mesh,
        in_specs=(
            P(("dp", "ep"), None),
            P(("dp", "ep"), None),
            P(("dp", "ep"), None),
            P("ep", None, "dp"),
            P("ep", None, "dp"),
            P("ep", "dp", None),
            P(("dp", "ep"), None, None),
            P(("dp", "ep"), None, None),
            P(("dp", "ep"), None, None),
            P("dp", None),
        ),
        out_specs=(P(("dp", "ep"), None, None), P(("dp", "ep"), None)),
        check_vma=False,
    )
```

```python
import functools

import jax
import jax.numpy as jnp
from jax import lax
from jax.experimental import pallas as pl
from jax.experimental.pallas import tpu as pltpu
from jax.sharding import PartitionSpec as P

LATENT = 512
TILE = 128
CHUNK = 256
ROWS = 16
score_scale = 192.0 ** (-0.5)
MESH = pl.DeviceIdType.MESH
LINES = (0, 1, -1, 2)
ORDERS = ((1, 2, 0), (2, 0, 1), (0, 1, 2))


class Links:
    def __init__(self, send, recv):
        self.send, self.recv = send, recv
        self.sent, self.got = {}, {}

    def start(self, sent, got, src, dst, device):
        pltpu.make_async_remote_copy(
            src_ref=src,
            dst_ref=dst,
            send_sem=self.send.at[self.sent.setdefault(sent, len(self.sent))],
            recv_sem=self.recv.at[self.got.setdefault(got, len(self.got))],
            device_id=device,
            device_id_type=MESH,
        ).start()

    def recv_wait(self, got, ref):
        pltpu.make_async_copy(ref, ref, self.recv.at[self.got[got]]).wait()

    def send_wait(self, sent, ref):
        pltpu.make_async_copy(ref, ref, self.send.at[self.sent[sent]]).wait()


def cut(part_tiles):
    first = (part_tiles + 1) // 2
    return ((0, first), (first, part_tiles - first))


def kernel(
    data_parts,
    hidden_hbm,
    ids_hbm,
    gates_hbm,
    tree_hbm,
    wg_hbm,
    wu_hbm,
    wd_hbm,
    queries,
    suffix,
    page,
    context,
    out,
    xs,
    wg,
    wu,
    wd,
    accg,
    accu,
    hid,
    dd,
    r1a,
    r2a,
    r1b,
    r2b,
    rc,
    exsrc,
    exin,
    backsrc,
    exback,
    window,
    q_all,
    near_all,
    hidden_rows,
    expert_ids,
    gate_weights,
    tree_sizes,
    wsem,
    asem,
    send_sem,
    recv_sem,
):
    ffq = wg.shape[2]
    half_cols = wg.shape[1]
    y = lax.axis_index("dp")
    ep = lax.axis_index("ep")
    core = lax.rem(ep, 2)
    x = ep // 8
    z = lax.rem(ep // 2, 4)
    here = (x, y, z)
    other = 1 - core

    def shift(axis, by):
        return lax.rem(here[axis] + (by + 4) % 4, 4)

    def device(axis, by):
        place = [x, y, z]
        place[axis] = shift(axis, by)
        return (place[1], place[0] * 8 + place[2] * 2 + core)

    sibling = (y, x * 8 + z * 2 + other)
    ahead = (y, lax.rem(ep + 2, 32))
    behind = (y, lax.rem(ep + 30, 32))

    barrier = pltpu.get_barrier_semaphore()
    greeted = [device(axis, by) for axis in range(3) for by in (1, -1, 2)] + [sibling, ahead, behind]
    for other_device in greeted:
        pl.semaphore_signal(barrier, inc=1, device_id=other_device, device_id_type=MESH)

    first_loads = [
        pltpu.make_async_copy(src, dst, asem.at[3 + i])
        for i, (src, dst) in enumerate(
            (
                (hidden_hbm, hidden_rows),
                (ids_hbm, expert_ids),
                (gates_hbm, gate_weights),
                (tree_hbm, tree_sizes),
            )
        )
    ]
    for load in first_loads:
        load.start()
    loads = []
    for half in range(2):
        rows = pl.ds(half * half_cols, half_cols)
        loads.append(pltpu.make_async_copy(wg_hbm.at[0, rows], wg.at[half], wsem.at[half]))
        loads.append(pltpu.make_async_copy(wu_hbm.at[0, rows], wu.at[half], wsem.at[2 + half]))
    for half in range(2):
        cols = pl.ds(half * half_cols, half_cols)
        loads.append(pltpu.make_async_copy(wd_hbm.at[0, :, cols], wd.at[half], wsem.at[4 + half]))
    att_loads = [
        pltpu.make_async_copy(queries, q_all, asem.at[0]),
        pltpu.make_async_copy(suffix, near_all, asem.at[1]),
        pltpu.make_async_copy(page.at[0], window.at[2], asem.at[2]),
    ]

    for load in first_loads:
        load.wait()
    rows_low = hidden_rows[:, pl.ds(0, half_cols)].astype(jnp.float32)
    rows_high = hidden_rows[:, pl.ds(half_cols, half_cols)].astype(jnp.float32)
    lane = lax.broadcasted_iota(jnp.int32, (8, TILE), 1)
    weight = jnp.zeros((8, TILE), jnp.float32)
    for k in range(expert_ids.shape[1]):
        chosen = lane == expert_ids[:, pl.ds(k, 1)]
        weight = weight + jnp.where(chosen, gate_weights[:, pl.ds(k, 1)], 0.0)
    coarse = weight.astype(jnp.bfloat16).astype(jnp.float32)
    fine = weight - coarse
    exsrc[:, pl.ds(0, half_cols)] = jnp.where(core == 0, rows_high, rows_low)
    exsrc[:, pl.ds(half_cols, TILE)] = jnp.where(core == 0, fine, coarse)

    pl.semaphore_wait(barrier, len(greeted))
    links = Links(send_sem, recv_sem)
    links.start("ex", "ex", exsrc, exin, sibling)
    for load in loads + att_loads:
        load.start()

    starts = []
    spans = []
    for p in range(3):
        starts.append(sum(data_parts[:p]))
        spans.append(data_parts[p] + (1 if p == 2 else 0))

    links.recv_wait("ex", exin)
    theirs = exin[:, pl.ds(0, half_cols)]
    mine = jnp.where(core == 0, rows_low, rows_high)
    low = jnp.where(core == 0, mine, theirs)
    high = jnp.where(core == 0, theirs, mine)
    xs[core, 0, 0, 0, :, pl.ds(0, half_cols)] = jnp.concatenate([low, high], axis=0).astype(jnp.bfloat16)
    theirs = exin[:, pl.ds(half_cols, TILE)]
    mine = jnp.where(core == 0, coarse, fine)
    low = jnp.where(core == 0, mine, theirs)
    high = jnp.where(core == 0, theirs, mine)
    xs[core, 0, 0, 0, :, pl.ds(half_cols, TILE)] = jnp.concatenate([low, high], axis=0).astype(
        jnp.bfloat16
    )

    REST = slice(1, 4)

    def chips(p, moves):
        index = [None, None, None]
        for axis, by in zip(ORDERS[p], moves):
            index[axis] = slice(0, 4) if by is None else by if isinstance(by, slice) else by % 4
        return tuple(index)

    def columns(p, piece):
        return pl.ds((starts[p] + piece[0]) * TILE, piece[1] * TILE)

    def rows_at(p, moves, piece):
        return xs.at[(core,) + chips(p, moves) + (slice(None), columns(p, piece))]

    def whole(p, lead):
        lead = tuple(pl.ds(0, n) if n else 0 for n in lead)
        return xs.at[(0,) + lead + (slice(None), columns(p, (0, spans[p])))]

    def gather(key, m, p, moves, piece, axis, by):
        there = [move - by if a == axis else move for a, move in zip(ORDERS[p], moves)]
        links.start(
            (key, p), (key, p) + m, rows_at(p, moves, piece), rows_at(p, there, piece), device(axis, by)
        )

    def share(name, p, by, line):
        ref = rows_at(p, (None, line, by), (0, spans[p]))
        links.start(("dd", p), ("dd", p, name), ref, ref, sibling)

    DIRS = ((0, 1), (1, -1))

    def start2(p, unit):
        pieces = cut(spans[p])
        for m in range(2):
            for d, by in DIRS:
                gather("a2", (m,), p, (unit, 0, 0), pieces[d ^ m], ORDERS[p][1], by)

    def wait2(p, m):
        links.recv_wait(("a2", p, m), whole(p, (0, 0, 4)))

    def forward2(p):
        wait2(p, 0)
        for d, by in DIRS:
            gather("a2", (2,), p, (None, -by, 0), cut(spans[p])[d], ORDERS[p][1], by)

    def start3(p, line, m, unit=None):
        pieces = cut(spans[p])
        for d, by in DIRS:
            gather("a3", (line, m), p, (unit, line, 0), pieces[d ^ m], ORDERS[p][2], by)

    def wait3(p, line, m):
        links.recv_wait(("a3", p, line, m), whole(p, (0, 0, 4)))

    def forward3(p, line):
        wait3(p, line, 0)
        for d, by in DIRS:
            gather("a3", (line, 2), p, (None, line, -by), cut(spans[p])[d], ORDERS[p][2], by)

    OWN = ((None, 0),)

    def places(p, spots):
        return [chips(p, (None, line, by)) for line, by in spots]

    def stacked(parts):
        parts = [part.reshape(-1, part.shape[-1]) for part in parts]
        return parts[0] if len(parts) == 1 else jnp.concatenate(parts, axis=0)

    def apart(value, ats):
        first = 0
        for at in ats:
            lead = (4,) * sum(isinstance(i, slice) for i in at)
            count = 4 ** len(lead) * ROWS
            yield at, value[first : first + count].reshape(lead + (ROWS, value.shape[-1]))
            first += count

    def layer1(p, spots):
        ats = places(p, spots)
        cols = pl.ds(starts[p] * TILE, data_parts[p] * TILE)
        x0, x1 = [stacked([xs[(half,) + at + (slice(None), cols)] for at in ats]) for half in range(2)]
        for acc, w in ((accg, wg), (accu, wu)):
            got = jnp.dot(x0, w[0, cols, :], preferred_element_type=jnp.float32)
            got = got + jnp.dot(x1, w[1, cols, :], preferred_element_type=jnp.float32)
            for at, rows in apart(got, ats):
                acc[at] += rows

    for p in range(3):
        for by in (1, -1, 2):
            gather("a1", (), p, (0, 0, 0), (0, spans[p]), ORDERS[p][0], by)
    for p in range(3):
        start2(p, 0)
    for p in range(3):
        start3(p, 0, 0, 0)
        start3(p, 0, 1, 0)

    @pl.loop(0, 4)
    def _(i):
        accg[i] = jnp.zeros_like(accg[i])
        accu[i] = jnp.zeros_like(accu[i])

    def beside(line):
        for p in range(3):
            wait3(p, line, 1)
            share(("near", line), p, 1, line)
            share(("near", line), p, -1, line)

    def far(line):
        for p in range(3):
            wait3(p, line, 2)
            share(("far", line in (0, 1)), p, 2, line)

    def first_own(p):
        links.recv_wait(("dd", p, "own"), whole(p, (0, 4, 4)))
        layer1(p, OWN)

    def first_near(p, line):
        links.recv_wait(("dd", p, ("near", line)), whole(p, (0, 2, 4)))
        layer1(p, ((line, 1), (line, -1)))

    def first_far(p, lines):
        links.recv_wait(("dd", p, ("far", 0 in lines)), whole(p, (0, 2, 4)))
        layer1(p, tuple((line, 2) for line in lines))

    for p in range(3):
        links.recv_wait(("a1", p), whole(p, (0, 0, 3)))
        start2(p, REST)
    for p in range(3):
        start3(p, 0, 0, REST)
        start3(p, 0, 1, REST)
        share("own", p, 0, 0)
    for p in range(3):
        forward2(p)
    for p in range(3):
        wait2(p, 1)
        start3(p, 1, 0)
        start3(p, -1, 0)
        share("own", p, 0, 1)
        share("own", p, 0, -1)
    for p in range(3):
        forward3(p, 0)
        start3(p, 1, 1)
    beside(0)
    for p in range(3):
        wait2(p, 2)
        share("own", p, 0, 2)
        start3(p, 2, 0)
        start3(p, -1, 1)
    for load in loads:
        load.wait()
    for p in range(3):
        forward3(p, 1)
        first_own(p)
    for p in range(3):
        forward3(p, -1)
        start3(p, 2, 1)
    far(0)
    first_near(0, 0)
    first_near(1, 0)
    beside(1)
    first_near(2, 0)
    for p in range(3):
        forward3(p, 2)
    beside(-1)
    for p in range(3):
        first_near(p, 1)
    far(1)
    first_near(0, -1)
    first_near(1, -1)
    far(-1)
    first_near(2, -1)
    first_far(0, (0, 1))
    beside(2)
    first_far(1, (0, 1))
    first_far(2, (0, 1))
    first_near(0, 2)
    far(2)
    links.start("page", "page", page.at[0], window.at[0], ahead)
    links.start("page", "page", page.at[0], window.at[4], behind)
    links.start("page", "near", page.at[0], window.at[1 + 2 * core], sibling)
    first_near(1, 2)
    first_near(2, 2)
    for p in range(3):
        first_far(p, (-1, 2))

    @pl.loop(0, 4)
    def _(i):
        @pl.loop(0, 4)
        def _(j):
            tile = pl.ds(half_cols, TILE)
            weight = xs[0, i, j, :, :, tile].astype(jnp.float32) + xs[1, i, j, :, :, tile].astype(
                jnp.float32
            )
            lane = lax.broadcasted_iota(jnp.int32, weight.shape, 2)
            weight = jnp.sum(jnp.where(lane == ep, weight, 0.0), axis=2, keepdims=True)
            gate = accg[i, j]
            hidden = gate * (1.0 / (1.0 + jnp.exp(-gate))) * accu[i, j] * weight
            hid[i, j] = hidden.astype(jnp.bfloat16)

    for p in range(3):
        links.send_wait(("a1", p), whole(p, (0, 0, 3)))
        links.send_wait(("a2", p), whole(p, (0, 3, 4)))
        links.send_wait(("a3", p), whole(p, (3, 4, 4)))
        links.send_wait(("dd", p), whole(p, (4, 4, 4)))

    def layer2(p, spots, half, extra=None):
        ats = places(p, spots)
        cols = pl.ds(starts[p] * TILE, data_parts[p] * TILE)
        rows = stacked([hid[at] for at in ats])
        got = jnp.dot(rows, wd[half, :, cols], preferred_element_type=jnp.float32)
        for at, part in apart(got, ats):
            if extra is not None:
                part = part + extra[at + (slice(None), cols)].astype(jnp.float32)
            xs[(half,) + at + (slice(None), cols)] = part.astype(jnp.bfloat16)

    def add_in(p, moves, piece, sources):
        at = chips(p, moves)
        free = [a for a in range(3) if isinstance(at[a], slice)]
        cols = columns(p, piece)
        width = piece[1] * TILE

        def one(i):
            unit = tuple(i if a in free else at[a] for a in range(3))
            index = (core,) + unit + (slice(None), cols)
            total = xs[index].astype(jnp.float32)
            for ref, lead, first in sources:
                lead = tuple(i if isinstance(l, slice) else l for l in lead)
                total = total + ref[lead + (slice(None), pl.ds(first, width))].astype(jnp.float32)
            xs[index] = total.astype(jnp.bfloat16)

        if free:
            pl.loop(at[free[0]].start, at[free[0]].stop)(one)
        else:
            one(0)

    def block(p, lead):
        lead = tuple(pl.ds(0, n) if n else 0 for n in lead)
        return dd.at[lead + (slice(None), columns(p, (0, data_parts[p])))]

    def make(p, name, spots):
        layer2(p, spots, other)
        for at in places(p, spots):
            at = at + (slice(None), columns(p, (0, data_parts[p])))
            links.start(("rd", p), ("rd", p, name), xs.at[(other,) + at], dd.at[at], sibling)

    def near_place(p, line, unit=None):
        at = chips(p, (unit, line, 0))
        return tuple(at[a] for a in range(3) if a != ORDERS[p][2])

    def scatter(key, m, p, moves, piece, dst, axis, by):
        links.start((key, p), (key, p) + m, rows_at(p, moves, piece), dst, device(axis, by))

    def far1(p, line):
        for d, by in DIRS:
            piece = cut(data_parts[p])[d]
            dst = r1a.at[
                (d,) + near_place(p, line) + (slice(None), pl.ds(starts[p] // 2 * TILE, piece[1] * TILE))
            ]
            scatter("r1", (line, 0), p, (None, line, 2), piece, dst, ORDERS[p][2], by)

    def near1(p, line, m, unit=None):
        last = "last" if unit == 0 else 1
        for d, by in DIRS:
            piece = cut(data_parts[p])[d if m == 2 else 1 - d]
            dst = r2a.at[(d,) + near_place(p, line, unit) + (slice(None), columns(p, piece))]
            scatter("r1", (line, last), p, (unit, line, by), piece, dst, ORDERS[p][2], by)

    def pass1(p, line, unit=None):
        if unit != 0:
            links.recv_wait(("r1", p, line, 0), block(p, (0, 0, 4)))
        for d, by in DIRS:
            piece = cut(data_parts[p])[d]
            place = (d,) + near_place(p, line, unit)
            add_in(p, (unit, line, by), piece, ((r1a, place, starts[p] // 2 * TILE),))
        near1(p, line, 2, unit)

    def lead_of(unit):
        return (0, 0, 2) if unit == 0 else (0, 2, 3) if unit == REST else (0, 2, 4)

    def end1(p, line, unit=None):
        links.recv_wait(("r1", p, line, "last" if unit == 0 else 1), block(p, lead_of(unit)))
        place = near_place(p, line, unit)
        first = starts[p] * TILE
        add_in(
            p,
            (unit, line, 0),
            (0, data_parts[p]),
            ((r2a, (0,) + place, first), (r2a, (1,) + place, first)),
        )

    def far2(p):
        for d, by in DIRS:
            piece = cut(data_parts[p])[d]
            dst = r1b.at[d, :, :, pl.ds(starts[p] // 2 * TILE, piece[1] * TILE)]
            scatter("r2", (0,), p, (None, 2, 0), piece, dst, ORDERS[p][1], by)

    def near2(p, d, m, unit):
        by = (1, -1)[d]
        piece = cut(data_parts[p])[d if m == 2 else 1 - d]
        dst = r2b.at[d, unit, :, columns(p, piece)]
        scatter("r2", ("last" if unit == 0 else 1,), p, (unit, by, 0), piece, dst, ORDERS[p][1], by)

    def pass2(p):
        links.recv_wait(("r2", p, 0), block(p, (0, 0, 4)))
        for d, by in DIRS:
            piece = cut(data_parts[p])[d]
            add_in(p, (None, by, 0), piece, ((r1b, (d, slice(None)), starts[p] // 2 * TILE),))
            near2(p, d, 2, REST)

    def end2(p, unit):
        links.recv_wait(("r2", p, "last" if unit == 0 else 1), block(p, lead_of(unit)))
        first = starts[p] * TILE
        add_in(
            p,
            (unit, 0, 0),
            (0, data_parts[p]),
            ((r2b, (0, unit), first), (r2b, (1, unit), first)),
        )

    def units(p):
        piece = (0, data_parts[p])
        for i, by in ((2, 2), (0, 1), (1, -1)):
            dst = rc.at[i, :, columns(p, piece)]
            scatter("r3", (), p, (by, 0, 0), piece, dst, ORDERS[p][0], by)

    def end3(p):
        links.recv_wait(("r3", p), block(p, (0, 0, 3)))
        first = starts[p] * TILE
        add_in(p, (0, 0, 0), (0, data_parts[p]), tuple((rc, (i,), first) for i in range(3)))

    BACK = (2, 1, -1, 0)

    def settle(p, name, spots):
        links.recv_wait(("rd", p, name), block(p, (0, 4 if name == "own" else len(spots), 4)))
        layer2(p, spots, core, dd)

    def onward(line):
        for p in range(3):
            end1(p, line)
            if line == 2:
                far2(p)
            else:
                near2(p, 0 if line == 1 else 1, 1, REST)

    begin, first_page, span = 0, 0, 0
    for i in range(tree_sizes.shape[1]):
        size = tree_sizes[0, i]
        inside = (begin <= ep) & (ep < begin + size)
        first_page = jnp.where(inside, begin, first_page)
        span = jnp.where(inside, size, span)
        begin = begin + size
    first_slot = jnp.clip(first_page - ep + 2, 0, 2)

    def dot_t(a, b):
        return lax.dot_general(a, b, (((1,), (1,)), ((), ())), preferred_element_type=jnp.float32)

    def attend(i):
        leaves = (2 * i, 2 * i + 1)
        rows = q_all[pl.ds(2 * i, 2)].reshape(2 * q_all.shape[1], q_all.shape[2])
        scores = []
        for k in range(3):
            got = jnp.dot(rows, window[first_slot + k], preferred_element_type=jnp.float32) * score_scale
            scores.append(jnp.where(k < span, got, -1e30))
        near = [
            jnp.dot(q_all[leaf], near_all[leaf], preferred_element_type=jnp.float32) * score_scale
            for leaf in leaves
        ]
        scores.append(jnp.concatenate(near, axis=0))
        top = scores[3].max(axis=1, keepdims=True)
        for k in range(3):
            top = jnp.maximum(top, scores[k].max(axis=1, keepdims=True))
        weights = [jnp.exp(got - top) for got in scores]
        total = weights[3].sum(axis=1, keepdims=True)
        for k in range(3):
            total = total + weights[k].sum(axis=1, keepdims=True)
        probs = [got.astype(jnp.bfloat16) for got in weights]
        heads = q_all.shape[1]
        mixed = jnp.concatenate(
            [
                dot_t(probs[3][n * heads : (n + 1) * heads], near_all[leaf, pl.ds(0, LATENT)])
                for n, leaf in enumerate(leaves)
            ],
            axis=0,
        )
        for k in range(3):
            mixed = mixed + dot_t(probs[k], window[first_slot + k, pl.ds(0, LATENT)])
        context[pl.ds(2 * i, 2)] = (mixed / total).astype(jnp.bfloat16).reshape(2, heads, LATENT)

    FAR, NEAR = ((2, 2),), ((2, 1), (2, -1))
    for p in range(3):
        make(p, "far", FAR)
    for p in range(3):
        make(p, "near", NEAR)
        settle(p, "far", FAR)
        far1(p, 2)
    tasks = [(p, line, ((line, 2), (line, 1), (line, -1))) for line in BACK[1:] for p in range(3)]
    tasks += [(p, "own", OWN) for p in range(3)]
    make(*tasks[0])
    settle(0, "near", NEAR)
    near1(0, 2, 1)
    make(*tasks[1])
    for p in (1, 2):
        settle(p, "near", NEAR)
        near1(p, 2, 1)
    for n, (p, line, spots) in enumerate(tasks):
        if n + 2 < len(tasks):
            make(*tasks[n + 2])
        settle(p, line, spots)
        if line != "own":
            far1(p, line)
            near1(p, line, 1, REST if line == 0 else None)
        if n == 2:
            for q in range(3):
                pass1(q, 2)
            links.recv_wait("page", window.at[pl.ds(0, 2)])
            links.start("page", "near", window.at[4 * other], window.at[3 - 2 * core], sibling)
        if n == 5:
            for q in range(3):
                pass1(q, 1)
            for load in att_loads:
                load.wait()
            links.recv_wait("near", window.at[pl.ds(0, 2)])
            attend(0)
    for p in range(3):
        pass1(p, -1)
    onward(2)
    attend(1)
    onward(1)
    for p in range(3):
        pass1(p, 0, REST)
    onward(-1)
    attend(2)
    for p in range(3):
        pass2(p)
    for p in range(3):
        near1(p, 0, 1, 0)
        pass1(p, 0, 0)
    for p in range(3):
        for d in range(2):
            near2(p, d, 1, 0)
            near2(p, d, 2, 0)
    attend(3)
    for p in range(3):
        end1(p, 0, REST)
    for p in range(3):
        end2(p, REST)
        units(p)
    for p in range(3):
        end1(p, 0, 0)
        end2(p, 0)
    mine = []
    for p in range(3):
        end3(p)
        cols = columns(p, (0, data_parts[p]))
        total = xs[core, 0, 0, 0, :, cols].astype(jnp.float32)
        low, high = total[:8], total[8:]
        backsrc[:, cols] = jnp.where(core == 0, high, low)
        links.start("back", "back", backsrc.at[:, cols], exback.at[:, cols], sibling)
        mine.append(jnp.where(core == 0, low, high))
    mine = jnp.concatenate(mine, axis=1)
    for p in range(3):
        links.send_wait(("rd", p), block(p, (4, 4, 4)))
        links.send_wait(("r1", p), block(p, (3, 4, 4)))
        links.send_wait(("r2", p), block(p, (0, 3, 4)))
        links.send_wait(("r3", p), block(p, (0, 0, 3)))
    links.send_wait("page", window.at[pl.ds(0, 4)])
    links.send_wait("ex", exsrc)
    links.recv_wait("back", exback)
    theirs = exback[...]
    out[:, pl.ds(0, half_cols)] = jnp.where(core == 0, mine, theirs).astype(jnp.bfloat16)
    out[:, pl.ds(half_cols, half_cols)] = jnp.where(core == 0, theirs, mine).astype(jnp.bfloat16)
    links.send_wait("back", backsrc)


def hand_over(context, mix, context_out, mix_out, sems):
    copies = [
        pltpu.make_async_copy(context, context_out, sems.at[0]),
        pltpu.make_async_copy(mix, mix_out, sems.at[1]),
    ]
    for copy in copies:
        copy.start()
    for copy in copies:
        copy.wait()


def local(
    hidden_rows,
    expert_ids,
    gate_weights,
    w_gate,
    w_up,
    w_down,
    queries,
    suffix_cache,
    prefix_pages,
    tree_sizes,
):
    leaves, width = hidden_rows.shape
    half = width // 2
    ffq = w_gate.shape[2]
    pairs = half // TILE // 2
    data_parts = [2 * ((pairs + 2 - p) // 3) for p in range(3)]
    grid = (4, 4, 4)
    bf16, f32 = jnp.bfloat16, jnp.float32
    first_cut = sum(cut(n)[0][1] for n in data_parts) * TILE
    heads, channels = queries.shape[1:]
    suffix_cache, prefix_pages = jnp.swapaxes(suffix_cache, 1, 2), jnp.swapaxes(prefix_pages, 1, 2)
    shapes = [
        ((2,) + grid + (ROWS, half + TILE), bf16),
        ((2, half, ffq), bf16),
        ((2, half, ffq), bf16),
        ((2, ffq, half), bf16),
        (grid + (ROWS, ffq), f32),
        (grid + (ROWS, ffq), f32),
        (grid + (ROWS, ffq), bf16),
        (grid + (ROWS, half), bf16),
        ((2, 4, 4, ROWS, first_cut), bf16),
        ((2, 4, 4, ROWS, half), bf16),
        ((2, 4, ROWS, first_cut), bf16),
        ((2, 4, ROWS, half), bf16),
        ((3, ROWS, half), bf16),
        ((leaves, half + TILE), f32),
        ((leaves, half + TILE), f32),
        ((leaves, half), f32),
        ((leaves, half), f32),
        ((5,) + prefix_pages.shape[1:], bf16),
        (queries.shape, bf16),
        (suffix_cache.shape, bf16),
        ((leaves, width), bf16),
        (expert_ids.shape, expert_ids.dtype),
        (gate_weights.shape, gate_weights.dtype),
    ]
    scratch = [pltpu.VMEM(shape, kind) for shape, kind in shapes]
    scratch.append(pltpu.SMEM(tree_sizes.shape, tree_sizes.dtype))
    scratch += [pltpu.SemaphoreType.DMA((n,)) for n in (6, 7, 27, 130)]
    vmem, hbm = pl.BlockSpec(memory_space=pltpu.VMEM), pl.BlockSpec(memory_space=pl.ANY)
    results = pl.pallas_call(
        functools.partial(kernel, data_parts),
        out_shape=(pltpu.VMEM((leaves, heads, LATENT), bf16), pltpu.VMEM((leaves, width), bf16)),
        in_specs=[hbm] * 10,
        out_specs=(vmem, vmem),
        scratch_shapes=scratch,
        compiler_params=pltpu.CompilerParams(
            collective_id=0, has_side_effects=True, vmem_limit_bytes=61 * 1024 * 1024
        ),
        name="experts",
    )(
        hidden_rows,
        expert_ids,
        gate_weights,
        tree_sizes,
        w_gate,
        w_up,
        w_down,
        queries,
        suffix_cache,
        prefix_pages,
    )
    results = [pltpu.with_memory_space_constraint(r, pltpu.VMEM) for r in results]
    return pl.pallas_call(
        hand_over,
        out_shape=tuple(jax.ShapeDtypeStruct(r.shape, r.dtype) for r in results),
        in_specs=[vmem] * 2,
        out_specs=(hbm, hbm),
        scratch_shapes=[pltpu.SemaphoreType.DMA((2,))],
        name="results",
    )(*results)


def solution(mesh):
    return jax.shard_map(
        local,
        mesh=mesh,
        in_specs=(
            P(("dp", "ep"), None),
            P(("dp", "ep"), None),
            P(("dp", "ep"), None),
            P("ep", None, "dp"),
            P("ep", None, "dp"),
            P("ep", "dp", None),
            P(("dp", "ep"), None, None),
            P(("dp", "ep"), None, None),
            P(("dp", "ep"), None, None),
            P("dp", None),
        ),
        out_specs=(P(("dp", "ep"), None, None), P(("dp", "ep"), None)),
        check_vma=False,
    )
```

```python
import functools

import jax
import jax.numpy as jnp
from jax import lax
from jax.experimental import pallas as pl
from jax.experimental.pallas import tpu as pltpu
from jax.sharding import PartitionSpec as P

LATENT = 512
TILE = 128
CHUNK = 256
ROWS = 16
score_scale = 192.0 ** (-0.5)
MESH = pl.DeviceIdType.MESH
LINES = (0, 1, -1, 2)
ORDERS = ((1, 2, 0), (2, 0, 1), (0, 1, 2))


class Links:
    def __init__(self, send, recv):
        self.send, self.recv = send, recv
        self.sent, self.got = {}, {}

    def start(self, sent, got, src, dst, device):
        pltpu.make_async_remote_copy(
            src_ref=src,
            dst_ref=dst,
            send_sem=self.send.at[self.sent.setdefault(sent, len(self.sent))],
            recv_sem=self.recv.at[self.got.setdefault(got, len(self.got))],
            device_id=device,
            device_id_type=MESH,
        ).start()

    def recv_wait(self, got, ref):
        pltpu.make_async_copy(ref, ref, self.recv.at[self.got[got]]).wait()

    def send_wait(self, sent, ref):
        pltpu.make_async_copy(ref, ref, self.send.at[self.sent[sent]]).wait()


def cut(part_tiles):
    first = (part_tiles + 1) // 2
    return ((0, first), (first, part_tiles - first))


def kernel(
    data_parts,
    hidden_hbm,
    ids_hbm,
    gates_hbm,
    tree_hbm,
    wg_hbm,
    wu_hbm,
    wd_hbm,
    queries,
    suffix,
    page,
    context,
    out,
    xs,
    wg,
    wu,
    wd,
    accg,
    accu,
    hid,
    dd,
    r1a,
    r2a,
    r1b,
    r2b,
    rc,
    exsrc,
    exin,
    backsrc,
    exback,
    window,
    q_all,
    near_all,
    hidden_rows,
    expert_ids,
    gate_weights,
    tree_sizes,
    wsem,
    asem,
    send_sem,
    recv_sem,
):
    ffq = wg.shape[2]
    half_cols = wg.shape[1]
    y = lax.axis_index("dp")
    ep = lax.axis_index("ep")
    core = lax.rem(ep, 2)
    x = ep // 8
    z = lax.rem(ep // 2, 4)
    here = (x, y, z)
    other = 1 - core

    def shift(axis, by):
        return lax.rem(here[axis] + (by + 4) % 4, 4)

    def device(axis, by):
        place = [x, y, z]
        place[axis] = shift(axis, by)
        return (place[1], place[0] * 8 + place[2] * 2 + core)

    sibling = (y, x * 8 + z * 2 + other)
    ahead = (y, lax.rem(ep + 2, 32))
    behind = (y, lax.rem(ep + 30, 32))

    barrier = pltpu.get_barrier_semaphore()
    greeted = [device(axis, by) for axis in range(3) for by in (1, -1, 2)] + [sibling, ahead, behind]
    for other_device in greeted:
        pl.semaphore_signal(barrier, inc=1, device_id=other_device, device_id_type=MESH)

    first_loads = [
        pltpu.make_async_copy(src, dst, asem.at[3 + i])
        for i, (src, dst) in enumerate(
            (
                (hidden_hbm, hidden_rows),
                (ids_hbm, expert_ids),
                (gates_hbm, gate_weights),
                (tree_hbm, tree_sizes),
            )
        )
    ]
    for load in first_loads:
        load.start()
    loads = []
    for half in range(2):
        rows = pl.ds(half * half_cols, half_cols)
        loads.append(pltpu.make_async_copy(wg_hbm.at[0, rows], wg.at[half], wsem.at[half]))
        loads.append(pltpu.make_async_copy(wu_hbm.at[0, rows], wu.at[half], wsem.at[2 + half]))
    for half in range(2):
        cols = pl.ds(half * half_cols, half_cols)
        loads.append(pltpu.make_async_copy(wd_hbm.at[0, :, cols], wd.at[half], wsem.at[4 + half]))
    att_loads = [
        pltpu.make_async_copy(queries, q_all, asem.at[0]),
        pltpu.make_async_copy(suffix, near_all, asem.at[1]),
        pltpu.make_async_copy(page.at[0], window.at[2], asem.at[2]),
    ]

    for load in first_loads:
        load.wait()
    rows_low = hidden_rows[:, pl.ds(0, half_cols)].astype(jnp.float32)
    rows_high = hidden_rows[:, pl.ds(half_cols, half_cols)].astype(jnp.float32)
    lane = lax.broadcasted_iota(jnp.int32, (8, TILE), 1)
    weight = jnp.zeros((8, TILE), jnp.float32)
    for k in range(expert_ids.shape[1]):
        chosen = lane == expert_ids[:, pl.ds(k, 1)]
        weight = weight + jnp.where(chosen, gate_weights[:, pl.ds(k, 1)], 0.0)
    coarse = weight.astype(jnp.bfloat16).astype(jnp.float32)
    fine = weight - coarse
    exsrc[:, pl.ds(0, half_cols)] = jnp.where(core == 0, rows_high, rows_low)
    exsrc[:, pl.ds(half_cols, TILE)] = jnp.where(core == 0, fine, coarse)

    pl.semaphore_wait(barrier, len(greeted))
    links = Links(send_sem, recv_sem)
    links.start("ex", "ex", exsrc, exin, sibling)
    for load in loads + att_loads:
        load.start()

    starts = []
    spans = []
    for p in range(3):
        starts.append(sum(data_parts[:p]))
        spans.append(data_parts[p] + (1 if p == 2 else 0))

    links.recv_wait("ex", exin)
    theirs = exin[:, pl.ds(0, half_cols)]
    mine = jnp.where(core == 0, rows_low, rows_high)
    low = jnp.where(core == 0, mine, theirs)
    high = jnp.where(core == 0, theirs, mine)
    xs[core, 0, 0, 0, :, pl.ds(0, half_cols)] = jnp.concatenate([low, high], axis=0).astype(jnp.bfloat16)
    theirs = exin[:, pl.ds(half_cols, TILE)]
    mine = jnp.where(core == 0, coarse, fine)
    low = jnp.where(core == 0, mine, theirs)
    high = jnp.where(core == 0, theirs, mine)
    xs[core, 0, 0, 0, :, pl.ds(half_cols, TILE)] = jnp.concatenate([low, high], axis=0).astype(
        jnp.bfloat16
    )

    REST = slice(1, 4)

    def chips(p, moves):
        index = [None, None, None]
        for axis, by in zip(ORDERS[p], moves):
            index[axis] = slice(0, 4) if by is None else by if isinstance(by, slice) else by % 4
        return tuple(index)

    def columns(p, piece):
        return pl.ds((starts[p] + piece[0]) * TILE, piece[1] * TILE)

    def rows_at(p, moves, piece):
        return xs.at[(core,) + chips(p, moves) + (slice(None), columns(p, piece))]

    def whole(p, lead):
        lead = tuple(pl.ds(0, n) if n else 0 for n in lead)
        return xs.at[(0,) + lead + (slice(None), columns(p, (0, spans[p])))]

    def gather(key, m, p, moves, piece, axis, by):
        there = [move - by if a == axis else move for a, move in zip(ORDERS[p], moves)]
        links.start(
            (key, p), (key, p) + m, rows_at(p, moves, piece), rows_at(p, there, piece), device(axis, by)
        )

    def share(name, p, by, line):
        ref = rows_at(p, (None, line, by), (0, spans[p]))
        links.start(("dd", p), ("dd", p, name), ref, ref, sibling)

    DIRS = ((0, 1), (1, -1))

    def start2(p, unit):
        pieces = cut(spans[p])
        for m in range(2):
            for d, by in DIRS:
                gather("a2", (m,), p, (unit, 0, 0), pieces[d ^ m], ORDERS[p][1], by)

    def wait2(p, m):
        links.recv_wait(("a2", p, m), whole(p, (0, 0, 4)))

    def forward2(p):
        wait2(p, 0)
        for d, by in DIRS:
            gather("a2", (2,), p, (None, -by, 0), cut(spans[p])[d], ORDERS[p][1], by)

    def start3(p, line, m, unit=None):
        pieces = cut(spans[p])
        for d, by in DIRS:
            gather("a3", (line, m), p, (unit, line, 0), pieces[d ^ m], ORDERS[p][2], by)

    def wait3(p, line, m):
        links.recv_wait(("a3", p, line, m), whole(p, (0, 0, 4)))

    def forward3(p, line):
        wait3(p, line, 0)
        for d, by in DIRS:
            gather("a3", (line, 2), p, (None, line, -by), cut(spans[p])[d], ORDERS[p][2], by)

    OWN = ((None, 0),)

    def places(p, spots):
        return [chips(p, (None, line, by)) for line, by in spots]

    def stacked(parts):
        parts = [part.reshape(-1, part.shape[-1]) for part in parts]
        return parts[0] if len(parts) == 1 else jnp.concatenate(parts, axis=0)

    def apart(value, ats):
        first = 0
        for at in ats:
            lead = (4,) * sum(isinstance(i, slice) for i in at)
            count = 4 ** len(lead) * ROWS
            yield at, value[first : first + count].reshape(lead + (ROWS, value.shape[-1]))
            first += count

    def layer1(p, spots):
        ats = places(p, spots)
        cols = pl.ds(starts[p] * TILE, data_parts[p] * TILE)
        x0, x1 = [stacked([xs[(half,) + at + (slice(None), cols)] for at in ats]) for half in range(2)]
        for acc, w in ((accg, wg), (accu, wu)):
            got = jnp.dot(x0, w[0, cols, :], preferred_element_type=jnp.float32)
            got = got + jnp.dot(x1, w[1, cols, :], preferred_element_type=jnp.float32)
            for at, rows in apart(got, ats):
                acc[at] += rows

    for p in range(3):
        for by in (1, -1, 2):
            gather("a1", (), p, (0, 0, 0), (0, spans[p]), ORDERS[p][0], by)
    for p in range(3):
        start2(p, 0)
    for p in range(3):
        start3(p, 0, 0, 0)
        start3(p, 0, 1, 0)

    @pl.loop(0, 4)
    def _(i):
        accg[i] = jnp.zeros_like(accg[i])
        accu[i] = jnp.zeros_like(accu[i])

    def beside(line):
        for p in range(3):
            wait3(p, line, 1)
            share(("near", line), p, 1, line)
            share(("near", line), p, -1, line)

    def far(line):
        for p in range(3):
            wait3(p, line, 2)
            share(("far", line in (0, 1)), p, 2, line)

    def first_own(p):
        links.recv_wait(("dd", p, "own"), whole(p, (0, 4, 4)))
        layer1(p, OWN)

    def first_near(p, line):
        links.recv_wait(("dd", p, ("near", line)), whole(p, (0, 2, 4)))
        layer1(p, ((line, 1), (line, -1)))

    def first_far(p, lines):
        links.recv_wait(("dd", p, ("far", 0 in lines)), whole(p, (0, 2, 4)))
        layer1(p, tuple((line, 2) for line in lines))

    for p in range(3):
        links.recv_wait(("a1", p), whole(p, (0, 0, 3)))
        start2(p, REST)
    for p in range(3):
        start3(p, 0, 0, REST)
        start3(p, 0, 1, REST)
        share("own", p, 0, 0)
    for p in range(3):
        forward2(p)
    for p in range(3):
        wait2(p, 1)
        start3(p, 1, 0)
        start3(p, -1, 0)
        share("own", p, 0, 1)
        share("own", p, 0, -1)
    for p in range(3):
        forward3(p, 0)
        start3(p, 1, 1)
    beside(0)
    for p in range(3):
        wait2(p, 2)
        share("own", p, 0, 2)
        start3(p, 2, 0)
        start3(p, -1, 1)
    for load in loads:
        load.wait()
    for p in range(3):
        forward3(p, 1)
        first_own(p)
    for p in range(3):
        forward3(p, -1)
        start3(p, 2, 1)
    far(0)
    first_near(0, 0)
    first_near(1, 0)
    beside(1)
    first_near(2, 0)
    for p in range(3):
        forward3(p, 2)
    beside(-1)
    for p in range(3):
        first_near(p, 1)
    far(1)
    first_near(0, -1)
    first_near(1, -1)
    far(-1)
    first_near(2, -1)
    first_far(0, (0, 1))
    beside(2)
    first_far(1, (0, 1))
    first_far(2, (0, 1))
    first_near(0, 2)
    far(2)
    links.start("page", "page", page.at[0], window.at[0], ahead)
    links.start("page", "page", page.at[0], window.at[4], behind)
    links.start("page", "near", page.at[0], window.at[1 + 2 * core], sibling)
    first_near(1, 2)
    first_near(2, 2)
    for p in range(3):
        first_far(p, (-1, 2))

    @pl.loop(0, 4)
    def _(i):
        @pl.loop(0, 4)
        def _(j):
            tile = pl.ds(half_cols, TILE)
            weight = xs[0, i, j, :, :, tile].astype(jnp.float32) + xs[1, i, j, :, :, tile].astype(
                jnp.float32
            )
            lane = lax.broadcasted_iota(jnp.int32, weight.shape, 2)
            weight = jnp.sum(jnp.where(lane == ep, weight, 0.0), axis=2, keepdims=True)
            gate = accg[i, j]
            hidden = gate * (1.0 / (1.0 + jnp.exp(-gate))) * accu[i, j] * weight
            hid[i, j] = hidden.astype(jnp.bfloat16)

    for p in range(3):
        links.send_wait(("a1", p), whole(p, (0, 0, 3)))
        links.send_wait(("a2", p), whole(p, (0, 3, 4)))
        links.send_wait(("a3", p), whole(p, (3, 4, 4)))
        links.send_wait(("dd", p), whole(p, (4, 4, 4)))

    def layer2(p, spots, half, extra=None):
        ats = places(p, spots)
        cols = pl.ds(starts[p] * TILE, data_parts[p] * TILE)
        rows = stacked([hid[at] for at in ats])
        got = jnp.dot(rows, wd[half, :, cols], preferred_element_type=jnp.float32)
        for at, part in apart(got, ats):
            if extra is not None:
                part = part + extra[at + (slice(None), cols)].astype(jnp.float32)
            xs[(half,) + at + (slice(None), cols)] = part.astype(jnp.bfloat16)

    def add_in(p, moves, piece, sources):
        at = chips(p, moves)
        free = [a for a in range(3) if isinstance(at[a], slice)]
        cols = columns(p, piece)
        width = piece[1] * TILE

        def one(i):
            unit = tuple(i if a in free else at[a] for a in range(3))
            index = (core,) + unit + (slice(None), cols)
            total = xs[index].astype(jnp.float32)
            for ref, lead, first in sources:
                lead = tuple(i if isinstance(l, slice) else l for l in lead)
                total = total + ref[lead + (slice(None), pl.ds(first, width))].astype(jnp.float32)
            xs[index] = total.astype(jnp.bfloat16)

        if free:
            pl.loop(at[free[0]].start, at[free[0]].stop)(one)
        else:
            one(0)

    def block(p, lead):
        lead = tuple(pl.ds(0, n) if n else 0 for n in lead)
        return dd.at[lead + (slice(None), columns(p, (0, data_parts[p])))]

    def make(p, name, spots):
        layer2(p, spots, other)
        ats = [chips(p, (None, name, REST))] if len(spots) == 3 else places(p, spots)
        for at in ats:
            at = at + (slice(None), columns(p, (0, data_parts[p])))
            links.start(("rd", p), ("rd", p, name), xs.at[(other,) + at], dd.at[at], sibling)

    def near_place(p, line, unit=None):
        at = chips(p, (unit, line, 0))
        return tuple(at[a] for a in range(3) if a != ORDERS[p][2])

    def scatter(key, m, p, moves, piece, dst, axis, by):
        links.start((key, p), (key, p) + m, rows_at(p, moves, piece), dst, device(axis, by))

    def far1(p, line):
        for d, by in DIRS:
            piece = cut(data_parts[p])[d]
            dst = r1a.at[
                (d,) + near_place(p, line) + (slice(None), pl.ds(starts[p] // 2 * TILE, piece[1] * TILE))
            ]
            scatter("r1", (line, 0), p, (None, line, 2), piece, dst, ORDERS[p][2], by)

    def near1(p, line, m, unit=None):
        last = "last" if unit == 0 else 1
        for d, by in DIRS:
            piece = cut(data_parts[p])[d if m == 2 else 1 - d]
            dst = r2a.at[(d,) + near_place(p, line, unit) + (slice(None), columns(p, piece))]
            scatter("r1", (line, last), p, (unit, line, by), piece, dst, ORDERS[p][2], by)

    def pass1(p, line, unit=None):
        if unit != 0:
            links.recv_wait(("r1", p, line, 0), block(p, (0, 0, 4)))
        for d, by in DIRS:
            piece = cut(data_parts[p])[d]
            place = (d,) + near_place(p, line, unit)
            add_in(p, (unit, line, by), piece, ((r1a, place, starts[p] // 2 * TILE),))
        near1(p, line, 2, unit)

    def lead_of(unit):
        return (0, 0, 2) if unit == 0 else (0, 2, 3) if unit == REST else (0, 2, 4)

    def end1(p, line, unit=None):
        links.recv_wait(("r1", p, line, "last" if unit == 0 else 1), block(p, lead_of(unit)))
        place = near_place(p, line, unit)
        first = starts[p] * TILE
        add_in(
            p,
            (unit, line, 0),
            (0, data_parts[p]),
            ((r2a, (0,) + place, first), (r2a, (1,) + place, first)),
        )

    def far2(p):
        for d, by in DIRS:
            piece = cut(data_parts[p])[d]
            dst = r1b.at[d, :, :, pl.ds(starts[p] // 2 * TILE, piece[1] * TILE)]
            scatter("r2", (0,), p, (None, 2, 0), piece, dst, ORDERS[p][1], by)

    def near2(p, d, m, unit):
        by = (1, -1)[d]
        piece = cut(data_parts[p])[d if m == 2 else 1 - d]
        dst = r2b.at[d, unit, :, columns(p, piece)]
        scatter("r2", ("last" if unit == 0 else 1,), p, (unit, by, 0), piece, dst, ORDERS[p][1], by)

    def pass2(p):
        links.recv_wait(("r2", p, 0), block(p, (0, 0, 4)))
        for d, by in DIRS:
            piece = cut(data_parts[p])[d]
            add_in(p, (None, by, 0), piece, ((r1b, (d, slice(None)), starts[p] // 2 * TILE),))
            near2(p, d, 2, REST)

    def end2(p, unit):
        links.recv_wait(("r2", p, "last" if unit == 0 else 1), block(p, lead_of(unit)))
        first = starts[p] * TILE
        add_in(
            p,
            (unit, 0, 0),
            (0, data_parts[p]),
            ((r2b, (0, unit), first), (r2b, (1, unit), first)),
        )

    def units(p):
        piece = (0, data_parts[p])
        for i, by in ((2, 2), (0, 1), (1, -1)):
            dst = rc.at[i, :, columns(p, piece)]
            scatter("r3", (), p, (by, 0, 0), piece, dst, ORDERS[p][0], by)

    def end3(p):
        links.recv_wait(("r3", p), block(p, (0, 0, 3)))
        first = starts[p] * TILE
        add_in(p, (0, 0, 0), (0, data_parts[p]), tuple((rc, (i,), first) for i in range(3)))

    BACK = (2, 1, -1, 0)

    def settle(p, name, spots):
        links.recv_wait(("rd", p, name), block(p, (0, 4 if name == "own" else len(spots), 4)))
        layer2(p, spots, core, dd)

    def onward(line):
        for p in range(3):
            end1(p, line)
            if line == 2:
                far2(p)
            else:
                near2(p, 0 if line == 1 else 1, 1, REST)

    begin, first_page, span = 0, 0, 0
    for i in range(tree_sizes.shape[1]):
        size = tree_sizes[0, i]
        inside = (begin <= ep) & (ep < begin + size)
        first_page = jnp.where(inside, begin, first_page)
        span = jnp.where(inside, size, span)
        begin = begin + size
    first_slot = jnp.clip(first_page - ep + 2, 0, 2)

    def dot_t(a, b):
        return lax.dot_general(a, b, (((1,), (1,)), ((), ())), preferred_element_type=jnp.float32)

    def attend(i):
        leaves = (2 * i, 2 * i + 1)
        rows = q_all[pl.ds(2 * i, 2)].reshape(2 * q_all.shape[1], q_all.shape[2])
        scores = []
        for k in range(3):
            got = jnp.dot(rows, window[first_slot + k], preferred_element_type=jnp.float32) * score_scale
            scores.append(jnp.where(k < span, got, -1e30))
        near = [
            jnp.dot(q_all[leaf], near_all[leaf], preferred_element_type=jnp.float32) * score_scale
            for leaf in leaves
        ]
        scores.append(jnp.concatenate(near, axis=0))
        top = scores[3].max(axis=1, keepdims=True)
        for k in range(3):
            top = jnp.maximum(top, scores[k].max(axis=1, keepdims=True))
        weights = [jnp.exp(got - top) for got in scores]
        total = weights[3].sum(axis=1, keepdims=True)
        for k in range(3):
            total = total + weights[k].sum(axis=1, keepdims=True)
        probs = [got.astype(jnp.bfloat16) for got in weights]
        heads = q_all.shape[1]
        mixed = jnp.concatenate(
            [
                dot_t(probs[3][n * heads : (n + 1) * heads], near_all[leaf, pl.ds(0, LATENT)])
                for n, leaf in enumerate(leaves)
            ],
            axis=0,
        )
        for k in range(3):
            mixed = mixed + dot_t(probs[k], window[first_slot + k, pl.ds(0, LATENT)])
        context[pl.ds(2 * i, 2)] = (mixed / total).astype(jnp.bfloat16).reshape(2, heads, LATENT)

    FAR, NEAR = ((2, 2),), ((2, 1), (2, -1))
    for p in range(3):
        make(p, "far", FAR)
    for p in range(3):
        make(p, "near", NEAR)
        settle(p, "far", FAR)
        far1(p, 2)
    tasks = [(p, line, ((line, 2), (line, 1), (line, -1))) for line in BACK[1:] for p in range(3)]
    tasks += [(p, "own", OWN) for p in range(3)]
    make(*tasks[0])
    settle(0, "near", NEAR)
    near1(0, 2, 1)
    make(*tasks[1])
    for p in (1, 2):
        settle(p, "near", NEAR)
        near1(p, 2, 1)
    for n, (p, line, spots) in enumerate(tasks):
        if n + 2 < len(tasks):
            make(*tasks[n + 2])
        settle(p, line, spots)
        if line != "own":
            far1(p, line)
            near1(p, line, 1, REST if line == 0 else None)
        if n == 2:
            for q in range(3):
                pass1(q, 2)
            links.recv_wait("page", window.at[pl.ds(0, 2)])
            links.start("page", "near", window.at[4 * other], window.at[3 - 2 * core], sibling)
        if n == 5:
            for q in range(3):
                pass1(q, 1)
            for load in att_loads:
                load.wait()
            links.recv_wait("near", window.at[pl.ds(0, 2)])
            attend(0)
    for p in range(3):
        pass1(p, -1)
    onward(2)
    attend(1)
    onward(1)
    for p in range(3):
        pass1(p, 0, REST)
    onward(-1)
    attend(2)
    for p in range(3):
        pass2(p)
    for p in range(3):
        near1(p, 0, 1, 0)
        pass1(p, 0, 0)
    for p in range(3):
        for d in range(2):
            near2(p, d, 1, 0)
            near2(p, d, 2, 0)
    attend(3)
    for p in range(3):
        end1(p, 0, REST)
    for p in range(3):
        end2(p, REST)
        units(p)
    for p in range(3):
        end1(p, 0, 0)
        end2(p, 0)
    mine = []
    for p in range(3):
        end3(p)
        cols = columns(p, (0, data_parts[p]))
        total = xs[core, 0, 0, 0, :, cols].astype(jnp.float32)
        low, high = total[:8], total[8:]
        backsrc[:, cols] = jnp.where(core == 0, high, low)
        links.start("back", "back", backsrc.at[:, cols], exback.at[:, cols], sibling)
        mine.append(jnp.where(core == 0, low, high))
    mine = jnp.concatenate(mine, axis=1)
    for p in range(3):
        links.send_wait(("rd", p), block(p, (4, 4, 4)))
        links.send_wait(("r1", p), block(p, (3, 4, 4)))
        links.send_wait(("r2", p), block(p, (0, 3, 4)))
        links.send_wait(("r3", p), block(p, (0, 0, 3)))
    links.send_wait("page", window.at[pl.ds(0, 4)])
    links.send_wait("ex", exsrc)
    links.recv_wait("back", exback)
    theirs = exback[...]
    out[:, pl.ds(0, half_cols)] = jnp.where(core == 0, mine, theirs).astype(jnp.bfloat16)
    out[:, pl.ds(half_cols, half_cols)] = jnp.where(core == 0, theirs, mine).astype(jnp.bfloat16)
    links.send_wait("back", backsrc)


def hand_over(context, mix, context_out, mix_out, sems):
    copies = [
        pltpu.make_async_copy(context, context_out, sems.at[0]),
        pltpu.make_async_copy(mix, mix_out, sems.at[1]),
    ]
    for copy in copies:
        copy.start()
    for copy in copies:
        copy.wait()


def local(
    hidden_rows,
    expert_ids,
    gate_weights,
    w_gate,
    w_up,
    w_down,
    queries,
    suffix_cache,
    prefix_pages,
    tree_sizes,
):
    leaves, width = hidden_rows.shape
    half = width // 2
    ffq = w_gate.shape[2]
    pairs = half // TILE // 2
    data_parts = [2 * ((pairs + 2 - p) // 3) for p in range(3)]
    grid = (4, 4, 4)
    bf16, f32 = jnp.bfloat16, jnp.float32
    first_cut = sum(cut(n)[0][1] for n in data_parts) * TILE
    heads, channels = queries.shape[1:]
    suffix_cache, prefix_pages = jnp.swapaxes(suffix_cache, 1, 2), jnp.swapaxes(prefix_pages, 1, 2)
    shapes = [
        ((2,) + grid + (ROWS, half + TILE), bf16),
        ((2, half, ffq), bf16),
        ((2, half, ffq), bf16),
        ((2, ffq, half), bf16),
        (grid + (ROWS, ffq), f32),
        (grid + (ROWS, ffq), f32),
        (grid + (ROWS, ffq), bf16),
        (grid + (ROWS, half), bf16),
        ((2, 4, 4, ROWS, first_cut), bf16),
        ((2, 4, 4, ROWS, half), bf16),
        ((2, 4, ROWS, first_cut), bf16),
        ((2, 4, ROWS, half), bf16),
        ((3, ROWS, half), bf16),
        ((leaves, half + TILE), f32),
        ((leaves, half + TILE), f32),
        ((leaves, half), f32),
        ((leaves, half), f32),
        ((5,) + prefix_pages.shape[1:], bf16),
        (queries.shape, bf16),
        (suffix_cache.shape, bf16),
        ((leaves, width), bf16),
        (expert_ids.shape, expert_ids.dtype),
        (gate_weights.shape, gate_weights.dtype),
    ]
    scratch = [pltpu.VMEM(shape, kind) for shape, kind in shapes]
    scratch.append(pltpu.SMEM(tree_sizes.shape, tree_sizes.dtype))
    scratch += [pltpu.SemaphoreType.DMA((n,)) for n in (6, 7, 27, 130)]
    vmem, hbm = pl.BlockSpec(memory_space=pltpu.VMEM), pl.BlockSpec(memory_space=pl.ANY)
    results = pl.pallas_call(
        functools.partial(kernel, data_parts),
        out_shape=(pltpu.VMEM((leaves, heads, LATENT), bf16), pltpu.VMEM((leaves, width), bf16)),
        in_specs=[hbm] * 10,
        out_specs=(vmem, vmem),
        scratch_shapes=scratch,
        compiler_params=pltpu.CompilerParams(
            collective_id=0, has_side_effects=True, vmem_limit_bytes=61 * 1024 * 1024
        ),
        name="experts",
    )(
        hidden_rows,
        expert_ids,
        gate_weights,
        tree_sizes,
        w_gate,
        w_up,
        w_down,
        queries,
        suffix_cache,
        prefix_pages,
    )
    results = [pltpu.with_memory_space_constraint(r, pltpu.VMEM) for r in results]
    return pl.pallas_call(
        hand_over,
        out_shape=tuple(jax.ShapeDtypeStruct(r.shape, r.dtype) for r in results),
        in_specs=[vmem] * 2,
        out_specs=(hbm, hbm),
        scratch_shapes=[pltpu.SemaphoreType.DMA((2,))],
        name="results",
    )(*results)


def solution(mesh):
    return jax.shard_map(
        local,
        mesh=mesh,
        in_specs=(
            P(("dp", "ep"), None),
            P(("dp", "ep"), None),
            P(("dp", "ep"), None),
            P("ep", None, "dp"),
            P("ep", None, "dp"),
            P("ep", "dp", None),
            P(("dp", "ep"), None, None),
            P(("dp", "ep"), None, None),
            P(("dp", "ep"), None, None),
            P("dp", None),
        ),
        out_specs=(P(("dp", "ep"), None, None), P(("dp", "ep"), None)),
        check_vma=False,
    )
```
